128 devices in a mesh: lat: 8 (over y_hi, x), lon: 16 (over z, y_lo, core).
Axes of the slice: x: 4, y: 4 (y_hi: 2, y_lo: 2; y = y_hi * 2 + y_lo), z: 4, core: 2. Of those that a mesh axis runs over, the one named last changes fastest.
Arguments:
- tokens: bfloat16 [1, 96, 768, 512], P(None, 'lat', 'lon'), may hold values from -6 to 6
- w_qkv_fine: bfloat16 [3, 512, 512], replicated
- w_proj_fine: bfloat16 [512, 512], replicated, may hold values from -0.25 to 0.25
- w_merge: bfloat16 [8192, 2048], P('lat'), may hold values from -0.0625 to 0.0625
- w_qkv_coarse: bfloat16 [3, 2048, 2048], P(None, None, 'lat')
- w_proj_coarse: bfloat16 [2048, 2048], P('lat'), may hold values from -0.125 to 0.125
- cot_fine: bfloat16 [1, 96, 768, 512], P(None, 'lat', 'lon'), may hold values from -6 to 6
- cot_coarse: bfloat16 [1, 24, 192, 2048], P(None, 'lat', 'lon'), may hold values from -6 to 6
Outputs:
- grad_tokens: bfloat16 [1, 96, 768, 512], P(None, 'lat', 'lon')
- grad_qkv_fine: float32 [3, 512, 512], replicated
- grad_proj_fine: float32 [512, 512], replicated
- grad_merge: float32 [8192, 2048], P('lat', 'lon')
- grad_qkv_coarse: float32 [3, 2048, 2048], P(None, 'lon', 'lat')
- grad_proj_coarse: float32 [2048, 2048], P('lat', 'lon')
The draws below stay inside these ranges and needn't reach their ends.
All inputs are finite; a program needn't handle non-finite values.
Results may differ from the reference program's by a relative error of at most 0.038.
Values may be sent and summed in bfloat16 or wider, within the bound.
A program may use at most 128 MiB of HBM per device.

```python
import jax
import jax.numpy as jnp
from jax import lax

E = 512
C = 2048
HEAD = 64
LEV = 1
WLAT = 6
WLON = 12
NLAT = 96
NLON = 768
NCLAT = 24
NCLON = 192
FM = 8192


def projection_triple(base_key, features):
    key_query, key_keys, key_values = jax.random.split(base_key, 3)
    scale = features ** (-0.5)
    queries = jax.random.normal(key_query, (features, features), jnp.float32) * scale
    key_part = jax.random.normal(key_keys, (features, features), jnp.float32) * scale
    values = jax.random.normal(key_values, (features, features), jnp.float32) * scale
    strong = jnp.arange(features) // HEAD % 4 == 0
    queries = jnp.where(strong[None, :], queries, queries)
    key_part = jnp.where(strong[None, :], key_part, key_part)
    return jnp.stack([queries, key_part, values])


def draw_w_qkv_fine(key, part):
    key = jax.random.fold_in(key, 7)
    return projection_triple(key, E).astype(jnp.bfloat16)


def draw_w_qkv_coarse(key, part):
    key = jax.random.fold_in(key, 13)
    return projection_triple(key, C).astype(jnp.bfloat16)


def with_spikes(array, own_key, source, target, parts, factor):
    owner, partner = [(jnp.arange(array.shape[position]) // (array.shape[position] // parts)).reshape([-1 if axis == position else 1 for axis in range(array.ndim)]) for position in (source, target)]
    chosen = jax.random.permutation(own_key, parts)[partner]
    strong = (owner == chosen) | (owner == (partner + parts // 2) % parts)
    return jnp.where(strong, factor * array, array)


def block_levels(stream_key, shape, cuts, least, high):
    factor_of, own = 1.0, jax.random.fold_in(stream_key, 6)
    for dim, parts in cuts:
        steps = jnp.exp(jax.random.uniform(jax.random.fold_in(own, dim), (parts,), jnp.float32, least / len(cuts), high / len(cuts)))
        factor_of = factor_of * jnp.repeat(steps, shape[dim] // parts).reshape([-1 if axis == dim else 1 for axis in range(len(shape))])
    return factor_of


def normal_values(stream_key, extent, scale, most, cuts=(), kind=jnp.bfloat16):
    loudness = block_levels(stream_key, extent, cuts, -0.22, 0.18) if cuts else 1.0
    values = jax.random.normal(stream_key, extent, jnp.float32) * scale * loudness
    return jnp.minimum(jnp.maximum(values, -most), most).astype(kind)


def noise_with(key, shape, deviation, most, cuts, heavy, kind=jnp.bfloat16):
    drawn = deviation * jax.random.normal(key, shape, jnp.float32)
    if cuts:
        drawn = drawn * block_levels(key, shape, cuts, -0.22, 0.18)
    return jnp.clip(with_spikes(drawn, jax.random.fold_in(key, 3), *heavy), -most, most).astype(kind)


def setup_inputs(seed: int = 0) -> dict:
    key_list = jax.random.split(jax.random.key(seed), 9)
    tokens = normal_values(key_list[0], (LEV, NLAT, NLON, E), 1.0, 6.0, ((1, 8), (2, 16)))
    w_qkv_fine = draw_w_qkv_fine(jax.random.fold_in(key_list[8], 71), 0)
    w_proj_fine = normal_values(key_list[2], (E, E), E ** -0.5, 0.25)
    w_merge = normal_values(key_list[3], (FM, C), FM ** -0.5, 0.0625, ((0, 8),))
    w_qkv_coarse = draw_w_qkv_coarse(jax.random.fold_in(key_list[8], 71), 0)
    w_proj_coarse = normal_values(key_list[5], (C, C), C ** -0.5, 0.125, ((0, 8),))
    cot_fine = normal_values(key_list[6], (LEV, NLAT, NLON, E), 1.0, 6.0, ((1, 8), (2, 16)))
    cot_coarse = noise_with(key_list[7], (LEV, NCLAT, NCLON, C), 1.0, 6.0, ((1, 8), (2, 16)), (2, 3, 16, 2.0))
    return {"tokens": tokens, "w_qkv_fine": w_qkv_fine, "w_proj_fine": w_proj_fine, "w_merge": w_merge, "w_qkv_coarse": w_qkv_coarse, "w_proj_coarse": w_proj_coarse, "cot_fine": cot_fine, "cot_coarse": cot_coarse}


epsilon = 1e-05

def normalize(values):
    average = lax.optimization_barrier(jnp.mean(values, axis=-1, keepdims=True))
    centred = values - average
    spread = lax.optimization_barrier(jnp.mean(centred * centred, axis=-1, keepdims=True))
    return centred * lax.rsqrt(spread + epsilon)

def norm_pullback(values, cotangent):
    return jax.vjp(normalize, values)[1](cotangent)[0]

def to_windows(field_grid):
    levels, lat_len, lon_len, features = field_grid.shape
    blocks = field_grid.reshape(levels, lat_len // WLAT, WLAT, lon_len // WLON, WLON, features)
    blocks = blocks.transpose(1, 3, 0, 2, 4, 5)
    return blocks.reshape(lat_len // WLAT * (lon_len // WLON), levels * WLAT * WLON, features)

def from_windows(windows, levels, lat_len, lon_len):
    features = windows.shape[-1]
    blocks = windows.reshape(lat_len // WLAT, lon_len // WLON, levels, WLAT, WLON, features)
    return blocks.transpose(2, 0, 3, 1, 4, 5).reshape(levels, lat_len, lon_len, features)

def coarsen(field_grid):
    levels, lat_len, lon_len, features = field_grid.shape
    blocks = field_grid.reshape(levels, lat_len // 4, 4, lon_len // 4, 4, features)
    return blocks.transpose(0, 1, 3, 2, 4, 5).reshape(levels, lat_len // 4, lon_len // 4, 16 * features)

def refine(coarse_grid, features):
    levels, lat_len, lon_len, merged = coarse_grid.shape
    blocks = coarse_grid.reshape(levels, lat_len, lon_len, 4, 4, features)
    return blocks.transpose(0, 1, 3, 2, 4, 5).reshape(levels, lat_len * 4, lon_len * 4, features)

def attend_forward(queries, key_rows, values, labels):
    win_count, win_len, features = queries.shape
    head_shape = (win_count, win_len, features // HEAD, HEAD)
    scores = jnp.einsum('wshd,wthd->whst', queries.reshape(head_shape).astype(jnp.float32), key_rows.reshape(head_shape).astype(jnp.float32)) * HEAD ** (-0.5)
    if labels is not None:
        scores = jnp.where((labels[:, :, None] == labels[:, None, :])[:, None], scores, -1e+30)
    row_top = lax.optimization_barrier(jnp.max(scores, axis=-1, keepdims=True))
    weights = jnp.exp(scores - row_top)
    probs_wide = weights / lax.optimization_barrier(jnp.sum(weights, axis=-1, keepdims=True))
    probs_bf = probs_wide.astype(jnp.bfloat16)
    mixed_heads = jnp.einsum('whst,wthd->wshd', probs_bf.astype(jnp.float32), values.reshape(head_shape).astype(jnp.float32))
    return (mixed_heads.reshape(win_count, win_len, features).astype(jnp.bfloat16), probs_wide, probs_bf)

def attend_backward(queries, key_rows, values, probs_wide, probs_bf, d_mixed):
    win_count, win_len, features = queries.shape
    head_shape = (win_count, win_len, features // HEAD, HEAD)
    d_heads = d_mixed.reshape(head_shape).astype(jnp.float32)
    d_probs = jnp.einsum('wshd,wthd->whst', d_heads, values.reshape(head_shape).astype(jnp.float32)).astype(jnp.bfloat16)
    d_probs = lax.optimization_barrier(d_probs).astype(jnp.float32)
    d_scores = probs_wide * (d_probs - lax.optimization_barrier(jnp.sum(d_probs * probs_wide, axis=-1, keepdims=True)))
    d_scores = (d_scores * HEAD ** (-0.5)).astype(jnp.bfloat16).astype(jnp.float32)
    d_query = jnp.einsum('whst,wthd->wshd', d_scores, key_rows.reshape(head_shape).astype(jnp.float32))
    d_key = jnp.einsum('whst,wshd->wthd', d_scores, queries.reshape(head_shape).astype(jnp.float32))
    d_value = jnp.einsum('whst,wshd->wthd', probs_bf.astype(jnp.float32), d_heads)
    return tuple((piece.reshape(win_count, win_len, features).astype(jnp.bfloat16) for piece in (d_query, d_key, d_value)))

def heads_forward(field_grid, labels, w_qkv):
    windows = to_windows(field_grid)
    win_count, win_len, features = windows.shape
    flat_rows = windows.reshape(win_count * win_len, features)
    triple = tuple((jnp.dot(flat_rows, w_qkv[member], preferred_element_type=jnp.float32).astype(jnp.bfloat16).reshape(win_count, win_len, w_qkv.shape[2]) for member in range(3)))
    win_labels = None
    if labels is not None:
        win_labels = to_windows(labels[..., None])[..., 0]
    mixed_heads, probs_wide, probs_bf = attend_forward(triple[0], triple[1], triple[2], win_labels)
    return (flat_rows, triple, mixed_heads, probs_wide, probs_bf)

def heads_backward(flat_rows, triple, probs_wide, probs_bf, d_mixed, w_qkv):
    gradients = attend_backward(triple[0], triple[1], triple[2], probs_wide, probs_bf, d_mixed)
    row_count = flat_rows.shape[0]
    pieces = [piece.reshape(row_count, -1) for piece in gradients]
    grad_weights = jnp.stack([jnp.dot(flat_rows.T, piece, preferred_element_type=jnp.float32) for piece in pieces])
    d_flat = jnp.dot(pieces[0], w_qkv[0].T, preferred_element_type=jnp.float32)
    d_flat = d_flat + jnp.dot(pieces[1], w_qkv[1].T, preferred_element_type=jnp.float32)
    d_flat = d_flat + jnp.dot(pieces[2], w_qkv[2].T, preferred_element_type=jnp.float32)
    return (d_flat, grad_weights)

def reference(tokens, w_qkv_fine, w_proj_fine, w_merge, w_qkv_coarse, w_proj_coarse, cot_fine, cot_coarse):
    half_lat = WLAT // 2
    half_lon = WLON // 2
    levels = tokens.shape[0]
    tokens_wide = tokens.astype(jnp.float32)
    normed = normalize(tokens_wide).astype(jnp.bfloat16)
    shifted = jnp.roll(normed, (-half_lat, -half_lon), axis=(1, 2))
    wrapped = (jnp.arange(NLAT, dtype=jnp.int32) + half_lat >= NLAT).astype(jnp.int32)
    labels = jnp.broadcast_to(wrapped[None, :, None], (levels, NLAT, NLON)).astype(jnp.int32)
    flat_fine, triple_fine, mixed_fine, probs_wide_f, probs_bf_f = heads_forward(shifted, labels, w_qkv_fine)
    mixed_flat = mixed_fine.reshape(flat_fine.shape[0], E)
    out_flat = jnp.dot(mixed_flat, w_proj_fine, preferred_element_type=jnp.float32).astype(jnp.bfloat16)
    attn_fine = jnp.roll(from_windows(out_flat.reshape(mixed_fine.shape), levels, NLAT, NLON), (half_lat, half_lon), axis=(1, 2))
    blended = tokens_wide + attn_fine.astype(jnp.float32)
    gathered = coarsen(blended)
    merged_in = normalize(gathered).astype(jnp.bfloat16)
    merged_flat = merged_in.reshape(-1, FM)
    coarse = jnp.dot(merged_flat, w_merge, preferred_element_type=jnp.float32).reshape(levels, NCLAT, NCLON, C)
    coarse_normed = normalize(coarse).astype(jnp.bfloat16)
    flat_coarse, triple_coarse, mixed_coarse, probs_wide_c, probs_bf_c = heads_forward(coarse_normed, None, w_qkv_coarse)
    rows_coarse = flat_coarse.shape[0]
    cot_flat = to_windows(cot_coarse).reshape(rows_coarse, C)
    coarse_scale = (levels * NCLAT * NCLON) ** (-0.5)
    fine_scale = (levels * NLAT * NLON) ** (-0.5)
    grad_proj_coarse = jnp.dot(mixed_coarse.reshape(rows_coarse, C).T, cot_flat, preferred_element_type=jnp.float32) * coarse_scale
    d_mixed_c = jnp.dot(cot_flat, w_proj_coarse.T, preferred_element_type=jnp.float32).astype(jnp.bfloat16).reshape(mixed_coarse.shape)
    d_flat_c, grad_qkv_c = heads_backward(flat_coarse, triple_coarse, probs_wide_c, probs_bf_c, d_mixed_c, w_qkv_coarse)
    d_normed_c = from_windows(d_flat_c.reshape(mixed_coarse.shape), levels, NCLAT, NCLON).astype(jnp.bfloat16)
    d_coarse = (cot_coarse.astype(jnp.float32) + norm_pullback(coarse, d_normed_c.astype(jnp.float32))).astype(jnp.bfloat16)
    d_coarse_flat = d_coarse.reshape(-1, C)
    grad_merge = jnp.dot(merged_flat.T, d_coarse_flat, preferred_element_type=jnp.float32) * coarse_scale
    d_merged = jnp.dot(d_coarse_flat, w_merge.T, preferred_element_type=jnp.float32).astype(jnp.bfloat16).reshape(merged_in.shape)
    d_blended = cot_fine.astype(jnp.float32) + refine(norm_pullback(gathered, d_merged.astype(jnp.float32)), E)
    d_attn = jnp.roll(d_blended.astype(jnp.bfloat16), (-half_lat, -half_lon), axis=(1, 2))
    d_out_flat = to_windows(d_attn).reshape(-1, E)
    grad_proj_fine = jnp.dot(mixed_flat.T, d_out_flat, preferred_element_type=jnp.float32) * fine_scale
    d_mixed_f = jnp.dot(d_out_flat, w_proj_fine.T, preferred_element_type=jnp.float32).astype(jnp.bfloat16).reshape(mixed_fine.shape)
    d_flat_f, grad_qkv_f = heads_backward(flat_fine, triple_fine, probs_wide_f, probs_bf_f, d_mixed_f, w_qkv_fine)
    d_shifted = from_windows(d_flat_f.astype(jnp.bfloat16).reshape(mixed_fine.shape), levels, NLAT, NLON)
    d_normed = jnp.roll(d_shifted, (half_lat, half_lon), axis=(1, 2))
    grad_tokens = (d_blended + norm_pullback(tokens_wide, d_normed.astype(jnp.float32))).astype(jnp.bfloat16)
    return (grad_tokens, grad_qkv_f * fine_scale, grad_proj_fine, grad_merge, grad_qkv_c * coarse_scale, grad_proj_coarse)
```

```python
import jax
import jax.numpy as jnp
import numpy as np
from jax import lax
from jax.experimental import pallas as pl
from jax.experimental.pallas import tpu as pltpu
from jax.sharding import PartitionSpec as P

MESH = pl.DeviceIdType.MESH
F32 = jnp.float32
BF16 = jnp.bfloat16
EPS = 1e-05
LATS = 8
ROWS, COLS = 12, 48
WL, WC = 6, 12
CELL = 40
WIN = 80
E = 512
HALO = ((0, 128), (128, 64), (192, 32))
VMEM_BYTES = 60 * 1024 * 1024


def tables():
    win = np.zeros((ROWS, COLS), np.int64)
    cell = np.zeros((ROWS, COLS), np.int64)
    for i in range(ROWS):
        for j in range(COLS):
            win[i, j] = ((i // WL) * 4 + j // WC) * WIN + (i % WL) * WC + j % WC
            cell[i, j] = ((i % 4) * 4 + j % 4) * CELL + (i // 4) * 12 + j // 4
    size = 16 * CELL
    to_cells = np.zeros((size, ROWS * COLS), np.float32)
    in_send = np.zeros((224, size), np.float32)
    in_own = np.zeros((size, size), np.float32)
    in_halo = np.zeros((size, 224), np.float32)
    out_send = np.zeros((224, size), np.float32)
    out_own = np.zeros((size, size), np.float32)
    out_halo = np.zeros((size, 224), np.float32)
    for i in range(ROWS):
        for j in range(COLS):
            to_cells[cell[i, j], i * COLS + j] = 1
            r, c = i + 3, j + 6
            if r < ROWS and c < COLS:
                in_own[win[i, j], cell[r, c]] = 1
                out_own[cell[r, c], win[i, j]] = 1
            else:
                if c < COLS:
                    slot = (r - ROWS) * 42 + c - 6
                elif r < ROWS:
                    slot = 128 + (r - 3) * 6 + c - COLS
                else:
                    slot = 192 + (r - ROWS) * 6 + c - COLS
                in_send[slot, cell[r % ROWS, c % COLS]] = 1
                in_halo[win[i, j], slot] = 1
                out_send[slot, win[i, j]] = 1
                out_halo[cell[r % ROWS, c % COLS], slot] = 1
    return [
        jnp.asarray(t, BF16)
        for t in (to_cells, in_send, in_own, in_halo, out_send, out_own, out_halo, to_cells.T)
    ]


def mm(a, b):
    return jnp.dot(a, b, preferred_element_type=F32)


def mm_nt(a, b):
    return lax.dot_general(a, b, (((1,), (1,)), ((), ())), preferred_element_type=F32)


def mm_tn(a, b):
    return lax.dot_general(a, b, (((0,), (0,)), ((), ())), preferred_element_type=F32)


def normalize(x):
    centred = x - jnp.mean(x, axis=-1, keepdims=True)
    return centred * lax.rsqrt(jnp.mean(centred * centred, axis=-1, keepdims=True) + EPS)


def pullback(x, dy):
    centred = x - jnp.mean(x, axis=-1, keepdims=True)
    rate = lax.rsqrt(jnp.mean(centred * centred, axis=-1, keepdims=True) + EPS)
    y = centred * rate
    inner = jnp.mean(dy * y, axis=-1, keepdims=True)
    return rate * (dy - jnp.mean(dy, axis=-1, keepdims=True) - y * inner)


def total(x, axes):
    s = jnp.sum(x, axis=-1, keepdims=True)
    return jnp.sum(s, axis=axes, keepdims=True)


def group_stats(x, axis, count):
    mean = total(x, axis) * (1.0 / count)
    centred = x - mean
    rate = lax.rsqrt(total(centred * centred, axis) * (1.0 / count) + EPS)
    return centred * rate, rate


def group_pullback(x, dy, axis, count):
    y, rate = group_stats(x, axis, count)
    inner = total(dy * y, axis) * (1.0 / count)
    return rate * (dy - total(dy, axis) * (1.0 / count) - y * inner)


def head_masks():
    lane = lax.broadcasted_iota(jnp.int32, (1, 256), 1) // 64
    return [jnp.where(lane == h, 1.0, 0.0) for h in range(4)]


def stack_heads(x, masks):
    return jnp.concatenate([x * m.astype(BF16) for m in masks], axis=0)


def pick_heads(x, masks):
    out = x[:WIN] * masks[0]
    for h in range(1, 4):
        out = out + x[h * WIN : (h + 1) * WIN] * masks[h]
    return out


def softmax_rows(scores):
    weights = jnp.exp(scores - jnp.max(scores, axis=-1, keepdims=True))
    return weights / jnp.sum(weights, axis=-1, keepdims=True)


def scores_back(probs, d_probs):
    d_probs = d_probs.astype(BF16).astype(F32)
    inner = jnp.sum(d_probs * probs, axis=-1, keepdims=True)
    return (probs * (d_probs - inner) * 0.125).astype(BF16)


def greet(devices):
    barrier = pltpu.get_barrier_semaphore()
    for device in devices:
        pl.semaphore_signal(barrier, inc=1, device_id=device, device_id_type=MESH)
    pl.semaphore_wait(barrier, len(devices))


def remote(src, dst, send, recv, device):
    return pltpu.make_async_remote_copy(
        src_ref=src, dst_ref=dst, send_sem=send, recv_sem=recv, device_id=device, device_id_type=MESH
    )


class Place:
    def __init__(self):
        self.lat = lax.axis_index("lat")
        self.lon = lax.axis_index("lon")

    def lat_peer(self, k):
        return lax.rem(self.lat + k, LATS)

    def at_lat(self, k):
        return (self.lat_peer(k), self.lon)

    def halo(self, step):
        up = lax.rem(self.lat + step + LATS, LATS)
        side = lax.rem(self.lon + step + 16, 16)
        return ((up, self.lon), (self.lat, side), (up, side))

    def lon_at(self, z, y, core):
        return (self.lat, z * 4 + y * 2 + core)


def start_halo(where, step, src, dst, sems):
    copies = []
    for n, device in enumerate(where.halo(step)):
        first, count = HALO[n]
        copies.append(
            remote(
                src.at[pl.ds(first, count)],
                dst.at[pl.ds(first, count)],
                sems.at[0, n],
                sems.at[1, n],
                device,
            )
        )
        copies[-1].start()
    return copies


def wait_all(copies):
    for copy in copies:
        copy.wait()


def start_spread(where, src_of, dst, sems):
    copies = []
    for k in range(1, LATS):
        copies.append(
            remote(
                src_of(where.lat_peer(k)),
                dst.at[where.lat],
                sems.at[0, k],
                sems.at[1, k],
                where.at_lat(k),
            )
        )
        copies[-1].start()
    return copies


def finish_spread(where, src_of, dst, sems):
    for k in range(1, LATS):
        source = where.lat_peer(LATS - k)
        remote(src_of(source), dst.at[source], sems.at[0, k], sems.at[1, k], where.at_lat(k)).wait()


def fine_forward(
    tokens, cot, w_qkv, w_proj, to_cells, in_send, in_own, in_halo, out_send, out_own, out_halo,
    x_out, q_out, k_out, v_out, p_out, mixed_out, tg_out, blended_out, slices_out, cots_out,
    merged, send_in, got_in, send_out, got_out, halo_sems, a2a_sems, cot_sems,
):
    where = Place()
    greet([where.at_lat(k) for k in range(1, LATS)] + list(where.halo(-1)[1:]) + list(where.halo(1)[1:]))
    start_spread(where, lambda peer: cot, cots_out, cot_sems)
    cots_out[where.lat] = cot[...]
    tg = mm(to_cells[...], tokens[...])
    tg_out[...] = tg.astype(BF16)
    normed = normalize(tg).astype(BF16)
    send_in[...] = mm(in_send[...], normed).astype(BF16)
    copies = start_halo(where, -1, send_in, got_in, halo_sems.at[0])
    own = mm(in_own[...], normed)
    wait_all(copies)
    x = (own + mm(in_halo[...], got_in[...])).astype(BF16)
    x_out[...] = x
    for m, ref in enumerate((q_out, k_out, v_out)):
        ref[...] = mm(x, w_qkv[m]).astype(BF16)
    masks = head_masks()
    key = lax.broadcasted_iota(jnp.int32, (4 * WIN, WIN), 1)
    query = lax.broadcasted_iota(jnp.int32, (4 * WIN, WIN), 0) % WIN
    real = key < 72
    same = (key < 36) == (query < 36)
    last = where.lat == LATS - 1

    def window(w, carry):
        rows = pl.ds(pl.multiple_of(w * WIN, WIN), WIN)
        bound = jnp.logical_and(last, w >= 4)
        for g in range(2):
            lanes = slice(g * 256, g * 256 + 256)
            scores = mm_nt(stack_heads(q_out[rows, lanes], masks), k_out[rows, lanes]) * 0.125
            allowed = jnp.logical_and(real, jnp.logical_or(same, jnp.logical_not(bound)))
            probs = softmax_rows(jnp.where(allowed, scores, -1e30))
            p_out[w * 2 + g] = probs
            mixed_out[rows, lanes] = pick_heads(
                mm(probs.astype(BF16), v_out[rows, lanes]), masks
            ).astype(BF16)
        return carry

    lax.fori_loop(0, 8, window, 0)
    out = mm(mixed_out[...], w_proj[...]).astype(BF16)
    send_out[...] = mm(out_send[...], out).astype(BF16)
    copies = start_halo(where, 1, send_out, got_out, halo_sems.at[1])
    own = mm(out_own[...], out)
    wait_all(copies)
    blended = tg + own + mm(out_halo[...], got_out[...])
    blended_out[...] = blended
    merged[...] = (
        group_stats(blended.reshape(16, CELL, E), 0, 16 * E)[0].reshape(LATS, WIN, E).astype(BF16)
    )
    start_spread(where, lambda peer: merged.at[peer], slices_out, a2a_sems)
    slices_out[where.lat] = merged[where.lat]
    finish_spread(where, lambda peer: merged.at[peer], slices_out, a2a_sems)
    finish_spread(where, lambda peer: cot, cots_out, cot_sems)


def unpack(x):
    x = x.astype(F32)
    width = x.shape[-1]
    halves = [x[:, :CELL].reshape(LATS * CELL, width), x[:, CELL:].reshape(LATS * CELL, width)]
    return jnp.concatenate(halves, axis=1).astype(BF16)


def pack(top, bottom):
    width = top.shape[-1]
    halves = [top.reshape(LATS, CELL, width), bottom.reshape(LATS, CELL, width)]
    return jnp.concatenate(halves, axis=1).astype(BF16)


def coarse_section(
    slices, cots, w_merge, w_qkv, w_proj,
    d_merged_out, grads_out,
    part, part_got, own_packed, normed_got, rows, rows_t, cot_rows, qkv, d_mixed, mixed, d_qkv,
    d_packed, d_got, d_part, d_part_got, slices_rows_t, d_slices,
    sems,
):
    where = Place()
    greet([where.at_lat(k) for k in range(1, LATS)])
    own_rows = unpack(slices[...])
    slices_rows_t[...] = own_rows.astype(F32).T.astype(BF16)

    def merge(c, carry):
        lanes = pl.ds(pl.multiple_of(c * 256, 256), 256)
        later = pl.ds(pl.multiple_of(1024 + c * 256, 256), 256)
        part[:, :, lanes] = pack(mm(own_rows, w_merge[:, lanes]), mm(own_rows, w_merge[:, later]))
        return carry

    lax.fori_loop(0, 4, merge, 0)
    start_spread(where, lambda peer: part.at[peer], part_got, sems.at[0])
    cot_rows[...] = unpack(cots[...])
    d_mixed[...] = mm_nt(cot_rows[...], w_proj[...]).astype(BF16)
    part_got[where.lat] = part[where.lat]
    finish_spread(where, lambda peer: part.at[peer], part_got, sems.at[0])
    coarse = part_got[0].astype(F32)
    for k in range(1, LATS):
        coarse = coarse + part_got[k].astype(F32)
    coarse = coarse.reshape(2, CELL, 1024)
    own_packed[...] = group_stats(coarse, 0, 2048)[0].reshape(WIN, 1024).astype(BF16)
    start_spread(where, lambda peer: own_packed, normed_got, sems.at[1])
    normed_got[where.lat] = own_packed[...]
    finish_spread(where, lambda peer: own_packed, normed_got, sems.at[1])
    rows[...] = unpack(normed_got[...])
    for m in range(3):
        qkv[m] = mm(rows[...], w_qkv[m]).astype(BF16)
    masks = head_masks()
    key = lax.broadcasted_iota(jnp.int32, (4 * WIN, WIN), 1)
    real = key % CELL < 36

    def window(w, carry):
        own = pl.ds(pl.multiple_of(w * WIN, WIN), WIN)
        heads = stack_heads(qkv[0, own], masks)
        d_heads = stack_heads(d_mixed[own], masks)
        scores = mm_nt(heads, qkv[1, own]) * 0.125
        probs = softmax_rows(jnp.where(real, scores, -1e30))
        probs_bf = probs.astype(BF16)
        mixed[own] = pick_heads(mm(probs_bf, qkv[2, own]), masks).astype(BF16)
        d_scores = scores_back(probs, mm_nt(d_heads, qkv[2, own]))
        d_qkv[own, :256] = pick_heads(mm(d_scores, qkv[1, own]), masks).astype(BF16)
        d_qkv[own, 256:512] = mm_tn(d_scores, heads).astype(BF16)
        d_qkv[own, 512:] = mm_tn(probs_bf, d_heads).astype(BF16)
        return carry

    lax.fori_loop(0, 4, window, 0)

    def back(c, carry):
        halves = []
        for first in (0, 1024):
            own = pl.ds(pl.multiple_of(first + c * 256, 256), 256)
            d_rows = mm_nt(d_qkv[:, :256], w_qkv[0, own])
            d_rows = d_rows + mm_nt(d_qkv[:, 256:512], w_qkv[1, own])
            halves.append(d_rows + mm_nt(d_qkv[:, 512:], w_qkv[2, own]))
        d_part[:, :, pl.ds(pl.multiple_of(c * 256, 256), 256)] = pack(*halves)
        return carry

    lax.fori_loop(0, 4, back, 0)
    start_spread(where, lambda peer: d_part.at[peer], d_part_got, sems.at[2])
    rows_t[...] = rows[...].astype(F32).T.astype(BF16)
    mixed_t = mixed[...].astype(F32).T.astype(BF16)

    def shares(m, carry):
        z, y = m // 2, m % 2
        grad = mm(mixed_t, cot_rows[:, pl.ds(pl.multiple_of(m * 256, 256), 256)]).astype(BF16)
        for core in range(2):
            grads_out[core, y, z, 1024:1280] = grad[:, core * 128 : core * 128 + 128]
            own = pl.ds(pl.multiple_of(m * 256 + core * 128, 128), 128)
            grad_qkv = mm(rows_t[own], d_qkv[...]).astype(BF16)
            for c in range(6):
                grads_out[core, y, z, 1280 + 128 * c : 1408 + 128 * c] = grad_qkv[
                    :, 128 * c : 128 * c + 128
                ]
        return carry

    lax.fori_loop(0, 8, shares, 0)
    d_part_got[where.lat] = d_part[where.lat]
    finish_spread(where, lambda peer: d_part.at[peer], d_part_got, sems.at[2])
    d_normed = d_part_got[0].astype(F32)
    for k in range(1, LATS):
        d_normed = d_normed + d_part_got[k].astype(F32)
    d_normed = d_normed.astype(BF16).astype(F32).reshape(2, CELL, 1024)
    d_coarse = group_pullback(coarse, d_normed, 0, 2048).reshape(WIN, 1024)
    d_packed[...] = (cots[where.lat].astype(F32) + d_coarse).astype(BF16)
    start_spread(where, lambda peer: d_packed, d_got, sems.at[3])
    d_got[where.lat] = d_packed[...]
    finish_spread(where, lambda peer: d_packed, d_got, sems.at[3])
    rows[...] = unpack(d_got[...])

    def slices_back(c, carry):
        lanes = pl.ds(pl.multiple_of(c * 256, 256), 256)
        later = pl.ds(pl.multiple_of(512 + c * 256, 256), 256)
        d_slices[:, :, lanes] = pack(mm_nt(rows[...], w_merge[lanes]), mm_nt(rows[...], w_merge[later]))
        return carry

    lax.fori_loop(0, 2, slices_back, 0)
    start_spread(where, lambda peer: d_slices.at[peer], d_merged_out, sems.at[4])

    def merge_shares(m, carry):
        z, y = m // 2, m % 2
        grad = mm(slices_rows_t[...], rows[:, pl.ds(pl.multiple_of(m * 256, 256), 256)]).astype(BF16)
        for core in range(2):
            grads_out[core, y, z, :1024] = grad[:, core * 128 : core * 128 + 128]
        return carry

    lax.fori_loop(0, 8, merge_shares, 0)
    d_merged_out[where.lat] = d_slices[where.lat]
    finish_spread(where, lambda peer: d_slices.at[peer], d_merged_out, sems.at[4])


def fine_backward(
    d_merged, blended, cot_fine, tg, x, q, k, v, probs, mixed, w_qkv, w_proj, grads,
    to_cells, in_send, in_own, in_halo, out_send, out_own, out_halo, to_grid,
    grad_tokens, grad_fine, grad_merge, grad_proj_c, grad_qkv_c,
    send_in, got_in, send_out, got_out, d_blended_ref, d_mixed, d_q, d_k, d_v,
    got_core, sum_core, got_y, sum_y, got_z,
    fine, fine_core, fine_sum, fine_lat, fine_part, fine_lon, fine_piece, fine_all, fine_rows,
    halo_sems, rs_sems, z_sems, core_sems, lat_sems, lon_sems,
    *, coarse_scale, fine_scale,
):
    where = Place()
    z, y, core = where.lon // 4, lax.rem(where.lon // 2, 2), lax.rem(where.lon, 2)
    chips = [(a, b) for a in range(4) for b in range(2)]
    around = [
        where.lon_at(lax.rem(z + a, 4), lax.rem(y + b, 2), core) for a, b in chips
    ]
    sibling = where.lon_at(z, y, 1 - core)
    greet(
        [where.at_lat(n) for n in range(1, LATS)]
        + around[1:]
        + [sibling]
        + list(where.halo(-1)[1:])
        + list(where.halo(1)[1:])
    )
    to_core = remote(grads.at[1 - core], got_core, rs_sems.at[0, 0], rs_sems.at[1, 0], sibling)
    to_core.start()
    d_gathered = group_pullback(
        blended[...].reshape(16, CELL, E), d_merged[...].astype(F32).reshape(16, CELL, E), 0, 16 * E
    )
    d_blended = mm(to_cells[...], cot_fine[...]) + d_gathered.reshape(16 * CELL, E)
    d_blended_ref[...] = d_blended
    d_bf = d_blended.astype(BF16)
    send_in[...] = mm(in_send[...], d_bf).astype(BF16)
    copies = start_halo(where, -1, send_in, got_in, halo_sems.at[0])
    own = mm(in_own[...], d_bf)
    wait_all(copies)
    d_out = (own + mm(in_halo[...], got_in[...])).astype(BF16)
    d_mixed[...] = mm_nt(d_out, w_proj[...]).astype(BF16)
    fine[3] = mm_tn(mixed[...], d_out).astype(BF16)

    to_core.wait()

    def add_core(n, carry):
        sum_core[n // 4, n % 4] = (
            grads[core, n // 4, n % 4].astype(F32) + got_core[n // 4, n % 4].astype(F32)
        ).astype(BF16)
        return carry

    lax.fori_loop(0, 8, add_core, 0)
    to_y = remote(
        sum_core.at[1 - y], got_y, rs_sems.at[0, 1], rs_sems.at[1, 1], where.lon_at(z, 1 - y, core)
    )
    to_y.start()
    masks = head_masks()

    def window(w, carry):
        rows = pl.ds(pl.multiple_of(w * WIN, WIN), WIN)
        for g in range(2):
            lanes = slice(g * 256, g * 256 + 256)
            p = probs[w * 2 + g]
            heads = stack_heads(q[rows, lanes], masks)
            d_heads = stack_heads(d_mixed[rows, lanes], masks)
            d_scores = scores_back(p, mm_nt(d_heads, v[rows, lanes]))
            d_q[rows, lanes] = pick_heads(mm(d_scores, k[rows, lanes]), masks).astype(BF16)
            d_k[rows, lanes] = mm_tn(d_scores, heads).astype(BF16)
            d_v[rows, lanes] = mm_tn(p.astype(BF16), d_heads).astype(BF16)
        return carry

    lax.fori_loop(0, 8, window, 0)
    x_t = x[...].astype(F32).T.astype(BF16)
    for m, ref in enumerate((d_q, d_k, d_v)):
        fine[m] = mm(x_t, ref[...]).astype(BF16)
    fine_to_core = remote(
        fine.at[pl.ds((1 - core) * 2, 2)], fine_core, core_sems.at[0, 0], core_sems.at[1, 0], sibling
    )
    fine_to_core.start()
    d_shifted = mm_nt(d_q[...], w_qkv[0]) + mm_nt(d_k[...], w_qkv[1]) + mm_nt(d_v[...], w_qkv[2])
    d_shifted = d_shifted.astype(BF16)
    send_out[...] = mm(out_send[...], d_shifted).astype(BF16)
    copies = start_halo(where, 1, send_out, got_out, halo_sems.at[1])
    own = mm(out_own[...], d_shifted)
    fine_to_core.wait()
    mine = [fine[core * 2 + n].astype(F32) + fine_core[n].astype(F32) for n in range(2)]
    for n in range(2):
        fine_sum[4 * n : 4 * n + 4] = mine[n].astype(BF16).reshape(4, 128, E)
    start_spread(where, lambda peer: fine_sum.at[peer], fine_lat, lat_sems.at[0])
    wait_all(copies)
    d_normed = (own + mm(out_halo[...], got_out[...])).astype(BF16).astype(F32)
    grad = d_blended_ref[...] + pullback(tg[...].astype(F32), d_normed)
    grad_tokens[...] = mm(to_grid[...], grad.astype(BF16)).astype(BF16)
    to_y.wait()

    def add_y(n, carry):
        sum_y[n] = (sum_core[y, n].astype(F32) + got_y[n].astype(F32)).astype(BF16)
        return carry

    lax.fori_loop(0, 4, add_y, 0)
    to_z = []
    for a in range(1, 4):
        to_z.append(
            remote(
                sum_y.at[lax.rem(z + a, 4)], got_z.at[a - 1], z_sems.at[0, a], z_sems.at[1, a],
                where.lon_at(lax.rem(z + a, 4), y, core),
            )
        )
        to_z[-1].start()
    fine_lat[where.lat] = fine_sum[where.lat]
    finish_spread(where, lambda peer: fine_sum.at[peer], fine_lat, lat_sems.at[0])
    piece = fine_lat[0].astype(F32)
    for n in range(1, LATS):
        piece = piece + fine_lat[n].astype(F32)
    fine_part[...] = piece.astype(BF16).reshape(8, 16, E)
    copies = []
    for n in range(1, 8):
        a, b = chips[n]
        there = lax.rem(z + a, 4) * 2 + lax.rem(y + b, 2)
        copies.append(
            remote(
                fine_part.at[there], fine_lon.at[n], lon_sems.at[0, 0, n], lon_sems.at[0, 1, n], around[n]
            )
        )
        copies[-1].start()
    here = z * 2 + y
    fine_lon[0] = fine_part[here]
    wait_all(copies)
    piece = fine_lon[0].astype(F32)
    for n in range(1, 8):
        piece = piece + fine_lon[n].astype(F32)
    fine_piece[...] = piece.astype(BF16)
    copies = []
    for n in range(1, 8):
        copies.append(
            remote(
                fine_piece, fine_all.at[here], lon_sems.at[1, 0, n], lon_sems.at[1, 1, n], around[n]
            )
        )
        copies[-1].start()
    fine_all[here] = fine_piece[...]
    for n in range(1, 8):
        a, b = chips[n]
        source = lax.rem(z - a + 4, 4) * 2 + lax.rem(y + b, 2)
        remote(
            fine_piece, fine_all.at[source], lon_sems.at[1, 0, n], lon_sems.at[1, 1, n], around[n]
        ).wait()
    start_spread(where, lambda peer: fine_all, fine_rows.at[core], lat_sems.at[1])
    fine_rows[core, where.lat] = fine_all[...]
    wait_all(to_z)
    coarse = sum_y[z].astype(F32)
    for a in range(3):
        coarse = coarse + got_z[a].astype(F32)
    coarse = coarse * coarse_scale
    grad_merge[...] = coarse[:1024]
    grad_proj_c[...] = coarse[1024:1280]
    for c in range(6):
        grad_qkv_c[c // 2, :, (c % 2) * 128 : (c % 2) * 128 + 128] = coarse[1280 + 128 * c : 1408 + 128 * c]
    finish_spread(where, lambda peer: fine_all, fine_rows.at[core], lat_sems.at[1])
    last = remote(
        fine_rows.at[core], fine_rows.at[core], core_sems.at[0, 1], core_sems.at[1, 1], sibling
    )
    last.start()
    remote(
        fine_rows.at[1 - core], fine_rows.at[1 - core], core_sems.at[0, 1], core_sems.at[1, 1], sibling
    ).wait()
    for c in range(2):
        for n in range(2):
            grad_fine[2 * c + n] = (
                fine_rows[c, 4 * n : 4 * n + 4].reshape(E, E).astype(F32) * fine_scale
            )


def call(kernel, number, outs, scratch, operands):
    vmem = pl.BlockSpec(memory_space=pltpu.VMEM)
    return pl.pallas_call(
        kernel,
        out_shape=[jax.ShapeDtypeStruct(shape, dtype) for shape, dtype in outs],
        in_specs=[vmem] * len(operands),
        out_specs=[vmem] * len(outs),
        scratch_shapes=scratch,
        compiler_params=pltpu.CompilerParams(
            collective_id=number, has_side_effects=True, vmem_limit_bytes=VMEM_BYTES
        ),
    )(*operands)


def dma(*shape):
    return pltpu.SemaphoreType.DMA(shape)


def bf(*shape):
    return pltpu.VMEM(shape, BF16)


def per_device(tokens, w_qkv_f, w_proj_f, w_merge, w_qkv_c, w_proj_c, cot_fine, cot_coarse):
    to_cells, in_send, in_own, in_halo, out_send, out_own, out_halo, to_grid = tables()
    flat = tokens.reshape(ROWS * COLS, E)
    cot_flat = cot_fine.reshape(ROWS * COLS, E)
    cot = jnp.pad(cot_coarse.reshape(36, 2048), ((0, 4), (0, 0)))
    cot = jnp.concatenate([cot[:, :1024], cot[:, 1024:]], axis=0)
    size = 16 * CELL
    x, q, k, v, probs, mixed, tg, blended, slices, cots = call(
        fine_forward,
        1,
        [((size, E), BF16)] * 4
        + [((16, 4 * WIN, WIN), F32), ((size, E), BF16), ((size, E), BF16), ((size, E), F32)]
        + [((LATS, WIN, E), BF16), ((LATS, WIN, 1024), BF16)],
        [bf(LATS, WIN, E), bf(224, E), bf(224, E), bf(224, E), bf(224, E)]
        + [dma(2, 2, 3), dma(2, LATS), dma(2, LATS)],
        (flat, cot, w_qkv_f, w_proj_f, to_cells, in_send, in_own, in_halo, out_send, out_own, out_halo),
    )
    d_merged, grads = call(
        coarse_section,
        2,
        [((LATS, WIN, E), BF16), ((2, 2, 4, 2048, 128), BF16)],
        [bf(LATS, WIN, 1024), bf(LATS, WIN, 1024), bf(WIN, 1024), bf(LATS, WIN, 1024)]
        + [bf(320, 2048), bf(2048, 320), bf(320, 2048), bf(3, 320, 256), bf(320, 256), bf(320, 256)]
        + [bf(320, 768), bf(WIN, 1024), bf(LATS, WIN, 1024), bf(LATS, WIN, 1024), bf(LATS, WIN, 1024)]
        + [bf(1024, 320), bf(LATS, WIN, E), dma(5, 2, LATS)],
        (slices, cots, w_merge, w_qkv_c, w_proj_c),
    )

    def back(*refs):
        fine_backward(*refs, coarse_scale=4608**-0.5, fine_scale=73728**-0.5)

    grad_tokens, grad_fine, grad_merge, grad_proj_c, grad_qkv_c = call(
        back,
        3,
        [((ROWS * COLS, E), BF16), ((4, E, E), F32), ((1024, 128), F32), ((256, 128), F32)]
        + [((3, 128, 256), F32)],
        [bf(224, E)] * 4
        + [pltpu.VMEM((size, E), F32)]
        + [bf(size, E)] * 4
        + [bf(2, 4, 2048, 128), bf(2, 4, 2048, 128), bf(4, 2048, 128), bf(4, 2048, 128)]
        + [bf(3, 2048, 128)]
        + [bf(4, E, E), bf(2, E, E), bf(8, 128, E), bf(8, 128, E), bf(8, 16, E), bf(8, 16, E)]
        + [bf(16, E), bf(8, 16, E), bf(2, 8, 8, 16, E)]
        + [dma(2, 2, 3), dma(2, 2), dma(2, 4), dma(2, 2), dma(2, 2, LATS), dma(2, 2, 8)],
        (d_merged.reshape(size, E), blended, cot_flat, tg, x, q, k, v, probs, mixed, w_qkv_f, w_proj_f)
        + (grads, to_cells, in_send, in_own, in_halo, out_send, out_own, out_halo, to_grid),
    )
    return (
        grad_tokens.reshape(tokens.shape),
        grad_fine[:3],
        grad_fine[3],
        grad_merge,
        grad_qkv_c,
        grad_proj_c,
    )


def solution(mesh):
    return jax.shard_map(
        per_device,
        mesh=mesh,
        in_specs=(
            P(None, "lat", "lon", None),
            P(),
            P(),
            P("lat", None),
            P(None, None, "lat"),
            P("lat", None),
            P(None, "lat", "lon", None),
            P(None, "lat", "lon", None),
        ),
        out_specs=(
            P(None, "lat", "lon", None),
            P(),
            P(),
            P("lat", "lon"),
            P(None, "lon", "lat"),
            P("lat", "lon"),
        ),
        check_vma=False,
    )
```

```python
import jax
import jax.numpy as jnp
import numpy as np
from jax import lax
from jax.experimental import pallas as pl
from jax.experimental.pallas import tpu as pltpu
from jax.sharding import PartitionSpec as P

MESH = pl.DeviceIdType.MESH
F32 = jnp.float32
BF16 = jnp.bfloat16
EPS = 1e-05
LATS = 8
ROWS, COLS = 12, 48
WL, WC = 6, 12
CELL = 40
WIN = 80
E = 512
HALO = ((0, 128), (128, 64), (192, 32))
VMEM_BYTES = 63 * 1024 * 1024


def tables():
    win = np.zeros((ROWS, COLS), np.int64)
    cell = np.zeros((ROWS, COLS), np.int64)
    for i in range(ROWS):
        for j in range(COLS):
            win[i, j] = ((i // WL) * 4 + j // WC) * WIN + (i % WL) * WC + j % WC
            cell[i, j] = ((i % 4) * 4 + j % 4) * CELL + (i // 4) * 12 + j // 4
    size = 16 * CELL
    to_cells = np.zeros((size, ROWS * COLS), np.float32)
    in_send = np.zeros((224, size), np.float32)
    in_own = np.zeros((size, size), np.float32)
    in_halo = np.zeros((size, 224), np.float32)
    out_send = np.zeros((224, size), np.float32)
    out_own = np.zeros((size, size), np.float32)
    out_halo = np.zeros((size, 224), np.float32)
    for i in range(ROWS):
        for j in range(COLS):
            to_cells[cell[i, j], i * COLS + j] = 1
            r, c = i + 3, j + 6
            if r < ROWS and c < COLS:
                in_own[win[i, j], cell[r, c]] = 1
                out_own[cell[r, c], win[i, j]] = 1
            else:
                if c < COLS:
                    slot = (r - ROWS) * 42 + c - 6
                elif r < ROWS:
                    slot = 128 + (r - 3) * 6 + c - COLS
                else:
                    slot = 192 + (r - ROWS) * 6 + c - COLS
                in_send[slot, cell[r % ROWS, c % COLS]] = 1
                in_halo[win[i, j], slot] = 1
                out_send[slot, win[i, j]] = 1
                out_halo[cell[r % ROWS, c % COLS], slot] = 1
    return [
        jnp.asarray(t, BF16)
        for t in (to_cells, in_send, in_own, in_halo, out_send, out_own, out_halo, to_cells.T)
    ]


def mm(a, b):
    return jnp.dot(a, b, preferred_element_type=F32)


def mm_nt(a, b):
    return lax.dot_general(a, b, (((1,), (1,)), ((), ())), preferred_element_type=F32)


def mm_tn(a, b):
    return lax.dot_general(a, b, (((0,), (0,)), ((), ())), preferred_element_type=F32)


def normalize(x):
    centred = x - jnp.mean(x, axis=-1, keepdims=True)
    return centred * lax.rsqrt(jnp.mean(centred * centred, axis=-1, keepdims=True) + EPS)


def pullback(x, dy):
    centred = x - jnp.mean(x, axis=-1, keepdims=True)
    rate = lax.rsqrt(jnp.mean(centred * centred, axis=-1, keepdims=True) + EPS)
    y = centred * rate
    inner = jnp.mean(dy * y, axis=-1, keepdims=True)
    return rate * (dy - jnp.mean(dy, axis=-1, keepdims=True) - y * inner)


def total(x, axes):
    s = jnp.sum(x, axis=-1, keepdims=True)
    return jnp.sum(s, axis=axes, keepdims=True)


def group_stats(x, axis, count):
    mean = total(x, axis) * (1.0 / count)
    centred = x - mean
    rate = lax.rsqrt(total(centred * centred, axis) * (1.0 / count) + EPS)
    return centred * rate, rate


def group_pullback(x, dy, axis, count):
    y, rate = group_stats(x, axis, count)
    inner = total(dy * y, axis) * (1.0 / count)
    return rate * (dy - total(dy, axis) * (1.0 / count) - y * inner)


def head_masks():
    lane = lax.broadcasted_iota(jnp.int32, (1, 256), 1) // 64
    return [jnp.where(lane == h, 1.0, 0.0) for h in range(4)]


def stack_heads(x, masks):
    return jnp.concatenate([x * m.astype(BF16) for m in masks], axis=0)


def pick_heads(x, masks):
    out = x[:WIN] * masks[0]
    for h in range(1, 4):
        out = out + x[h * WIN : (h + 1) * WIN] * masks[h]
    return out


def softmax_rows(scores):
    weights = jnp.exp(scores - jnp.max(scores, axis=-1, keepdims=True))
    return weights / jnp.sum(weights, axis=-1, keepdims=True)


def scores_back(probs, d_probs):
    d_probs = d_probs.astype(BF16).astype(F32)
    inner = jnp.sum(d_probs * probs, axis=-1, keepdims=True)
    return (probs * (d_probs - inner) * 0.125).astype(BF16)


def greet(devices):
    barrier = pltpu.get_barrier_semaphore()
    for device in devices:
        pl.semaphore_signal(barrier, inc=1, device_id=device, device_id_type=MESH)
    pl.semaphore_wait(barrier, len(devices))


def remote(src, dst, send, recv, device):
    return pltpu.make_async_remote_copy(
        src_ref=src, dst_ref=dst, send_sem=send, recv_sem=recv, device_id=device, device_id_type=MESH
    )


class Place:
    def __init__(self):
        self.lat = lax.axis_index("lat")
        self.lon = lax.axis_index("lon")

    def lat_peer(self, k):
        return lax.rem(self.lat + k, LATS)

    def at_lat(self, k):
        return (self.lat_peer(k), self.lon)

    def halo(self, step):
        up = lax.rem(self.lat + step + LATS, LATS)
        side = lax.rem(self.lon + step + 16, 16)
        return ((up, self.lon), (self.lat, side), (up, side))

    def lon_at(self, z, y, core):
        return (self.lat, z * 4 + y * 2 + core)


def start_halo(where, step, src, dst, sems):
    copies = []
    for n, device in enumerate(where.halo(step)):
        first, count = HALO[n]
        copies.append(
            remote(
                src.at[pl.ds(first, count)],
                dst.at[pl.ds(first, count)],
                sems.at[0, n],
                sems.at[1, n],
                device,
            )
        )
        copies[-1].start()
    return copies


def wait_all(copies):
    for copy in copies:
        copy.wait()


def start_spread(where, src_of, dst, sems):
    copies = []
    for k in range(1, LATS):
        copies.append(
            remote(
                src_of(where.lat_peer(k)),
                dst.at[where.lat],
                sems.at[0, k],
                sems.at[1, k],
                where.at_lat(k),
            )
        )
        copies[-1].start()
    return copies


def finish_spread(where, src_of, dst, sems):
    for k in range(1, LATS):
        source = where.lat_peer(LATS - k)
        remote(src_of(source), dst.at[source], sems.at[0, k], sems.at[1, k], where.at_lat(k)).wait()


def unpack(x):
    x = x.astype(F32)
    width = x.shape[-1]
    halves = [x[:, :CELL].reshape(LATS * CELL, width), x[:, CELL:].reshape(LATS * CELL, width)]
    return jnp.concatenate(halves, axis=1).astype(BF16)


def pack(top, bottom):
    width = top.shape[-1]
    halves = [top.reshape(LATS, CELL, width), bottom.reshape(LATS, CELL, width)]
    return jnp.concatenate(halves, axis=1).astype(BF16)


class Flights:
    def __init__(self):
        self.open = {}

    def start(self, name, copies):
        self.open[name] = copies
        for copy in copies:
            copy.start()

    def wait(self, name):
        for copy in self.open.pop(name):
            copy.wait()


def spread(where, src_of, dst, sems):
    return [
        remote(
            src_of(where.lat_peer(k)), dst.at[where.lat], sems.at[0, k], sems.at[1, k], where.at_lat(k)
        )
        for k in range(1, LATS)
    ]


def halo_copies(where, step, src, dst, sems):
    copies = []
    for n, device in enumerate(where.halo(step)):
        rows = pl.ds(*HALO[n])
        copies.append(remote(src.at[rows], dst.at[rows], sems.at[0, n], sems.at[1, n], device))
    return copies


def sum_slots(ref):
    value = ref[0].astype(F32)
    for n in range(1, ref.shape[0]):
        value = value + ref[n].astype(F32)
    return value


def whole(
    tokens_h, cot, to_cells, in_send, in_own, in_halo,
    out_send_h, out_own_h, out_halo_h, to_grid_h, cot_fine_h,
    w_qkv_f_h, w_proj_f_h, w_merge_h, w_qkv_c_h, w_proj_c_h,
    grad_tokens, fine_rows, coarse_sums,
    out_send, out_own, out_halo, to_grid, grid_in, w_qkv_f, w_proj_f, w_merge, w_qkv_c, w_proj_c,
    x, q, k, v, probs, mixed_f, tg, blended, merged, slices,
    send_in, got_in, send_out, got_out, got_in2, got_out2,
    part, part_got, coarse_ref, packed, normed_got, rows, rows_t, cot_rows, qkv, d_mixed_c, mixed_c, d_qkv,
    d_packed, slices_t,
    share, core_a, z_a, line_a, y_a,
    core_b, z_b, line_b, y_b,
    fine, fine_core, fine_sum, fine_lat, fine_part, fine_lon, fine_piece, fine_all,
    load_sems, halo_sems, lat_sems, share_sems, z_sems, core_sems, lon_sems,
):
    where = Place()
    z, y, core = where.lon // 4, lax.rem(where.lon // 2, 2), lax.rem(where.lon, 2)
    chips = [(a, b) for a in range(4) for b in range(2)]
    around = [where.lon_at(lax.rem(z + a, 4), lax.rem(y + b, 2), core) for a, b in chips]
    sibling = where.lon_at(z, y, 1 - core)
    other_y = where.lon_at(z, 1 - y, core)
    flights = Flights()

    def body():
        barrier = pltpu.get_barrier_semaphore()
        friends = [where.at_lat(n) for n in range(1, LATS)] + around[1:] + [sibling]
        friends += list(where.halo(-1)[1:]) + list(where.halo(1)[1:])
        for device in friends:
            pl.semaphore_signal(barrier, inc=1, device_id=device, device_id_type=MESH)
        flights.start("tokens", [pltpu.make_async_copy(tokens_h, grid_in, load_sems.at[9])])
        loads = (
            ("w_qkv_f", w_qkv_f_h, w_qkv_f), ("w_proj_f", w_proj_f_h, w_proj_f),
            ("out_send", out_send_h, out_send), ("out_own", out_own_h, out_own),
            ("out_halo", out_halo_h, out_halo), ("w_merge", w_merge_h, w_merge),
            ("w_proj_c", w_proj_c_h, w_proj_c), ("w_qkv_c", w_qkv_c_h, w_qkv_c),
            ("to_grid", to_grid_h, to_grid),
        )
        for n, (name, far, near) in enumerate(loads):
            flights.start(name, [pltpu.make_async_copy(far, near, load_sems.at[n])])

        flights.wait("tokens")
        cells = mm(to_cells[...], grid_in[...])
        tg[...] = cells.astype(BF16)
        flights.start("cot_fine", [pltpu.make_async_copy(cot_fine_h, grid_in, load_sems.at[9])])
        normed = normalize(cells).astype(BF16)
        send_in[...] = mm(in_send[...], normed).astype(BF16)
        pl.semaphore_wait(barrier, len(friends))
        flights.start("halo1", halo_copies(where, -1, send_in, got_in, halo_sems.at[0]))
        own = mm(in_own[...], normed)
        flights.wait("halo1")
        flights.start("cots", spread(where, lambda peer: cot, normed_got, lat_sems.at[0]))
        normed_got[where.lat] = cot[...]
        x[...] = (own + mm(in_halo[...], got_in[...])).astype(BF16)
        flights.wait("w_qkv_f")
        for m, ref in enumerate((q, k, v)):
            ref[...] = mm(x[...], w_qkv_f[m]).astype(BF16)
        masks = head_masks()
        key = lax.broadcasted_iota(jnp.int32, (4 * WIN, WIN), 1)
        query = lax.broadcasted_iota(jnp.int32, (4 * WIN, WIN), 0) % WIN
        real = key < 72
        same = (key < 36) == (query < 36)
        last = where.lat == LATS - 1

        def window(w, carry):
            own_rows = pl.ds(pl.multiple_of(w * WIN, WIN), WIN)
            bound = jnp.logical_and(last, w >= 4)
            for g in range(2):
                lanes = slice(g * 256, g * 256 + 256)
                scores = mm_nt(stack_heads(q[own_rows, lanes], masks), k[own_rows, lanes]) * 0.125
                allowed = jnp.logical_and(real, jnp.logical_or(same, jnp.logical_not(bound)))
                weights = softmax_rows(jnp.where(allowed, scores, -1e30))
                probs[w * 2 + g] = weights
                mixed_f[own_rows, lanes] = pick_heads(
                    mm(weights.astype(BF16), v[own_rows, lanes]), masks
                ).astype(BF16)
            return carry

        lax.fori_loop(0, 8, window, 0)
        flights.wait("w_proj_f")
        out = mm(mixed_f[...], w_proj_f[...]).astype(BF16)
        flights.wait("out_send")
        send_out[...] = mm(out_send[...], out).astype(BF16)
        flights.start("halo2", halo_copies(where, 1, send_out, got_out, halo_sems.at[1]))
        flights.wait("out_own")
        flights.wait("out_halo")
        own = tg[...].astype(F32) + mm(out_own[...], out)
        flights.wait("halo2")
        blended[...] = own + mm(out_halo[...], got_out[...])
        merged[...] = (
            group_stats(blended[...].reshape(16, CELL, E), 0, 16 * E)[0]
            .reshape(LATS, WIN, E)
            .astype(BF16)
        )
        flights.start("merged", spread(where, lambda peer: merged.at[peer], slices, lat_sems.at[1]))
        slices[where.lat] = merged[where.lat]
        flights.wait("cots")
        cot_rows[...] = unpack(normed_got[...])
        flights.wait("w_proj_c")
        d_mixed_c[...] = mm_nt(cot_rows[...], w_proj_c[...]).astype(BF16)
        flights.wait("w_merge")
        flights.wait("merged")

        own_rows = unpack(slices[...])

        def merge(c, carry):
            lanes = pl.ds(pl.multiple_of(c * 256, 256), 256)
            later = pl.ds(pl.multiple_of(1024 + c * 256, 256), 256)
            part[:, :, lanes] = pack(mm(own_rows, w_merge[:, lanes]), mm(own_rows, w_merge[:, later]))
            return carry

        lax.fori_loop(0, 4, merge, 0)
        flights.start("part", spread(where, lambda peer: part.at[peer], part_got, lat_sems.at[2]))
        part_got[where.lat] = part[where.lat]
        slices_t[...] = own_rows.astype(F32).T.astype(BF16)
        flights.wait("part")
        coarse_ref[...] = sum_slots(part_got)
        packed[...] = (
            group_stats(coarse_ref[...].reshape(2, CELL, 1024), 0, 2048)[0]
            .reshape(WIN, 1024)
            .astype(BF16)
        )
        flights.start("normed", spread(where, lambda peer: packed, normed_got, lat_sems.at[3]))
        normed_got[where.lat] = packed[...]
        flights.wait("w_qkv_c")
        flights.wait("normed")
        rows[...] = unpack(normed_got[...])
        for m in range(3):
            qkv[m] = mm(rows[...], w_qkv_c[m]).astype(BF16)
        real_c = key % CELL < 36

        def window_c(w, carry):
            own_rows = pl.ds(pl.multiple_of(w * WIN, WIN), WIN)
            heads = stack_heads(qkv[0, own_rows], masks)
            d_heads = stack_heads(d_mixed_c[own_rows], masks)
            scores = mm_nt(heads, qkv[1, own_rows]) * 0.125
            weights = softmax_rows(jnp.where(real_c, scores, -1e30))
            weights_bf = weights.astype(BF16)
            mixed_c[own_rows] = pick_heads(mm(weights_bf, qkv[2, own_rows]), masks).astype(BF16)
            d_scores = scores_back(weights, mm_nt(d_heads, qkv[2, own_rows]))
            d_qkv[own_rows, :256] = pick_heads(mm(d_scores, qkv[1, own_rows]), masks).astype(BF16)
            d_qkv[own_rows, 256:512] = mm_tn(d_scores, heads).astype(BF16)
            d_qkv[own_rows, 512:] = mm_tn(weights_bf, d_heads).astype(BF16)
            return carry

        lax.fori_loop(0, 4, window_c, 0)

        def back(c, carry):
            halves = []
            for first in (0, 1024):
                part_rows = pl.ds(pl.multiple_of(first + c * 256, 256), 256)
                d_rows = mm_nt(d_qkv[:, :256], w_qkv_c[0, part_rows])
                d_rows = d_rows + mm_nt(d_qkv[:, 256:512], w_qkv_c[1, part_rows])
                halves.append(d_rows + mm_nt(d_qkv[:, 512:], w_qkv_c[2, part_rows]))
            part[:, :, pl.ds(pl.multiple_of(c * 256, 256), 256)] = pack(*halves)
            return carry

        lax.fori_loop(0, 4, back, 0)
        flights.start("d_part", spread(where, lambda peer: part.at[peer], part_got, lat_sems.at[4]))
        part_got[where.lat] = part[where.lat]
        rows_t[...] = rows[...].astype(F32).T.astype(BF16)
        mixed_t = mixed_c[...].astype(F32).T.astype(BF16)

        def shares(m, carry):
            grad = mm(mixed_t, cot_rows[:, pl.ds(pl.multiple_of(m * 256, 256), 256)]).astype(BF16)
            for c in range(2):
                share[c, m // 2, m % 2, :256] = grad[:, c * 128 : c * 128 + 128]
                own_rows = pl.ds(pl.multiple_of(m * 256 + c * 128, 128), 128)
                grad_qkv = mm(rows_t[own_rows], d_qkv[...]).astype(BF16)
                for n in range(6):
                    share[c, m // 2, m % 2, 256 + 128 * n : 384 + 128 * n] = grad_qkv[
                        :, 128 * n : 128 * n + 128
                    ]
            return carry

        lax.fori_loop(0, 8, shares, 0)
        flights.start(
            "core_a",
            [remote(share.at[1 - core], core_a, share_sems.at[0, 0], share_sems.at[1, 0], sibling)],
        )

        def add_pairs(got):
            def add(n, carry):
                got[n] = (share[core, n].astype(F32) + got[n].astype(F32)).astype(BF16)
                return carry

            lax.fori_loop(0, 4, add, 0)

        def z_copies(src, dst, sems):
            copies = []
            for a in range(1, 4):
                there = lax.rem(z + a, 4)
                copies.append(
                    remote(
                        src.at[there], dst.at[a], sems.at[0, a], sems.at[1, a],
                        where.lon_at(there, y, core),
                    )
                )
            return copies

        flights.wait("d_part")
        d_normed = sum_slots(part_got).astype(BF16).astype(F32).reshape(2, CELL, 1024)
        d_coarse = group_pullback(coarse_ref[...].reshape(2, CELL, 1024), d_normed, 0, 2048)
        d_packed[...] = (cot[...].astype(F32) + d_coarse.reshape(WIN, 1024)).astype(BF16)
        flights.start("d_coarse", spread(where, lambda peer: d_packed, normed_got, lat_sems.at[5]))
        normed_got[where.lat] = d_packed[...]
        flights.wait("core_a")
        add_pairs(core_a)
        flights.start("z_a", z_copies(core_a, z_a, z_sems.at[0]))
        flights.wait("d_coarse")
        rows[...] = unpack(normed_got[...])

        def slices_back(c, carry):
            lanes = pl.ds(pl.multiple_of(c * 256, 256), 256)
            later = pl.ds(pl.multiple_of(512 + c * 256, 256), 256)
            merged[:, :, lanes] = pack(
                mm_nt(rows[...], w_merge[lanes]), mm_nt(rows[...], w_merge[later])
            )
            return carry

        lax.fori_loop(0, 2, slices_back, 0)
        flights.start("d_slices", spread(where, lambda peer: merged.at[peer], slices, lat_sems.at[6]))
        slices[where.lat] = merged[where.lat]

        def merge_shares(m, carry):
            grad = mm(slices_t[...], rows[:, pl.ds(pl.multiple_of(m * 256, 256), 256)]).astype(BF16)
            for c in range(2):
                share[c, m // 2, m % 2] = grad[:, c * 128 : c * 128 + 128]
            return carry

        lax.fori_loop(0, 8, merge_shares, 0)
        flights.start(
            "core_b",
            [remote(share.at[1 - core], core_b, share_sems.at[0, 1], share_sems.at[1, 1], sibling)],
        )
        flights.wait("d_slices")

        d_gathered = group_pullback(
            blended[...].reshape(16, CELL, E),
            slices[...].astype(F32).reshape(16, CELL, E),
            0,
            16 * E,
        )
        flights.wait("cot_fine")
        blended[...] = mm(to_cells[...], grid_in[...]) + d_gathered.reshape(16 * CELL, E)
        d_bf = blended[...].astype(BF16)
        send_in[...] = mm(in_send[...], d_bf).astype(BF16)
        flights.start("halo3", halo_copies(where, -1, send_in, got_in2, halo_sems.at[2]))
        own = mm(in_own[...], d_bf)
        flights.wait("core_b")
        add_pairs(core_b)
        flights.wait("z_a")
        z_a[0] = core_a[z]
        line_a[...] = sum_slots(z_a).astype(BF16)
        flights.start("z_b", z_copies(core_b, z_b, z_sems.at[1]))
        flights.start(
            "y_a", [remote(line_a.at[1 - y], y_a, share_sems.at[0, 2], share_sems.at[1, 2], other_y)]
        )
        flights.wait("halo3")
        d_out = (own + mm(in_halo[...], got_in2[...])).astype(BF16)
        fine[3] = mm_tn(mixed_f[...], d_out).astype(BF16)
        mixed_f[...] = mm_nt(d_out, w_proj_f[...]).astype(BF16)

        def window_b(w, carry):
            own_rows = pl.ds(pl.multiple_of(w * WIN, WIN), WIN)
            for g in range(2):
                lanes = slice(g * 256, g * 256 + 256)
                weights = probs[w * 2 + g]
                heads = stack_heads(q[own_rows, lanes], masks)
                d_heads = stack_heads(mixed_f[own_rows, lanes], masks)
                d_scores = scores_back(weights, mm_nt(d_heads, v[own_rows, lanes]))
                new_q = pick_heads(mm(d_scores, k[own_rows, lanes]), masks).astype(BF16)
                new_k = mm_tn(d_scores, heads).astype(BF16)
                v[own_rows, lanes] = mm_tn(weights.astype(BF16), d_heads).astype(BF16)
                q[own_rows, lanes] = new_q
                k[own_rows, lanes] = new_k
            return carry

        lax.fori_loop(0, 8, window_b, 0)
        x_t = x[...].astype(F32).T.astype(BF16)
        for m, ref in enumerate((q, k, v)):
            fine[m] = mm(x_t, ref[...]).astype(BF16)
        flights.start(
            "fine_core",
            [
                remote(
                    fine.at[pl.ds((1 - core) * 2, 2)], fine_core,
                    core_sems.at[0, 0], core_sems.at[1, 0], sibling,
                )
            ],
        )
        d_shifted = mm_nt(q[...], w_qkv_f[0]) + mm_nt(k[...], w_qkv_f[1])
        d_shifted = (d_shifted + mm_nt(v[...], w_qkv_f[2])).astype(BF16)
        send_out[...] = mm(out_send[...], d_shifted).astype(BF16)
        flights.start("halo4", halo_copies(where, 1, send_out, got_out2, halo_sems.at[3]))
        flights.wait("fine_core")
        for n in range(2):
            pair = fine[core * 2 + n].astype(F32) + fine_core[n].astype(F32)
            fine_sum[4 * n : 4 * n + 4] = pair.astype(BF16).reshape(4, 128, E)
        flights.start("fine_lat", spread(where, lambda peer: fine_sum.at[peer], fine_lat, lat_sems.at[7]))
        fine_lat[where.lat] = fine_sum[where.lat]
        own = mm(out_own[...], d_shifted)
        flights.wait("halo4")
        d_normed = (own + mm(out_halo[...], got_out2[...])).astype(BF16).astype(F32)
        grad = blended[...] + pullback(tg[...].astype(F32), d_normed)
        flights.wait("to_grid")
        grad_tokens[...] = mm(to_grid[...], grad.astype(BF16)).astype(BF16)
        flights.wait("z_b")
        z_b[0] = core_b[z]
        line_b[...] = sum_slots(z_b).astype(BF16)
        flights.start(
            "y_b", [remote(line_b.at[1 - y], y_b, share_sems.at[0, 3], share_sems.at[1, 3], other_y)]
        )
        flights.wait("fine_lat")
        fine_part[...] = sum_slots(fine_lat).astype(BF16).reshape(8, 16, E)
        here = z * 2 + y
        copies = []
        for n in range(1, 8):
            a, b = chips[n]
            there = lax.rem(z + a, 4) * 2 + lax.rem(y + b, 2)
            copies.append(
                remote(
                    fine_part.at[there], fine_lon.at[n],
                    lon_sems.at[0, 0, n], lon_sems.at[0, 1, n], around[n],
                )
            )
        flights.start("fine_lon", copies)
        fine_lon[0] = fine_part[here]
        flights.wait("fine_lon")
        fine_piece[...] = sum_slots(fine_lon).astype(BF16)
        copies = []
        for n in range(1, 8):
            copies.append(
                remote(
                    fine_piece, fine_all.at[here],
                    lon_sems.at[1, 0, n], lon_sems.at[1, 1, n], around[n],
                )
            )
        flights.start("fine_all", copies)
        fine_all[here] = fine_piece[...]
        flights.wait("fine_all")
        flights.start("fine_rows", spread(where, lambda peer: fine_all, fine_rows.at[core], lat_sems.at[8]))
        fine_rows[core, where.lat] = fine_all[...]
        flights.wait("y_a")
        coarse_sums[:1024] = line_a[y].astype(F32) + y_a[...].astype(F32)
        flights.wait("y_b")
        coarse_sums[1024:] = line_b[y].astype(F32) + y_b[...].astype(F32)
        flights.wait("fine_rows")
        flights.start(
            "last",
            [
                remote(
                    fine_rows.at[core], fine_rows.at[core],
                    core_sems.at[0, 1], core_sems.at[1, 1], sibling,
                )
            ],
        )
        flights.wait("last")

    body()


def dma(*shape):
    return pltpu.SemaphoreType.DMA(shape)


def bf(*shape):
    return pltpu.VMEM(shape, BF16)


def f32(*shape):
    return pltpu.VMEM(shape, F32)


def per_device(tokens, w_qkv_f, w_proj_f, w_merge, w_qkv_c, w_proj_c, cot_fine, cot_coarse):
    to_cells, in_send, in_own, in_halo, out_send, out_own, out_halo, to_grid = tables()
    flat = tokens.reshape(ROWS * COLS, E)
    cot_flat = cot_fine.reshape(ROWS * COLS, E)
    cot = jnp.pad(cot_coarse.reshape(36, 2048), ((0, 4), (0, 0)))
    cot = jnp.concatenate([cot[:, :1024], cot[:, 1024:]], axis=0)
    size = 16 * CELL
    wide = (LATS, WIN, 1024)
    slim = (LATS, WIN, E)
    near = pl.BlockSpec(memory_space=pltpu.VMEM)
    far = pl.BlockSpec(memory_space=pl.ANY)
    shares = [bf(4, 2, 1024, 128)] * 2 + [bf(2, 1024, 128), bf(1024, 128)]
    grad_tokens, fine_rows, coarse_sums = pl.pallas_call(
        whole,
        out_shape=[
            jax.ShapeDtypeStruct((ROWS * COLS, E), BF16),
            jax.ShapeDtypeStruct((2, 8, 8, 16, E), BF16),
            jax.ShapeDtypeStruct((2048, 128), F32),
        ],
        in_specs=[far] + [near] * 5 + [far] * 10,
        out_specs=[near] * 3,
        scratch_shapes=[
            *[bf(*t.shape) for t in (out_send, out_own, out_halo, to_grid, cot_flat)],
            *[bf(*t.shape) for t in (w_qkv_f, w_proj_f, w_merge, w_qkv_c, w_proj_c)],
            *[bf(size, E)] * 4, f32(16, 4 * WIN, WIN), bf(size, E), bf(size, E), f32(size, E),
            bf(*slim), bf(*slim),
            *[bf(224, E)] * 6,
            bf(*wide), bf(*wide), f32(WIN, 1024), bf(WIN, 1024), bf(*wide), bf(320, 2048), bf(2048, 320),
            bf(320, 2048), bf(3, 320, 256), bf(320, 256), bf(320, 256), bf(320, 768),
            bf(WIN, 1024), bf(1024, 320),
            bf(2, 4, 2, 1024, 128), *shares, *shares,
            bf(4, E, E), bf(2, E, E), bf(8, 128, E), bf(8, 128, E), bf(8, 16, E), bf(8, 16, E),
            bf(16, E), bf(8, 16, E),
            dma(10), dma(4, 2, 3), dma(9, 2, LATS), dma(2, 4), dma(2, 2, 4), dma(2, 2), dma(2, 2, 8),
        ],
        compiler_params=pltpu.CompilerParams(
            collective_id=1, has_side_effects=True, vmem_limit_bytes=VMEM_BYTES
        ),
    )(
        flat, cot, to_cells, in_send, in_own, in_halo, out_send, out_own, out_halo, to_grid, cot_flat,
        w_qkv_f, w_proj_f, w_merge, w_qkv_c, w_proj_c,
    )
    grad_fine = fine_rows.reshape(4, E, E).astype(F32) * 73728**-0.5
    coarse_sums = coarse_sums * 4608**-0.5
    grad_qkv_c = coarse_sums[256:1024].reshape(3, 2, 128, 128).transpose(0, 2, 1, 3)
    return (
        grad_tokens.reshape(tokens.shape),
        grad_fine[:3],
        grad_fine[3],
        coarse_sums[1024:],
        grad_qkv_c.reshape(3, 128, 256),
        coarse_sums[:256],
    )


def solution(mesh):
    return jax.shard_map(
        per_device,
        mesh=mesh,
        in_specs=(
            P(None, "lat", "lon", None),
            P(),
            P(),
            P("lat", None),
            P(None, None, "lat"),
            P("lat", None),
            P(None, "lat", "lon", None),
            P(None, "lat", "lon", None),
        ),
        out_specs=(
            P(None, "lat", "lon", None),
            P(),
            P(),
            P("lat", "lon"),
            P(None, "lon", "lat"),
            P("lat", "lon"),
        ),
        check_vma=False,
    )
```

```python
import jax
import jax.numpy as jnp
import numpy as np
from jax import lax
from jax.experimental import pallas as pl
from jax.experimental.pallas import tpu as pltpu
from jax.sharding import PartitionSpec as P

MESH = pl.DeviceIdType.MESH
F32 = jnp.float32
BF16 = jnp.bfloat16
EPS = 1e-05
LATS = 8
ROWS, COLS = 12, 48
WL, WC = 6, 12
CELL = 40
WIN = 80
E = 512
HALO = ((0, 128), (128, 64), (192, 32))
VMEM_BYTES = 63 * 1024 * 1024


def tables():
    win = np.zeros((ROWS, COLS), np.int64)
    cell = np.zeros((ROWS, COLS), np.int64)
    for i in range(ROWS):
        for j in range(COLS):
            win[i, j] = ((i // WL) * 4 + j // WC) * WIN + (i % WL) * WC + j % WC
            cell[i, j] = ((i % 4) * 4 + j % 4) * CELL + (i // 4) * 12 + j // 4
    size = 16 * CELL
    to_cells = np.zeros((size, ROWS * COLS), np.float32)
    in_send = np.zeros((224, size), np.float32)
    in_own = np.zeros((size, size), np.float32)
    in_halo = np.zeros((size, 224), np.float32)
    out_send = np.zeros((224, size), np.float32)
    out_own = np.zeros((size, size), np.float32)
    out_halo = np.zeros((size, 224), np.float32)
    for i in range(ROWS):
        for j in range(COLS):
            to_cells[cell[i, j], i * COLS + j] = 1
            r, c = i + 3, j + 6
            if r < ROWS and c < COLS:
                in_own[win[i, j], cell[r, c]] = 1
                out_own[cell[r, c], win[i, j]] = 1
            else:
                if c < COLS:
                    slot = (r - ROWS) * 42 + c - 6
                elif r < ROWS:
                    slot = 128 + (r - 3) * 6 + c - COLS
                else:
                    slot = 192 + (r - ROWS) * 6 + c - COLS
                in_send[slot, cell[r % ROWS, c % COLS]] = 1
                in_halo[win[i, j], slot] = 1
                out_send[slot, win[i, j]] = 1
                out_halo[cell[r % ROWS, c % COLS], slot] = 1
    return [
        jnp.asarray(t, BF16)
        for t in (to_cells, in_send, in_own, in_halo, out_send, out_own, out_halo, to_cells.T)
    ]


def mm(a, b):
    return jnp.dot(a, b, preferred_element_type=F32)


def mm_nt(a, b):
    return lax.dot_general(a, b, (((1,), (1,)), ((), ())), preferred_element_type=F32)


def mm_tn(a, b):
    return lax.dot_general(a, b, (((0,), (0,)), ((), ())), preferred_element_type=F32)


def normalize(x):
    centred = x - jnp.mean(x, axis=-1, keepdims=True)
    return centred * lax.rsqrt(jnp.mean(centred * centred, axis=-1, keepdims=True) + EPS)


def pullback(x, dy):
    centred = x - jnp.mean(x, axis=-1, keepdims=True)
    rate = lax.rsqrt(jnp.mean(centred * centred, axis=-1, keepdims=True) + EPS)
    y = centred * rate
    inner = jnp.mean(dy * y, axis=-1, keepdims=True)
    return rate * (dy - jnp.mean(dy, axis=-1, keepdims=True) - y * inner)


def total(x, axes):
    s = jnp.sum(x, axis=-1, keepdims=True)
    return jnp.sum(s, axis=axes, keepdims=True)


def group_stats(x, axis, count):
    mean = total(x, axis) * (1.0 / count)
    centred = x - mean
    rate = lax.rsqrt(total(centred * centred, axis) * (1.0 / count) + EPS)
    return centred * rate, rate


def group_pullback(x, dy, axis, count):
    y, rate = group_stats(x, axis, count)
    inner = total(dy * y, axis) * (1.0 / count)
    return rate * (dy - total(dy, axis) * (1.0 / count) - y * inner)


def head_masks():
    lane = lax.broadcasted_iota(jnp.int32, (1, 256), 1) // 64
    return [jnp.where(lane == h, 1.0, 0.0) for h in range(4)]


def stack_heads(x, masks):
    return jnp.concatenate([x * m.astype(BF16) for m in masks], axis=0)


def pick_heads(x, masks):
    out = x[:WIN] * masks[0]
    for h in range(1, 4):
        out = out + x[h * WIN : (h + 1) * WIN] * masks[h]
    return out


def softmax_rows(scores):
    weights = jnp.exp(scores - jnp.max(scores, axis=-1, keepdims=True))
    return weights / jnp.sum(weights, axis=-1, keepdims=True)


def scores_back(probs, d_probs):
    d_probs = d_probs.astype(BF16).astype(F32)
    inner = jnp.sum(d_probs * probs, axis=-1, keepdims=True)
    return (probs * (d_probs - inner) * 0.125).astype(BF16)


def greet(devices):
    barrier = pltpu.get_barrier_semaphore()
    for device in devices:
        pl.semaphore_signal(barrier, inc=1, device_id=device, device_id_type=MESH)
    pl.semaphore_wait(barrier, len(devices))


def remote(src, dst, send, recv, device):
    return pltpu.make_async_remote_copy(
        src_ref=src, dst_ref=dst, send_sem=send, recv_sem=recv, device_id=device, device_id_type=MESH
    )


class Place:
    def __init__(self):
        self.lat = lax.axis_index("lat")
        self.lon = lax.axis_index("lon")

    def lat_peer(self, k):
        return lax.rem(self.lat + k, LATS)

    def at_lat(self, k):
        return (self.lat_peer(k), self.lon)

    def halo(self, step):
        up = lax.rem(self.lat + step + LATS, LATS)
        side = lax.rem(self.lon + step + 16, 16)
        return ((up, self.lon), (self.lat, side), (up, side))

    def lon_at(self, z, y, core):
        return (self.lat, z * 4 + y * 2 + core)


def start_halo(where, step, src, dst, sems):
    copies = []
    for n, device in enumerate(where.halo(step)):
        first, count = HALO[n]
        copies.append(
            remote(
                src.at[pl.ds(first, count)],
                dst.at[pl.ds(first, count)],
                sems.at[0, n],
                sems.at[1, n],
                device,
            )
        )
        copies[-1].start()
    return copies


def wait_all(copies):
    for copy in copies:
        copy.wait()


def start_spread(where, src_of, dst, sems):
    copies = []
    for k in range(1, LATS):
        copies.append(
            remote(
                src_of(where.lat_peer(k)),
                dst.at[where.lat],
                sems.at[0, k],
                sems.at[1, k],
                where.at_lat(k),
            )
        )
        copies[-1].start()
    return copies


def finish_spread(where, src_of, dst, sems):
    for k in range(1, LATS):
        source = where.lat_peer(LATS - k)
        remote(src_of(source), dst.at[source], sems.at[0, k], sems.at[1, k], where.at_lat(k)).wait()


def unpack(x):
    x = x.astype(F32)
    width = x.shape[-1]
    halves = [x[:, :CELL].reshape(LATS * CELL, width), x[:, CELL:].reshape(LATS * CELL, width)]
    return jnp.concatenate(halves, axis=1).astype(BF16)


def pack(top, bottom):
    width = top.shape[-1]
    halves = [top.reshape(LATS, CELL, width), bottom.reshape(LATS, CELL, width)]
    return jnp.concatenate(halves, axis=1).astype(BF16)


class Flights:
    def __init__(self):
        self.open = {}

    def start(self, name, copies):
        self.open[name] = copies
        for copy in copies:
            copy.start()

    def wait(self, name):
        for copy in self.open.pop(name):
            copy.wait()


def spread(where, src_of, dst_of, sems):
    return [
        remote(
            src_of(where.lat_peer(k)), dst_of(where.lat), sems.at[0, k], sems.at[1, k], where.at_lat(k)
        )
        for k in range(1, LATS)
    ]


def halo_copies(where, step, src, dst, sems):
    copies = []
    for n, device in enumerate(where.halo(step)):
        rows = pl.ds(*HALO[n])
        copies.append(remote(src.at[rows], dst.at[rows], sems.at[0, n], sems.at[1, n], device))
    return copies


def sum_slots(ref):
    value = ref[0].astype(F32)
    for n in range(1, ref.shape[0]):
        value = value + ref[n].astype(F32)
    return value


def whole(
    tokens_h, cot, to_cells, in_send, in_own, in_halo,
    out_send_h, out_own_h, out_halo_h, to_grid_h, cot_fine_h,
    w_qkv_f_h, w_proj_f_h, w_merge_h, w_qkv_c_h, w_proj_c_h,
    grad_tokens, grad_qkv_f, grad_proj_f, grad_merge, grad_qkv_c, grad_proj_c,
    out_send, out_own, out_halo, to_grid, grid_in, w_qkv_f, w_proj_f, w_merge, w_qkv_c, w_proj_c,
    x, q, k, v, probs, mixed_f, tg, blended, merged, slices,
    send_in, got_in, send_out, got_out, got_in2, got_out2,
    part, part_got, coarse_ref, packed, normed_got, rows, rows_t, cot_rows, qkv, d_mixed_c, mixed_c, d_qkv,
    d_packed, slices_t,
    share, core_a, z_a, line_a, y_a,
    core_b, z_b, line_b, y_b,
    fine_0, pair_0, lat_0, lon_0, piece_0, fine_1, pair_1, lat_1, lon_1, piece_1,
    load_sems, halo_sems, lat_sems, share_sems, z_sems, core_sems, lon_sems, pass_sems,
):
    where = Place()
    z, y, core = where.lon // 4, lax.rem(where.lon // 2, 2), lax.rem(where.lon, 2)
    chips = [(a, b) for a in range(4) for b in range(2)]
    around = [where.lon_at(lax.rem(z + a, 4), lax.rem(y + b, 2), core) for a, b in chips]
    sibling = where.lon_at(z, y, 1 - core)
    other_y = where.lon_at(z, 1 - y, core)
    flights = Flights()

    def body():
        barrier = pltpu.get_barrier_semaphore()
        friends = [where.at_lat(n) for n in range(1, LATS)] + around[1:] + [sibling]
        friends += list(where.halo(-1)[1:]) + list(where.halo(1)[1:])
        for device in friends:
            pl.semaphore_signal(barrier, inc=1, device_id=device, device_id_type=MESH)
        flights.start("tokens", [pltpu.make_async_copy(tokens_h, grid_in, load_sems.at[9])])
        loads = (
            ("w_qkv_f", w_qkv_f_h, w_qkv_f), ("w_proj_f", w_proj_f_h, w_proj_f),
            ("out_send", out_send_h, out_send), ("out_own", out_own_h, out_own),
            ("out_halo", out_halo_h, out_halo), ("w_merge", w_merge_h, w_merge),
            ("w_proj_c", w_proj_c_h, w_proj_c), ("w_qkv_c", w_qkv_c_h, w_qkv_c),
            ("to_grid", to_grid_h, to_grid),
        )
        for n, (name, far, near) in enumerate(loads):
            flights.start(name, [pltpu.make_async_copy(far, near, load_sems.at[n])])

        flights.wait("tokens")
        cells = mm(to_cells[...], grid_in[...])
        tg[...] = cells.astype(BF16)
        flights.start("cot_fine", [pltpu.make_async_copy(cot_fine_h, grid_in, load_sems.at[9])])
        normed = normalize(cells).astype(BF16)
        send_in[...] = mm(in_send[...], normed).astype(BF16)
        pl.semaphore_wait(barrier, len(friends))
        flights.start("halo1", halo_copies(where, -1, send_in, got_in, halo_sems.at[0]))
        flights.start("cots", spread(where, lambda peer: cot, lambda lat: normed_got.at[lat], lat_sems.at[0]))
        normed_got[where.lat] = cot[...]
        own = mm(in_own[...], normed)
        flights.wait("halo1")
        x[...] = (own + mm(in_halo[...], got_in[...])).astype(BF16)
        flights.wait("w_qkv_f")
        for m, ref in enumerate((q, k, v)):
            ref[...] = mm(x[...], w_qkv_f[m]).astype(BF16)
        masks = head_masks()
        key = lax.broadcasted_iota(jnp.int32, (4 * WIN, WIN), 1)
        query = lax.broadcasted_iota(jnp.int32, (4 * WIN, WIN), 0) % WIN
        real = key < 72
        same = (key < 36) == (query < 36)
        last = where.lat == LATS - 1

        def window(w, carry):
            own_rows = pl.ds(pl.multiple_of(w * WIN, WIN), WIN)
            bound = jnp.logical_and(last, w >= 4)
            for g in range(2):
                lanes = slice(g * 256, g * 256 + 256)
                scores = mm_nt(stack_heads(q[own_rows, lanes], masks), k[own_rows, lanes]) * 0.125
                allowed = jnp.logical_and(real, jnp.logical_or(same, jnp.logical_not(bound)))
                weights = softmax_rows(jnp.where(allowed, scores, -1e30))
                probs[w * 2 + g] = weights
                mixed_f[own_rows, lanes] = pick_heads(
                    mm(weights.astype(BF16), v[own_rows, lanes]), masks
                ).astype(BF16)
            return carry

        lax.fori_loop(0, 8, window, 0, unroll=2)
        flights.wait("w_proj_f")
        out = mm(mixed_f[...], w_proj_f[...]).astype(BF16)
        flights.wait("out_send")
        send_out[...] = mm(out_send[...], out).astype(BF16)
        flights.start("halo2", halo_copies(where, 1, send_out, got_out, halo_sems.at[1]))
        flights.wait("out_own")
        flights.wait("out_halo")
        own = tg[...].astype(F32) + mm(out_own[...], out)
        flights.wait("halo2")
        blended[...] = own + mm(out_halo[...], got_out[...])
        merged[...] = (
            group_stats(blended[...].reshape(16, CELL, E), 0, 16 * E)[0]
            .reshape(LATS, WIN, E)
            .astype(BF16)
        )
        flights.start("merged", spread(where, lambda peer: merged.at[peer], lambda lat: slices.at[lat], lat_sems.at[1]))
        slices[where.lat] = merged[where.lat]
        flights.wait("cots")
        cot_rows[...] = unpack(normed_got[...])
        flights.wait("w_proj_c")
        d_mixed_c[...] = mm_nt(cot_rows[...], w_proj_c[...]).astype(BF16)
        flights.wait("w_merge")
        flights.wait("merged")

        own_rows = unpack(slices[...])

        def merge(c, carry):
            lanes = pl.ds(pl.multiple_of(c * 256, 256), 256)
            later = pl.ds(pl.multiple_of(1024 + c * 256, 256), 256)
            part[:, :, lanes] = pack(mm(own_rows, w_merge[:, lanes]), mm(own_rows, w_merge[:, later]))
            return carry

        def half(first, number):
            lanes = pl.ds(first * 512, 512)
            return spread(
                where,
                lambda peer: part.at[peer, :, lanes],
                lambda lat: part_got.at[lat, :, lanes],
                lat_sems.at[number],
            )

        lax.fori_loop(0, 2, merge, 0)
        flights.start("part_0", half(0, 2))
        lax.fori_loop(2, 4, merge, 0)
        flights.start("part_1", half(1, 3))
        part_got[where.lat] = part[where.lat]
        slices_t[...] = own_rows.astype(F32).T.astype(BF16)
        flights.wait("part_0")
        flights.wait("part_1")
        coarse_ref[...] = sum_slots(part_got)
        packed[...] = (
            group_stats(coarse_ref[...].reshape(2, CELL, 1024), 0, 2048)[0]
            .reshape(WIN, 1024)
            .astype(BF16)
        )
        flights.start("normed", spread(where, lambda peer: packed, lambda lat: normed_got.at[lat], lat_sems.at[4]))
        normed_got[where.lat] = packed[...]
        flights.wait("w_qkv_c")
        flights.wait("normed")
        rows[...] = unpack(normed_got[...])
        for m in range(3):
            qkv[m] = mm(rows[...], w_qkv_c[m]).astype(BF16)
        real_c = key % CELL < 36

        def window_c(w, carry):
            own_rows = pl.ds(pl.multiple_of(w * WIN, WIN), WIN)
            heads = stack_heads(qkv[0, own_rows], masks)
            d_heads = stack_heads(d_mixed_c[own_rows], masks)
            scores = mm_nt(heads, qkv[1, own_rows]) * 0.125
            weights = softmax_rows(jnp.where(real_c, scores, -1e30))
            weights_bf = weights.astype(BF16)
            mixed_c[own_rows] = pick_heads(mm(weights_bf, qkv[2, own_rows]), masks).astype(BF16)
            d_scores = scores_back(weights, mm_nt(d_heads, qkv[2, own_rows]))
            d_qkv[own_rows, :256] = pick_heads(mm(d_scores, qkv[1, own_rows]), masks).astype(BF16)
            d_qkv[own_rows, 256:512] = mm_tn(d_scores, heads).astype(BF16)
            d_qkv[own_rows, 512:] = mm_tn(weights_bf, d_heads).astype(BF16)
            return carry

        lax.fori_loop(0, 4, window_c, 0, unroll=2)

        def back(c, carry):
            halves = []
            for first in (0, 1024):
                part_rows = pl.ds(pl.multiple_of(first + c * 256, 256), 256)
                d_rows = mm_nt(d_qkv[:, :256], w_qkv_c[0, part_rows])
                d_rows = d_rows + mm_nt(d_qkv[:, 256:512], w_qkv_c[1, part_rows])
                halves.append(d_rows + mm_nt(d_qkv[:, 512:], w_qkv_c[2, part_rows]))
            part[:, :, pl.ds(pl.multiple_of(c * 256, 256), 256)] = pack(*halves)
            return carry

        lax.fori_loop(0, 2, back, 0)
        flights.start("d_part_0", half(0, 5))
        lax.fori_loop(2, 4, back, 0)
        flights.start("d_part_1", half(1, 6))
        part_got[where.lat] = part[where.lat]
        rows_t[...] = rows[...].astype(F32).T.astype(BF16)
        mixed_t = mixed_c[...].astype(F32).T.astype(BF16)

        def shares(m, carry):
            grad = mm(mixed_t, cot_rows[:, pl.ds(pl.multiple_of(m * 256, 256), 256)]).astype(BF16)
            for c in range(2):
                share[c, m // 2, m % 2, :256] = grad[:, c * 128 : c * 128 + 128]
                own_rows = pl.ds(pl.multiple_of(m * 256 + c * 128, 128), 128)
                grad_qkv = mm(rows_t[own_rows], d_qkv[...]).astype(BF16)
                for n in range(6):
                    share[c, m // 2, m % 2, 256 + 128 * n : 384 + 128 * n] = grad_qkv[
                        :, 128 * n : 128 * n + 128
                    ]
            return carry

        lax.fori_loop(0, 8, shares, 0)
        flights.start(
            "core_a",
            [remote(share.at[1 - core], core_a, share_sems.at[0, 0], share_sems.at[1, 0], sibling)],
        )

        def add_pairs(got):
            def add(n, carry):
                got[n] = (share[core, n].astype(F32) + got[n].astype(F32)).astype(BF16)
                return carry

            lax.fori_loop(0, 4, add, 0)

        def z_copies(src, dst, sems):
            copies = []
            for a in range(1, 4):
                there = lax.rem(z + a, 4)
                copies.append(
                    remote(
                        src.at[there], dst.at[a], sems.at[0, a], sems.at[1, a],
                        where.lon_at(there, y, core),
                    )
                )
            return copies

        flights.wait("d_part_0")
        flights.wait("d_part_1")
        d_normed = sum_slots(part_got).astype(BF16).astype(F32).reshape(2, CELL, 1024)
        d_coarse = group_pullback(coarse_ref[...].reshape(2, CELL, 1024), d_normed, 0, 2048)
        d_packed[...] = (cot[...].astype(F32) + d_coarse.reshape(WIN, 1024)).astype(BF16)
        flights.start("d_coarse", spread(where, lambda peer: d_packed, lambda lat: normed_got.at[lat], lat_sems.at[7]))
        normed_got[where.lat] = d_packed[...]
        flights.wait("core_a")
        add_pairs(core_a)
        flights.start("z_a", z_copies(core_a, z_a, z_sems.at[0]))
        flights.wait("d_coarse")
        rows[...] = unpack(normed_got[...])

        def slices_back(c, carry):
            lanes = pl.ds(pl.multiple_of(c * 256, 256), 256)
            later = pl.ds(pl.multiple_of(512 + c * 256, 256), 256)
            merged[:, :, lanes] = pack(
                mm_nt(rows[...], w_merge[lanes]), mm_nt(rows[...], w_merge[later])
            )
            return carry

        lax.fori_loop(0, 2, slices_back, 0)
        flights.start(
            "d_slices",
            spread(where, lambda peer: merged.at[peer], lambda lat: slices.at[lat], lat_sems.at[8]),
        )
        slices[where.lat] = merged[where.lat]

        def merge_shares(m, carry):
            grad = mm(slices_t[...], rows[:, pl.ds(pl.multiple_of(m * 256, 256), 256)]).astype(BF16)
            for c in range(2):
                share[c, m // 2, m % 2] = grad[:, c * 128 : c * 128 + 128]
            return carry

        lax.fori_loop(0, 8, merge_shares, 0)
        flights.start(
            "core_b",
            [remote(share.at[1 - core], core_b, share_sems.at[0, 1], share_sems.at[1, 1], sibling)],
        )
        flights.wait("d_slices")

        d_gathered = group_pullback(
            blended[...].reshape(16, CELL, E),
            slices[...].astype(F32).reshape(16, CELL, E),
            0,
            16 * E,
        )
        flights.wait("cot_fine")
        blended[...] = mm(to_cells[...], grid_in[...]) + d_gathered.reshape(16 * CELL, E)
        d_bf = blended[...].astype(BF16)
        send_in[...] = mm(in_send[...], d_bf).astype(BF16)
        flights.start("halo3", halo_copies(where, -1, send_in, got_in2, halo_sems.at[2]))
        own = mm(in_own[...], d_bf)
        flights.wait("core_b")
        add_pairs(core_b)
        flights.wait("z_a")
        z_a[0] = core_a[z]
        line_a[...] = sum_slots(z_a).astype(BF16)
        flights.start("z_b", z_copies(core_b, z_b, z_sems.at[1]))
        flights.start(
            "y_a", [remote(line_a.at[1 - y], y_a, share_sems.at[0, 2], share_sems.at[1, 2], other_y)]
        )
        flights.wait("halo3")
        d_out = (own + mm(in_halo[...], got_in2[...])).astype(BF16)
        grad = mm_tn(mixed_f[...], d_out).astype(BF16)
        for c in range(2):
            fine_0[:, :, c] = grad[:, c * 256 : c * 256 + 256].reshape(2, 8, 32, 256)
        mixed_f[...] = mm_nt(d_out, w_proj_f[...]).astype(BF16)

        def window_b(g):
            lanes = slice(g * 256, g * 256 + 256)

            def step(w, carry):
                own_rows = pl.ds(pl.multiple_of(w * WIN, WIN), WIN)
                weights = probs[w * 2 + g]
                heads = stack_heads(q[own_rows, lanes], masks)
                d_heads = stack_heads(mixed_f[own_rows, lanes], masks)
                d_scores = scores_back(weights, mm_nt(d_heads, v[own_rows, lanes]))
                new_q = pick_heads(mm(d_scores, k[own_rows, lanes]), masks).astype(BF16)
                new_k = mm_tn(d_scores, heads).astype(BF16)
                v[own_rows, lanes] = mm_tn(weights.astype(BF16), d_heads).astype(BF16)
                q[own_rows, lanes] = new_q
                k[own_rows, lanes] = new_k
                return carry

            return step

        def to_core(name, fine, pair, sems):
            flights.start(
                name, [remote(fine.at[1 - core], pair, sems.at[0], sems.at[1], sibling)]
            )

        def add_core(fine, pair):
            pair[...] = (fine[core].astype(F32) + pair[...].astype(F32)).astype(BF16)

        def to_lat(name, pair, got, sems):
            flights.start(name, spread(where, lambda peer: pair.at[peer], lambda lat: got.at[lat], sems))
            got[where.lat] = pair[where.lat]

        def to_lon(name, piece, got, sems):
            here = z * 2 + y
            copies = []
            for n in range(1, 8):
                copies.append(remote(piece, got.at[here], sems.at[0, n], sems.at[1, n], around[n]))
            flights.start(name, copies)
            got[here] = piece[...]

        def to_all(name, src, dst_of, sems, pass_sems):
            copies = spread(where, lambda peer: src, dst_of, sems)
            for copy in copies:
                copy.start()

            def to_sibling(n):
                rows_of = dst_of(lax.rem(where.lat - n + LATS, LATS))
                return remote(rows_of, rows_of, pass_sems.at[0, n], pass_sems.at[1, n], sibling)

            passed = [to_sibling(n) for n in range(LATS)]
            passed[0].start()

            def finish():
                for n in range(1, LATS):
                    copies[n - 1].wait()
                    passed[n].start()
                for copy in passed:
                    copy.wait()

            return finish

        def qkv_half(g):
            return lambda lat: grad_qkv_f.at[:, core, lat, :, pl.ds(g * 256, 256)]

        lax.fori_loop(0, 8, window_b(0), 0, unroll=2)
        x_t = x[...].astype(F32).T.astype(BF16)
        for m, ref in enumerate((q, k, v)):
            fine_0[:, :, 2 + m] = mm(x_t, ref[:, :256]).astype(BF16).reshape(2, 8, 32, 256)
        to_core("core_0", fine_0, pair_0, core_sems.at[0])
        lax.fori_loop(0, 4, window_b(1), 0, unroll=2)
        flights.wait("core_0")
        add_core(fine_0, pair_0)
        to_lat("lat_0", pair_0, lat_0, lat_sems.at[9])
        lax.fori_loop(4, 8, window_b(1), 0, unroll=2)
        for m, ref in enumerate((q, k, v)):
            fine_1[:, :, m] = mm(x_t, ref[:, 256:]).astype(BF16).reshape(2, 8, 32, 256)
        to_core("core_1", fine_1, pair_1, core_sems.at[1])
        d_shifted = mm_nt(q[...], w_qkv_f[0]) + mm_nt(k[...], w_qkv_f[1])
        d_shifted = (d_shifted + mm_nt(v[...], w_qkv_f[2])).astype(BF16)
        send_out[...] = mm(out_send[...], d_shifted).astype(BF16)
        flights.start("halo4", halo_copies(where, 1, send_out, got_out2, halo_sems.at[3]))
        flights.wait("core_1")
        add_core(fine_1, pair_1)
        to_lat("lat_1", pair_1, lat_1, lat_sems.at[10])
        flights.wait("lat_0")
        piece_0[...] = sum_slots(lat_0).astype(BF16)
        to_lon("lon_0", piece_0, lon_0, lon_sems.at[0])
        own = mm(out_own[...], d_shifted)
        flights.wait("halo4")
        d_normed = (own + mm(out_halo[...], got_out2[...])).astype(BF16).astype(F32)
        grad = blended[...] + pullback(tg[...].astype(F32), d_normed)
        flights.wait("to_grid")
        grad_tokens[...] = mm(to_grid[...], grad.astype(BF16)).astype(BF16)
        flights.wait("lat_1")
        piece_1[...] = sum_slots(lat_1).astype(BF16)
        to_lon("lon_1", piece_1, lon_1, lon_sems.at[1])
        flights.wait("lon_0")
        piece_0[...] = sum_slots(lon_0).astype(BF16)
        grad_qkv_f[:, core, where.lat, :, :256] = piece_0[2:]
        grad_proj_f[:, core, where.lat] = piece_0[:2]
        ends = [
            to_all("qkv_0", piece_0.at[pl.ds(2, 3)], qkv_half(0), lat_sems.at[11], pass_sems.at[0]),
            to_all(
                "proj", piece_0.at[pl.ds(0, 2)], lambda lat: grad_proj_f.at[:, core, lat],
                lat_sems.at[12], pass_sems.at[1],
            ),
        ]
        flights.wait("z_b")
        z_b[0] = core_b[z]
        line_b[...] = sum_slots(z_b).astype(BF16)
        flights.start(
            "y_b", [remote(line_b.at[1 - y], y_b, share_sems.at[0, 3], share_sems.at[1, 3], other_y)]
        )
        flights.wait("lon_1")
        piece_1[...] = sum_slots(lon_1).astype(BF16)
        grad_qkv_f[:, core, where.lat, :, 256:] = piece_1[...]
        ends.append(to_all("qkv_1", piece_1, qkv_half(1), lat_sems.at[13], pass_sems.at[2]))
        flights.wait("y_a")
        grad_proj_c[...] = line_a[y, :256].astype(F32) + y_a[:256].astype(F32)
        for n in range(6):
            own_rows = slice(256 + 128 * n, 384 + 128 * n)
            grad_qkv_c[n // 2, :, (n % 2) * 128 : (n % 2) * 128 + 128] = line_a[y, own_rows].astype(
                F32
            ) + y_a[own_rows].astype(F32)
        flights.wait("y_b")
        grad_merge[...] = line_b[y].astype(F32) + y_b[...].astype(F32)
        for end in ends:
            end()

    body()


def dma(*shape):
    return pltpu.SemaphoreType.DMA(shape)


def bf(*shape):
    return pltpu.VMEM(shape, BF16)


def f32(*shape):
    return pltpu.VMEM(shape, F32)


def per_device(tokens, w_qkv_f, w_proj_f, w_merge, w_qkv_c, w_proj_c, cot_fine, cot_coarse):
    to_cells, in_send, in_own, in_halo, out_send, out_own, out_halo, to_grid = tables()
    flat = tokens.reshape(ROWS * COLS, E)
    cot_flat = cot_fine.reshape(ROWS * COLS, E)
    cot = jnp.pad(cot_coarse.reshape(36, 2048), ((0, 4), (0, 0)))
    cot = jnp.concatenate([cot[:, :1024], cot[:, 1024:]], axis=0)
    size = 16 * CELL
    wide = (LATS, WIN, 1024)
    slim = (LATS, WIN, E)
    near = pl.BlockSpec(memory_space=pltpu.VMEM)
    far = pl.BlockSpec(memory_space=pl.ANY)
    shares = [bf(4, 2, 1024, 128)] * 2 + [bf(2, 1024, 128), bf(1024, 128)]
    grad_tokens, grad_qkv_f, grad_proj_f, grad_merge, grad_qkv_c, grad_proj_c = pl.pallas_call(
        whole,
        out_shape=[
            jax.ShapeDtypeStruct((ROWS * COLS, E), BF16),
            jax.ShapeDtypeStruct((3, 2, 8, 32, E), BF16),
            jax.ShapeDtypeStruct((2, 2, 8, 32, 256), BF16),
            jax.ShapeDtypeStruct((1024, 128), F32),
            jax.ShapeDtypeStruct((3, 128, 256), F32),
            jax.ShapeDtypeStruct((256, 128), F32),
        ],
        in_specs=[far] + [near] * 5 + [far] * 10,
        out_specs=[near] * 6,
        scratch_shapes=[
            *[bf(*t.shape) for t in (out_send, out_own, out_halo, to_grid, cot_flat)],
            *[bf(*t.shape) for t in (w_qkv_f, w_proj_f, w_merge, w_qkv_c, w_proj_c)],
            *[bf(size, E)] * 4, f32(16, 4 * WIN, WIN), bf(size, E), bf(size, E), f32(size, E),
            bf(*slim), bf(*slim),
            *[bf(224, E)] * 6,
            bf(*wide), bf(*wide), f32(WIN, 1024), bf(WIN, 1024), bf(*wide), bf(320, 2048), bf(2048, 320),
            bf(320, 2048), bf(3, 320, 256), bf(320, 256), bf(320, 256), bf(320, 768),
            bf(WIN, 1024), bf(1024, 320),
            bf(2, 4, 2, 1024, 128), *shares, *shares,
            bf(2, 8, 5, 32, 256), *[bf(8, 5, 32, 256)] * 3, bf(5, 32, 256),
            bf(2, 8, 3, 32, 256), *[bf(8, 3, 32, 256)] * 3, bf(3, 32, 256),
            dma(10), dma(4, 2, 3), dma(14, 2, LATS), dma(2, 4), dma(2, 2, 4), dma(2, 2), dma(2, 2, 8),
            dma(3, 2, LATS),
        ],
        compiler_params=pltpu.CompilerParams(
            collective_id=1, has_side_effects=True, vmem_limit_bytes=VMEM_BYTES
        ),
    )(
        flat, cot, to_cells, in_send, in_own, in_halo, out_send, out_own, out_halo, to_grid, cot_flat,
        w_qkv_f, w_proj_f, w_merge, w_qkv_c, w_proj_c,
    )
    fine_scale, coarse_scale = 73728**-0.5, 4608**-0.5
    proj_f = grad_proj_f.reshape(2, E, 256).astype(F32) * fine_scale
    return (
        grad_tokens.reshape(tokens.shape),
        grad_qkv_f.reshape(3, E, E).astype(F32) * fine_scale,
        jnp.concatenate([proj_f[0], proj_f[1]], axis=1),
        grad_merge * coarse_scale,
        grad_qkv_c * coarse_scale,
        grad_proj_c * coarse_scale,
    )


def solution(mesh):
    return jax.shard_map(
        per_device,
        mesh=mesh,
        in_specs=(
            P(None, "lat", "lon", None),
            P(),
            P(),
            P("lat", None),
            P(None, None, "lat"),
            P("lat", None),
            P(None, "lat", "lon", None),
            P(None, "lat", "lon", None),
        ),
        out_specs=(
            P(None, "lat", "lon", None),
            P(),
            P(),
            P("lat", "lon"),
            P(None, "lon", "lat"),
            P("lat", "lon"),
        ),
        check_vma=False,
    )
```

```python
import jax
import jax.numpy as jnp
import numpy as np
from jax import lax
from jax.experimental import pallas as pl
from jax.experimental.pallas import tpu as pltpu
from jax.sharding import PartitionSpec as P

MESH = pl.DeviceIdType.MESH
F32 = jnp.float32
BF16 = jnp.bfloat16
EPS = 1e-05
LATS = 8
ROWS, COLS = 12, 48
WL, WC = 6, 12
CELL = 40
WIN = 80
E = 512
HALO = ((0, 128), (128, 64), (192, 32))
VMEM_BYTES = 63 * 1024 * 1024


def tables():
    win = np.zeros((ROWS, COLS), np.int64)
    cell = np.zeros((ROWS, COLS), np.int64)
    for i in range(ROWS):
        for j in range(COLS):
            win[i, j] = ((i // WL) * 4 + j // WC) * WIN + (i % WL) * WC + j % WC
            cell[i, j] = ((i % 4) * 4 + j % 4) * CELL + (i // 4) * 12 + j // 4
    size = 16 * CELL
    to_cells = np.zeros((size, ROWS * COLS), np.float32)
    in_send = np.zeros((224, size), np.float32)
    in_own = np.zeros((size, size), np.float32)
    in_halo = np.zeros((size, 224), np.float32)
    out_send = np.zeros((224, size), np.float32)
    out_own = np.zeros((size, size), np.float32)
    out_halo = np.zeros((size, 224), np.float32)
    for i in range(ROWS):
        for j in range(COLS):
            to_cells[cell[i, j], i * COLS + j] = 1
            r, c = i + 3, j + 6
            if r < ROWS and c < COLS:
                in_own[win[i, j], cell[r, c]] = 1
                out_own[cell[r, c], win[i, j]] = 1
            else:
                if c < COLS:
                    slot = (r - ROWS) * 42 + c - 6
                elif r < ROWS:
                    slot = 128 + (r - 3) * 6 + c - COLS
                else:
                    slot = 192 + (r - ROWS) * 6 + c - COLS
                in_send[slot, cell[r % ROWS, c % COLS]] = 1
                in_halo[win[i, j], slot] = 1
                out_send[slot, win[i, j]] = 1
                out_halo[cell[r % ROWS, c % COLS], slot] = 1
    return [
        jnp.asarray(t, BF16)
        for t in (to_cells, in_send, in_own, in_halo, out_send, out_own, out_halo, to_cells.T)
    ]


def mm(a, b):
    return jnp.dot(a, b, preferred_element_type=F32)


def mm_nt(a, b):
    return lax.dot_general(a, b, (((1,), (1,)), ((), ())), preferred_element_type=F32)


def mm_tn(a, b):
    return lax.dot_general(a, b, (((0,), (0,)), ((), ())), preferred_element_type=F32)


def normalize(x):
    centred = x - jnp.mean(x, axis=-1, keepdims=True)
    return centred * lax.rsqrt(jnp.mean(centred * centred, axis=-1, keepdims=True) + EPS)


def pullback(x, dy):
    centred = x - jnp.mean(x, axis=-1, keepdims=True)
    rate = lax.rsqrt(jnp.mean(centred * centred, axis=-1, keepdims=True) + EPS)
    y = centred * rate
    inner = jnp.mean(dy * y, axis=-1, keepdims=True)
    return rate * (dy - jnp.mean(dy, axis=-1, keepdims=True) - y * inner)


def total(x, axes):
    s = jnp.sum(x, axis=-1, keepdims=True)
    return jnp.sum(s, axis=axes, keepdims=True)


def group_stats(x, axis, count):
    mean = total(x, axis) * (1.0 / count)
    centred = x - mean
    rate = lax.rsqrt(total(centred * centred, axis) * (1.0 / count) + EPS)
    return centred * rate, rate


def group_pullback(x, dy, axis, count):
    y, rate = group_stats(x, axis, count)
    inner = total(dy * y, axis) * (1.0 / count)
    return rate * (dy - total(dy, axis) * (1.0 / count) - y * inner)


def head_masks():
    lane = lax.broadcasted_iota(jnp.int32, (1, 256), 1) // 64
    return [jnp.where(lane == h, 1.0, 0.0) for h in range(4)]


def stack_heads(x, masks):
    return jnp.concatenate([x * m.astype(BF16) for m in masks], axis=0)


def pick_heads(x, masks):
    out = x[:WIN] * masks[0]
    for h in range(1, 4):
        out = out + x[h * WIN : (h + 1) * WIN] * masks[h]
    return out


def softmax_rows(scores):
    weights = jnp.exp(scores - jnp.max(scores, axis=-1, keepdims=True))
    return weights / jnp.sum(weights, axis=-1, keepdims=True)


def scores_back(probs, d_probs):
    d_probs = d_probs.astype(BF16).astype(F32)
    inner = jnp.sum(d_probs * probs, axis=-1, keepdims=True)
    return (probs * (d_probs - inner) * 0.125).astype(BF16)


def greet(devices):
    barrier = pltpu.get_barrier_semaphore()
    for device in devices:
        pl.semaphore_signal(barrier, inc=1, device_id=device, device_id_type=MESH)
    pl.semaphore_wait(barrier, len(devices))


def remote(src, dst, send, recv, device):
    return pltpu.make_async_remote_copy(
        src_ref=src, dst_ref=dst, send_sem=send, recv_sem=recv, device_id=device, device_id_type=MESH
    )


class Place:
    def __init__(self):
        self.lat = lax.axis_index("lat")
        self.lon = lax.axis_index("lon")

    def lat_peer(self, k):
        return lax.rem(self.lat + k, LATS)

    def at_lat(self, k):
        return (self.lat_peer(k), self.lon)

    def halo(self, step):
        up = lax.rem(self.lat + step + LATS, LATS)
        side = lax.rem(self.lon + step + 16, 16)
        return ((up, self.lon), (self.lat, side), (up, side))

    def lon_at(self, z, y, core):
        return (self.lat, z * 4 + y * 2 + core)


def start_halo(where, step, src, dst, sems):
    copies = []
    for n, device in enumerate(where.halo(step)):
        first, count = HALO[n]
        copies.append(
            remote(
                src.at[pl.ds(first, count)],
                dst.at[pl.ds(first, count)],
                sems.at[0, n],
                sems.at[1, n],
                device,
            )
        )
        copies[-1].start()
    return copies


def wait_all(copies):
    for copy in copies:
        copy.wait()


def start_spread(where, src_of, dst, sems):
    copies = []
    for k in range(1, LATS):
        copies.append(
            remote(
                src_of(where.lat_peer(k)),
                dst.at[where.lat],
                sems.at[0, k],
                sems.at[1, k],
                where.at_lat(k),
            )
        )
        copies[-1].start()
    return copies


def finish_spread(where, src_of, dst, sems):
    for k in range(1, LATS):
        source = where.lat_peer(LATS - k)
        remote(src_of(source), dst.at[source], sems.at[0, k], sems.at[1, k], where.at_lat(k)).wait()


def unpack(x):
    x = x.astype(F32)
    width = x.shape[-1]
    halves = [x[:, :CELL].reshape(LATS * CELL, width), x[:, CELL:].reshape(LATS * CELL, width)]
    return jnp.concatenate(halves, axis=1).astype(BF16)


def pack(top, bottom):
    width = top.shape[-1]
    halves = [top.reshape(LATS, CELL, width), bottom.reshape(LATS, CELL, width)]
    return jnp.concatenate(halves, axis=1).astype(BF16)


def swap_halves(x):
    low = lax.broadcasted_iota(jnp.int32, x.shape, 0) % 8 < 4
    count = x.shape[0]
    return jnp.where(low, pltpu.roll(x, count - 4, 0), pltpu.roll(x, 4, 0))


def fold(parts):
    n, _, width = parts[0].shape
    low = lax.broadcasted_iota(jnp.int32, (n * 8, width), 0) % 8 < 4
    pieces = [p[:, :32] for p in parts]
    for c in (0, 2):
        first = parts[c][:, 32:].reshape(n * 8, width)
        second = swap_halves(parts[c + 1][:, 32:].reshape(n * 8, width))
        pieces.append(jnp.where(low, first, second).reshape(n, 8, width))
    return jnp.concatenate(pieces, axis=1)


def unfold(x):
    n, _, width = x.shape
    low = lax.broadcasted_iota(jnp.int32, (n * 8, width), 0) % 8 < 4
    parts = []
    for c in range(4):
        tail = x[:, 128 + c // 2 * 8 : 136 + c // 2 * 8].reshape(n * 8, width)
        if c % 2:
            tail = swap_halves(tail)
        tail = jnp.where(low, tail, 0.0).reshape(n, 8, width)
        parts.append(jnp.concatenate([x[:, c * 32 : c * 32 + 32], tail], axis=1))
    return parts


def unfold_rows(x):
    parts = [p.reshape(LATS * CELL, 512) for p in unfold(x.astype(F32))]
    return jnp.concatenate(parts, axis=1).astype(BF16)


def unfold_one(x):
    return jnp.concatenate(unfold(x[None]), axis=0)


def fold_one(x):
    return fold([x[c : c + 1] for c in range(4)])[0]


class Flights:
    def __init__(self):
        self.open = {}

    def start(self, name, copies):
        self.open[name] = copies
        for copy in copies:
            copy.start()

    def wait(self, name):
        for copy in self.open.pop(name):
            copy.wait()


def spread(where, src_of, dst_of, sems):
    return [
        remote(
            src_of(where.lat_peer(k)), dst_of(where.lat), sems.at[0, k], sems.at[1, k], where.at_lat(k)
        )
        for k in range(1, LATS)
    ]


def halo_copies(where, step, src, dst, sems):
    copies = []
    for n, device in enumerate(where.halo(step)):
        rows = pl.ds(*HALO[n])
        copies.append(remote(src.at[rows], dst.at[rows], sems.at[0, n], sems.at[1, n], device))
    return copies


def sum_slots(ref):
    value = ref[0].astype(F32)
    for n in range(1, ref.shape[0]):
        value = value + ref[n].astype(F32)
    return value


def whole(
    tokens_h, cot_rows_in, to_cells, in_send, in_own, in_halo,
    out_send_h, out_own_h, out_halo_h, to_grid_h, cot_fine_h,
    w_qkv_f_h, w_proj_f_h, w_merge_h, w_qkv_c_h, w_proj_c_h,
    grad_tokens, grad_qkv_f, grad_proj_f, grad_merge, grad_qkv_c, grad_proj_c,
    out_send, out_own, out_halo, to_grid, grid_in, w_qkv_f, w_proj_f, w_merge, w_qkv_c, w_proj_c,
    x, q, k, v, probs, mixed_f, tg, blended, merged, slices,
    send_in, got_in, send_out, got_out, got_in2, got_out2,
    cot, part, part_got, coarse_ref, packed, normed_got, rows, rows_t, cot_rows, qkv, d_mixed_c, mixed_c, d_qkv,
    d_packed, slices_t,
    share, core_a, z_a, line_a, y_a,
    core_b, z_b, line_b, y_b,
    fine_0, pair_0, lat_0, lon_0, piece_0, fine_1, pair_1, lat_1, lon_1, piece_1,
    load_sems, halo_sems, lat_sems, share_sems, z_sems, core_sems, lon_sems, pass_sems,
):
    where = Place()
    z, y, core = where.lon // 4, lax.rem(where.lon // 2, 2), lax.rem(where.lon, 2)
    chips = [(a, b) for a in range(4) for b in range(2)]
    around = [where.lon_at(lax.rem(z + a, 4), lax.rem(y + b, 2), core) for a, b in chips]
    sibling = where.lon_at(z, y, 1 - core)
    other_y = where.lon_at(z, 1 - y, core)
    flights = Flights()

    def body():
        barrier = pltpu.get_barrier_semaphore()
        friends = [where.at_lat(n) for n in range(1, LATS)] + around[1:] + [sibling]
        friends += list(where.halo(-1)[1:]) + list(where.halo(1)[1:])
        for device in friends:
            pl.semaphore_signal(barrier, inc=1, device_id=device, device_id_type=MESH)
        flights.start("tokens", [pltpu.make_async_copy(tokens_h, grid_in, load_sems.at[9])])
        loads = (
            ("w_qkv_f", w_qkv_f_h, w_qkv_f), ("w_proj_f", w_proj_f_h, w_proj_f),
            ("out_send", out_send_h, out_send), ("out_own", out_own_h, out_own),
            ("out_halo", out_halo_h, out_halo), ("w_merge", w_merge_h, w_merge),
            ("w_proj_c", w_proj_c_h, w_proj_c), ("w_qkv_c", w_qkv_c_h, w_qkv_c),
            ("to_grid", to_grid_h, to_grid),
        )
        for n, (name, far, near) in enumerate(loads):
            flights.start(name, [pltpu.make_async_copy(far, near, load_sems.at[n])])

        cot_wide = cot_rows_in[...].astype(F32)
        cot[...] = fold([cot_wide[None, :, c * 512 : c * 512 + 512] for c in range(4)])[0].astype(BF16)
        flights.wait("tokens")
        cells = mm(to_cells[...], grid_in[...])
        tg[...] = cells.astype(BF16)
        flights.start("cot_fine", [pltpu.make_async_copy(cot_fine_h, grid_in, load_sems.at[9])])
        normed = normalize(cells).astype(BF16)
        send_in[...] = mm(in_send[...], normed).astype(BF16)
        pl.semaphore_wait(barrier, len(friends))
        flights.start("halo1", halo_copies(where, -1, send_in, got_in, halo_sems.at[0]))
        flights.start("cots", spread(where, lambda peer: cot, lambda lat: normed_got.at[lat], lat_sems.at[0]))
        normed_got[where.lat] = cot[...]
        own = mm(in_own[...], normed)
        flights.wait("halo1")
        x[...] = (own + mm(in_halo[...], got_in[...])).astype(BF16)
        flights.wait("w_qkv_f")
        for m, ref in enumerate((q, k, v)):
            ref[...] = mm(x[...], w_qkv_f[m]).astype(BF16)
        masks = head_masks()
        key = lax.broadcasted_iota(jnp.int32, (4 * WIN, WIN), 1)
        query = lax.broadcasted_iota(jnp.int32, (4 * WIN, WIN), 0) % WIN
        real = key < 72
        same = (key < 36) == (query < 36)
        last = where.lat == LATS - 1

        def window(w, carry):
            own_rows = pl.ds(pl.multiple_of(w * WIN, WIN), WIN)
            bound = jnp.logical_and(last, w >= 4)
            for g in range(2):
                lanes = slice(g * 256, g * 256 + 256)
                scores = mm_nt(stack_heads(q[own_rows, lanes], masks), k[own_rows, lanes]) * 0.125
                allowed = jnp.logical_and(real, jnp.logical_or(same, jnp.logical_not(bound)))
                weights = softmax_rows(jnp.where(allowed, scores, -1e30))
                probs[w * 2 + g] = weights
                mixed_f[own_rows, lanes] = pick_heads(
                    mm(weights.astype(BF16), v[own_rows, lanes]), masks
                ).astype(BF16)
            return carry

        lax.fori_loop(0, 8, window, 0, unroll=2)
        flights.wait("w_proj_f")
        out = mm(mixed_f[...], w_proj_f[...]).astype(BF16)
        flights.wait("out_send")
        send_out[...] = mm(out_send[...], out).astype(BF16)
        flights.start("halo2", halo_copies(where, 1, send_out, got_out, halo_sems.at[1]))
        flights.wait("out_own")
        flights.wait("out_halo")
        own = tg[...].astype(F32) + mm(out_own[...], out)
        flights.wait("halo2")
        blended[...] = own + mm(out_halo[...], got_out[...])
        merged[...] = (
            group_stats(blended[...].reshape(16, CELL, E), 0, 16 * E)[0]
            .reshape(LATS, WIN, E)
            .astype(BF16)
        )
        flights.start("merged", spread(where, lambda peer: merged.at[peer], lambda lat: slices.at[lat], lat_sems.at[1]))
        slices[where.lat] = merged[where.lat]
        flights.wait("cots")
        cot_rows[...] = unfold_rows(normed_got[...])
        flights.wait("w_proj_c")
        d_mixed_c[...] = mm_nt(cot_rows[...], w_proj_c[...]).astype(BF16)
        flights.wait("w_merge")
        flights.wait("merged")

        own_rows = unpack(slices[...])

        def merge(c, carry):
            quarters = []
            for n in range(4):
                lanes = pl.ds(pl.multiple_of(n * 512 + c * 256, 256), 256)
                quarters.append(mm(own_rows, w_merge[:, lanes]).reshape(LATS, CELL, 256))
            part[:, :, pl.ds(pl.multiple_of(c * 256, 256), 256)] = fold(quarters).astype(BF16)
            return carry

        def half(first, number):
            lanes = pl.ds(first * 256, 256)
            return spread(
                where,
                lambda peer: part.at[peer, :, lanes],
                lambda lat: part_got.at[lat, :, lanes],
                lat_sems.at[number],
            )

        merge(0, 0)
        flights.start("part_0", half(0, 2))
        merge(1, 0)
        flights.start("part_1", half(1, 3))
        part_got[where.lat] = part[where.lat]
        slices_t[...] = own_rows.astype(F32).T.astype(BF16)
        flights.wait("part_0")
        flights.wait("part_1")
        coarse_ref[...] = unfold_one(sum_slots(part_got))
        packed[...] = fold_one(group_stats(coarse_ref[...], 0, 2048)[0]).astype(BF16)
        flights.start("normed", spread(where, lambda peer: packed, lambda lat: normed_got.at[lat], lat_sems.at[4]))
        normed_got[where.lat] = packed[...]
        flights.wait("w_qkv_c")
        flights.wait("normed")
        rows[...] = unfold_rows(normed_got[...])
        for m in range(3):
            qkv[m] = mm(rows[...], w_qkv_c[m]).astype(BF16)
        real_c = key % CELL < 36

        def window_c(w, carry):
            own_rows = pl.ds(pl.multiple_of(w * WIN, WIN), WIN)
            heads = stack_heads(qkv[0, own_rows], masks)
            d_heads = stack_heads(d_mixed_c[own_rows], masks)
            scores = mm_nt(heads, qkv[1, own_rows]) * 0.125
            weights = softmax_rows(jnp.where(real_c, scores, -1e30))
            weights_bf = weights.astype(BF16)
            mixed_c[own_rows] = pick_heads(mm(weights_bf, qkv[2, own_rows]), masks).astype(BF16)
            d_scores = scores_back(weights, mm_nt(d_heads, qkv[2, own_rows]))
            d_qkv[own_rows, :256] = pick_heads(mm(d_scores, qkv[1, own_rows]), masks).astype(BF16)
            d_qkv[own_rows, 256:512] = mm_tn(d_scores, heads).astype(BF16)
            d_qkv[own_rows, 512:] = mm_tn(weights_bf, d_heads).astype(BF16)
            return carry

        lax.fori_loop(0, 4, window_c, 0, unroll=2)

        def back(c, carry):
            quarters = []
            for n in range(4):
                part_rows = pl.ds(pl.multiple_of(n * 512 + c * 256, 256), 256)
                d_rows = mm_nt(d_qkv[:, :256], w_qkv_c[0, part_rows])
                d_rows = d_rows + mm_nt(d_qkv[:, 256:512], w_qkv_c[1, part_rows])
                d_rows = d_rows + mm_nt(d_qkv[:, 512:], w_qkv_c[2, part_rows])
                quarters.append(d_rows.reshape(LATS, CELL, 256))
            part[:, :, pl.ds(pl.multiple_of(c * 256, 256), 256)] = fold(quarters).astype(BF16)
            return carry

        back(0, 0)
        flights.start("d_part_0", half(0, 5))
        back(1, 0)
        flights.start("d_part_1", half(1, 6))
        part_got[where.lat] = part[where.lat]
        rows_t[...] = rows[...].astype(F32).T.astype(BF16)
        mixed_t = mixed_c[...].astype(F32).T.astype(BF16)

        def shares(m, carry):
            grad = mm(mixed_t, cot_rows[:, pl.ds(pl.multiple_of(m * 256, 256), 256)]).astype(BF16)
            for c in range(2):
                share[c, m // 2, m % 2, :256] = grad[:, c * 128 : c * 128 + 128]
                own_rows = pl.ds(pl.multiple_of(m * 256 + c * 128, 128), 128)
                grad_qkv = mm(rows_t[own_rows], d_qkv[...]).astype(BF16)
                for n in range(6):
                    share[c, m // 2, m % 2, 256 + 128 * n : 384 + 128 * n] = grad_qkv[
                        :, 128 * n : 128 * n + 128
                    ]
            return carry

        lax.fori_loop(0, 8, shares, 0)
        flights.start(
            "core_a",
            [remote(share.at[1 - core], core_a, share_sems.at[0, 0], share_sems.at[1, 0], sibling)],
        )

        def add_pairs(got):
            def add(n, carry):
                got[n] = (share[core, n].astype(F32) + got[n].astype(F32)).astype(BF16)
                return carry

            lax.fori_loop(0, 4, add, 0)

        def z_copies(src, dst, sems):
            copies = []
            for a in range(1, 4):
                there = lax.rem(z + a, 4)
                copies.append(
                    remote(
                        src.at[there], dst.at[a], sems.at[0, a], sems.at[1, a],
                        where.lon_at(there, y, core),
                    )
                )
            return copies

        flights.wait("d_part_0")
        flights.wait("d_part_1")
        d_normed = unfold_one(sum_slots(part_got).astype(BF16).astype(F32))
        d_coarse = fold_one(group_pullback(coarse_ref[...], d_normed, 0, 2048))
        d_packed[...] = (cot[...].astype(F32) + d_coarse).astype(BF16)
        flights.start("d_coarse", spread(where, lambda peer: d_packed, lambda lat: normed_got.at[lat], lat_sems.at[7]))
        normed_got[where.lat] = d_packed[...]
        flights.wait("core_a")
        add_pairs(core_a)
        flights.start("z_a", z_copies(core_a, z_a, z_sems.at[0]))
        flights.wait("d_coarse")
        rows[...] = unfold_rows(normed_got[...])

        def slices_back(c, carry):
            lanes = pl.ds(pl.multiple_of(c * 256, 256), 256)
            later = pl.ds(pl.multiple_of(512 + c * 256, 256), 256)
            merged[:, :, lanes] = pack(
                mm_nt(rows[...], w_merge[lanes]), mm_nt(rows[...], w_merge[later])
            )
            return carry

        lax.fori_loop(0, 2, slices_back, 0)
        flights.start(
            "d_slices",
            spread(where, lambda peer: merged.at[peer], lambda lat: slices.at[lat], lat_sems.at[8]),
        )
        slices[where.lat] = merged[where.lat]

        def merge_shares(m, carry):
            grad = mm(slices_t[...], rows[:, pl.ds(pl.multiple_of(m * 256, 256), 256)]).astype(BF16)
            for c in range(2):
                share[c, m // 2, m % 2] = grad[:, c * 128 : c * 128 + 128]
            return carry

        lax.fori_loop(0, 8, merge_shares, 0)
        flights.start(
            "core_b",
            [remote(share.at[1 - core], core_b, share_sems.at[0, 1], share_sems.at[1, 1], sibling)],
        )
        flights.wait("d_slices")

        d_gathered = group_pullback(
            blended[...].reshape(16, CELL, E),
            slices[...].astype(F32).reshape(16, CELL, E),
            0,
            16 * E,
        )
        flights.wait("cot_fine")
        blended[...] = mm(to_cells[...], grid_in[...]) + d_gathered.reshape(16 * CELL, E)
        d_bf = blended[...].astype(BF16)
        send_in[...] = mm(in_send[...], d_bf).astype(BF16)
        flights.start("halo3", halo_copies(where, -1, send_in, got_in2, halo_sems.at[2]))
        own = mm(in_own[...], d_bf)
        flights.wait("core_b")
        add_pairs(core_b)
        flights.wait("z_a")
        z_a[0] = core_a[z]
        line_a[...] = sum_slots(z_a).astype(BF16)
        flights.start("z_b", z_copies(core_b, z_b, z_sems.at[1]))
        flights.start(
            "y_a", [remote(line_a.at[1 - y], y_a, share_sems.at[0, 2], share_sems.at[1, 2], other_y)]
        )
        flights.wait("halo3")
        d_out = (own + mm(in_halo[...], got_in2[...])).astype(BF16)
        grad = mm_tn(mixed_f[...], d_out).astype(BF16)
        for c in range(2):
            fine_0[:, :, c] = grad[:, c * 256 : c * 256 + 256].reshape(2, 8, 32, 256)
        mixed_f[...] = mm_nt(d_out, w_proj_f[...]).astype(BF16)

        def window_b(g):
            lanes = slice(g * 256, g * 256 + 256)

            def step(w, carry):
                own_rows = pl.ds(pl.multiple_of(w * WIN, WIN), WIN)
                weights = probs[w * 2 + g]
                heads = stack_heads(q[own_rows, lanes], masks)
                d_heads = stack_heads(mixed_f[own_rows, lanes], masks)
                d_scores = scores_back(weights, mm_nt(d_heads, v[own_rows, lanes]))
                new_q = pick_heads(mm(d_scores, k[own_rows, lanes]), masks).astype(BF16)
                new_k = mm_tn(d_scores, heads).astype(BF16)
                v[own_rows, lanes] = mm_tn(weights.astype(BF16), d_heads).astype(BF16)
                q[own_rows, lanes] = new_q
                k[own_rows, lanes] = new_k
                return carry

            return step

        def to_core(name, fine, pair, sems):
            flights.start(
                name, [remote(fine.at[1 - core], pair, sems.at[0], sems.at[1], sibling)]
            )

        def add_core(fine, pair):
            pair[...] = (fine[core].astype(F32) + pair[...].astype(F32)).astype(BF16)

        def to_lat(name, pair, got, sems):
            flights.start(name, spread(where, lambda peer: pair.at[peer], lambda lat: got.at[lat], sems))
            got[where.lat] = pair[where.lat]

        def to_lon(name, piece, got, sems):
            here = z * 2 + y
            copies = []
            for n in range(1, 8):
                copies.append(remote(piece, got.at[here], sems.at[0, n], sems.at[1, n], around[n]))
            flights.start(name, copies)
            got[here] = piece[...]

        def to_all(name, src, dst_of, sems, pass_sems):
            copies = spread(where, lambda peer: src, dst_of, sems)
            for copy in copies:
                copy.start()

            def to_sibling(n):
                rows_of = dst_of(lax.rem(where.lat - n + LATS, LATS))
                return remote(rows_of, rows_of, pass_sems.at[0, n], pass_sems.at[1, n], sibling)

            passed = [to_sibling(n) for n in range(LATS)]
            passed[0].start()

            def finish():
                for n in range(1, LATS):
                    copies[n - 1].wait()
                    passed[n].start()
                for copy in passed:
                    copy.wait()

            return finish

        def shard(lat):
            return pl.ds(pl.multiple_of(core * 256 + lat * 32, 32), 32)

        def qkv_half(g):
            return lambda lat: grad_qkv_f.at[:, shard(lat), pl.ds(g * 256, 256)]

        lax.fori_loop(0, 8, window_b(0), 0, unroll=2)
        x_t = x[...].astype(F32).T.astype(BF16)
        for m, ref in enumerate((q, k, v)):
            fine_0[:, :, 2 + m] = mm(x_t, ref[:, :256]).astype(BF16).reshape(2, 8, 32, 256)
        to_core("core_0", fine_0, pair_0, core_sems.at[0])
        lax.fori_loop(0, 4, window_b(1), 0, unroll=2)
        flights.wait("core_0")
        add_core(fine_0, pair_0)
        to_lat("lat_0", pair_0, lat_0, lat_sems.at[9])
        lax.fori_loop(4, 8, window_b(1), 0, unroll=2)
        for m, ref in enumerate((q, k, v)):
            fine_1[:, :, m] = mm(x_t, ref[:, 256:]).astype(BF16).reshape(2, 8, 32, 256)
        to_core("core_1", fine_1, pair_1, core_sems.at[1])
        d_shifted = mm_nt(q[...], w_qkv_f[0]) + mm_nt(k[...], w_qkv_f[1])
        d_shifted = (d_shifted + mm_nt(v[...], w_qkv_f[2])).astype(BF16)
        send_out[...] = mm(out_send[...], d_shifted).astype(BF16)
        flights.start("halo4", halo_copies(where, 1, send_out, got_out2, halo_sems.at[3]))
        flights.wait("lat_0")
        piece_0[...] = sum_slots(lat_0).astype(BF16)
        to_lon("lon_0", piece_0, lon_0, lon_sems.at[0])
        flights.wait("core_1")
        add_core(fine_1, pair_1)
        to_lat("lat_1", pair_1, lat_1, lat_sems.at[10])
        own = mm(out_own[...], d_shifted)
        flights.wait("halo4")
        flights.wait("lon_0")
        piece_0[...] = sum_slots(lon_0).astype(BF16)
        grad_qkv_f[:, shard(where.lat), :256] = piece_0[2:]
        grad_proj_f[:, shard(where.lat)] = piece_0[:2]
        ends = [
            to_all("qkv_0", piece_0.at[pl.ds(2, 3)], qkv_half(0), lat_sems.at[11], pass_sems.at[0]),
            to_all(
                "proj", piece_0.at[pl.ds(0, 2)], lambda lat: grad_proj_f.at[:, shard(lat)],
                lat_sems.at[12], pass_sems.at[1],
            ),
        ]
        d_normed = (own + mm(out_halo[...], got_out2[...])).astype(BF16).astype(F32)
        grad = blended[...] + pullback(tg[...].astype(F32), d_normed)
        flights.wait("to_grid")
        grad_tokens[...] = mm(to_grid[...], grad.astype(BF16)).astype(BF16)
        flights.wait("lat_1")
        piece_1[...] = sum_slots(lat_1).astype(BF16)
        to_lon("lon_1", piece_1, lon_1, lon_sems.at[1])
        flights.wait("z_b")
        z_b[0] = core_b[z]
        line_b[...] = sum_slots(z_b).astype(BF16)
        flights.start(
            "y_b", [remote(line_b.at[1 - y], y_b, share_sems.at[0, 3], share_sems.at[1, 3], other_y)]
        )
        flights.wait("lon_1")
        piece_1[...] = sum_slots(lon_1).astype(BF16)
        grad_qkv_f[:, shard(where.lat), 256:] = piece_1[...]
        ends.append(to_all("qkv_1", piece_1, qkv_half(1), lat_sems.at[13], pass_sems.at[2]))
        flights.wait("y_a")
        grad_proj_c[...] = line_a[y, :256].astype(F32) + y_a[:256].astype(F32)
        for n in range(6):
            own_rows = slice(256 + 128 * n, 384 + 128 * n)
            grad_qkv_c[n // 2, :, (n % 2) * 128 : (n % 2) * 128 + 128] = line_a[y, own_rows].astype(
                F32
            ) + y_a[own_rows].astype(F32)
        flights.wait("y_b")
        grad_merge[...] = line_b[y].astype(F32) + y_b[...].astype(F32)
        for end in ends:
            end()

    body()


def dma(*shape):
    return pltpu.SemaphoreType.DMA(shape)


def bf(*shape):
    return pltpu.VMEM(shape, BF16)


def f32(*shape):
    return pltpu.VMEM(shape, F32)


def per_device(tokens, w_qkv_f, w_proj_f, w_merge, w_qkv_c, w_proj_c, cot_fine, cot_coarse):
    to_cells, in_send, in_own, in_halo, out_send, out_own, out_halo, to_grid = tables()
    flat = tokens.reshape(ROWS * COLS, E)
    cot_flat = cot_fine.reshape(ROWS * COLS, E)
    cot = jnp.pad(cot_coarse.reshape(36, 2048), ((0, 4), (0, 0)))
    size = 16 * CELL
    wide = (LATS, 144, E)
    slim = (LATS, WIN, E)
    near = pl.BlockSpec(memory_space=pltpu.VMEM)
    far = pl.BlockSpec(memory_space=pl.ANY)
    shares = [bf(4, 2, 1024, 128)] * 2 + [bf(2, 1024, 128), bf(1024, 128)]
    grad_tokens, grad_qkv_f, grad_proj_f, grad_merge, grad_qkv_c, grad_proj_c = pl.pallas_call(
        whole,
        out_shape=[
            jax.ShapeDtypeStruct((ROWS * COLS, E), BF16),
            jax.ShapeDtypeStruct((3, E, E), BF16),
            jax.ShapeDtypeStruct((2, E, 256), BF16),
            jax.ShapeDtypeStruct((1024, 128), F32),
            jax.ShapeDtypeStruct((3, 128, 256), F32),
            jax.ShapeDtypeStruct((256, 128), F32),
        ],
        in_specs=[far] + [near] * 5 + [far] * 10,
        out_specs=[near] * 6,
        scratch_shapes=[
            *[bf(*t.shape) for t in (out_send, out_own, out_halo, to_grid, cot_flat)],
            *[bf(*t.shape) for t in (w_qkv_f, w_proj_f, w_merge, w_qkv_c, w_proj_c)],
            *[bf(size, E)] * 4, f32(16, 4 * WIN, WIN), bf(size, E), bf(size, E), f32(size, E),
            bf(*slim), bf(*slim),
            *[bf(224, E)] * 6,
            bf(144, E), bf(*wide), bf(*wide), f32(4, CELL, E), bf(144, E), bf(*wide), bf(320, 2048), bf(2048, 320),
            bf(320, 2048), bf(3, 320, 256), bf(320, 256), bf(320, 256), bf(320, 768),
            bf(144, E), bf(1024, 320),
            bf(2, 4, 2, 1024, 128), *shares, *shares,
            bf(2, 8, 5, 32, 256), *[bf(8, 5, 32, 256)] * 3, bf(5, 32, 256),
            bf(2, 8, 3, 32, 256), *[bf(8, 3, 32, 256)] * 3, bf(3, 32, 256),
            dma(10), dma(4, 2, 3), dma(14, 2, LATS), dma(2, 4), dma(2, 2, 4), dma(2, 2), dma(2, 2, 8),
            dma(3, 2, LATS),
        ],
        compiler_params=pltpu.CompilerParams(
            collective_id=1, has_side_effects=True, vmem_limit_bytes=VMEM_BYTES
        ),
    )(
        flat, cot, to_cells, in_send, in_own, in_halo, out_send, out_own, out_halo, to_grid, cot_flat,
        w_qkv_f, w_proj_f, w_merge, w_qkv_c, w_proj_c,
    )
    fine_scale, coarse_scale = 73728**-0.5, 4608**-0.5
    proj_f = grad_proj_f.astype(F32) * fine_scale
    return (
        grad_tokens.reshape(tokens.shape),
        grad_qkv_f.astype(F32) * fine_scale,
        jnp.concatenate([proj_f[0], proj_f[1]], axis=1),
        grad_merge * coarse_scale,
        grad_qkv_c * coarse_scale,
        grad_proj_c * coarse_scale,
    )


def solution(mesh):
    return jax.shard_map(
        per_device,
        mesh=mesh,
        in_specs=(
            P(None, "lat", "lon", None),
            P(),
            P(),
            P("lat", None),
            P(None, None, "lat"),
            P("lat", None),
            P(None, "lat", "lon", None),
            P(None, "lat", "lon", None),
        ),
        out_specs=(
            P(None, "lat", "lon", None),
            P(),
            P(),
            P("lat", "lon"),
            P(None, "lon", "lat"),
            P("lat", "lon"),
        ),
        check_vma=False,
    )
```

```python
import jax
import jax.numpy as jnp
import numpy as np
from jax import lax
from jax.experimental import pallas as pl
from jax.experimental.pallas import tpu as pltpu
from jax.sharding import PartitionSpec as P

MESH = pl.DeviceIdType.MESH
F32 = jnp.float32
BF16 = jnp.bfloat16
EPS = 1e-05
LATS = 8
ROWS, COLS = 12, 48
WL, WC = 6, 12
CELL = 40
WIN = 80
E = 512
HALO = ((0, 128), (128, 64), (192, 32))
VMEM_BYTES = 63 * 1024 * 1024


def tables():
    win = np.zeros((ROWS, COLS), np.int64)
    cell = np.zeros((ROWS, COLS), np.int64)
    for i in range(ROWS):
        for j in range(COLS):
            win[i, j] = ((i // WL) * 4 + j // WC) * WIN + (i % WL) * WC + j % WC
            cell[i, j] = ((i % 4) * 4 + j % 4) * CELL + (i // 4) * 12 + j // 4
    size = 16 * CELL
    to_cells = np.zeros((size, ROWS * COLS), np.float32)
    in_send = np.zeros((224, size), np.float32)
    in_own = np.zeros((size, size), np.float32)
    in_halo = np.zeros((size, 224), np.float32)
    out_send = np.zeros((224, size), np.float32)
    out_own = np.zeros((size, size), np.float32)
    out_halo = np.zeros((size, 224), np.float32)
    for i in range(ROWS):
        for j in range(COLS):
            to_cells[cell[i, j], i * COLS + j] = 1
            r, c = i + 3, j + 6
            if r < ROWS and c < COLS:
                in_own[win[i, j], cell[r, c]] = 1
                out_own[cell[r, c], win[i, j]] = 1
            else:
                if c < COLS:
                    slot = (r - ROWS) * 42 + c - 6
                elif r < ROWS:
                    slot = 128 + (r - 3) * 6 + c - COLS
                else:
                    slot = 192 + (r - ROWS) * 6 + c - COLS
                in_send[slot, cell[r % ROWS, c % COLS]] = 1
                in_halo[win[i, j], slot] = 1
                out_send[slot, win[i, j]] = 1
                out_halo[cell[r % ROWS, c % COLS], slot] = 1
    return [
        jnp.asarray(t, BF16)
        for t in (to_cells, in_send, in_own, in_halo, out_send, out_own, out_halo, to_cells.T)
    ]


def mm(a, b):
    return jnp.dot(a, b, preferred_element_type=F32)


def mm_nt(a, b):
    return lax.dot_general(a, b, (((1,), (1,)), ((), ())), preferred_element_type=F32)


def mm_tn(a, b):
    return lax.dot_general(a, b, (((0,), (0,)), ((), ())), preferred_element_type=F32)


def normalize(x):
    centred = x - jnp.mean(x, axis=-1, keepdims=True)
    return centred * lax.rsqrt(jnp.mean(centred * centred, axis=-1, keepdims=True) + EPS)


def pullback(x, dy):
    centred = x - jnp.mean(x, axis=-1, keepdims=True)
    rate = lax.rsqrt(jnp.mean(centred * centred, axis=-1, keepdims=True) + EPS)
    y = centred * rate
    inner = jnp.mean(dy * y, axis=-1, keepdims=True)
    return rate * (dy - jnp.mean(dy, axis=-1, keepdims=True) - y * inner)


def total(x, axes):
    s = jnp.sum(x, axis=-1, keepdims=True)
    return jnp.sum(s, axis=axes, keepdims=True)


def group_stats(x, axis, count):
    mean = total(x, axis) * (1.0 / count)
    centred = x - mean
    rate = lax.rsqrt(total(centred * centred, axis) * (1.0 / count) + EPS)
    return centred * rate, rate


def group_pullback(x, dy, axis, count):
    y, rate = group_stats(x, axis, count)
    inner = total(dy * y, axis) * (1.0 / count)
    return rate * (dy - total(dy, axis) * (1.0 / count) - y * inner)


def head_masks():
    lane = lax.broadcasted_iota(jnp.int32, (1, 256), 1) // 64
    return [jnp.where(lane == h, 1.0, 0.0) for h in range(4)]


def stack_heads(x, masks):
    return jnp.concatenate([x * m.astype(BF16) for m in masks], axis=0)


def pick_heads(x, masks):
    out = x[:WIN] * masks[0]
    for h in range(1, 4):
        out = out + x[h * WIN : (h + 1) * WIN] * masks[h]
    return out


def softmax_rows(scores):
    weights = jnp.exp(scores - jnp.max(scores, axis=-1, keepdims=True))
    return weights / jnp.sum(weights, axis=-1, keepdims=True)


def scores_back(probs, d_probs):
    d_probs = d_probs.astype(BF16).astype(F32)
    inner = jnp.sum(d_probs * probs, axis=-1, keepdims=True)
    return (probs * (d_probs - inner) * 0.125).astype(BF16)


def greet(devices):
    barrier = pltpu.get_barrier_semaphore()
    for device in devices:
        pl.semaphore_signal(barrier, inc=1, device_id=device, device_id_type=MESH)
    pl.semaphore_wait(barrier, len(devices))


def remote(src, dst, send, recv, device):
    return pltpu.make_async_remote_copy(
        src_ref=src, dst_ref=dst, send_sem=send, recv_sem=recv, device_id=device, device_id_type=MESH
    )


class Place:
    def __init__(self):
        self.lat = lax.axis_index("lat")
        self.lon = lax.axis_index("lon")

    def lat_peer(self, k):
        return lax.rem(self.lat + k, LATS)

    def at_lat(self, k):
        return (self.lat_peer(k), self.lon)

    def halo(self, step):
        up = lax.rem(self.lat + step + LATS, LATS)
        side = lax.rem(self.lon + step + 16, 16)
        return ((up, self.lon), (self.lat, side), (up, side))

    def lon_at(self, z, y, core):
        return (self.lat, z * 4 + y * 2 + core)


def start_halo(where, step, src, dst, sems):
    copies = []
    for n, device in enumerate(where.halo(step)):
        first, count = HALO[n]
        copies.append(
            remote(
                src.at[pl.ds(first, count)],
                dst.at[pl.ds(first, count)],
                sems.at[0, n],
                sems.at[1, n],
                device,
            )
        )
        copies[-1].start()
    return copies


def wait_all(copies):
    for copy in copies:
        copy.wait()


def start_spread(where, src_of, dst, sems):
    copies = []
    for k in range(1, LATS):
        copies.append(
            remote(
                src_of(where.lat_peer(k)),
                dst.at[where.lat],
                sems.at[0, k],
                sems.at[1, k],
                where.at_lat(k),
            )
        )
        copies[-1].start()
    return copies


def finish_spread(where, src_of, dst, sems):
    for k in range(1, LATS):
        source = where.lat_peer(LATS - k)
        remote(src_of(source), dst.at[source], sems.at[0, k], sems.at[1, k], where.at_lat(k)).wait()


def unpack(x):
    x = x.astype(F32)
    width = x.shape[-1]
    halves = [x[:, :CELL].reshape(LATS * CELL, width), x[:, CELL:].reshape(LATS * CELL, width)]
    return jnp.concatenate(halves, axis=1).astype(BF16)


def pack(top, bottom):
    width = top.shape[-1]
    halves = [top.reshape(LATS, CELL, width), bottom.reshape(LATS, CELL, width)]
    return jnp.concatenate(halves, axis=1).astype(BF16)


def swap_halves(x):
    low = lax.broadcasted_iota(jnp.int32, x.shape, 0) % 8 < 4
    count = x.shape[0]
    return jnp.where(low, pltpu.roll(x, count - 4, 0), pltpu.roll(x, 4, 0))


def fold(parts):
    n, _, width = parts[0].shape
    low = lax.broadcasted_iota(jnp.int32, (n * 8, width), 0) % 8 < 4
    pieces = [p[:, :32] for p in parts]
    for c in (0, 2):
        first = parts[c][:, 32:].reshape(n * 8, width)
        second = swap_halves(parts[c + 1][:, 32:].reshape(n * 8, width))
        pieces.append(jnp.where(low, first, second).reshape(n, 8, width))
    return jnp.concatenate(pieces, axis=1)


def unfold(x):
    n, _, width = x.shape
    low = lax.broadcasted_iota(jnp.int32, (n * 8, width), 0) % 8 < 4
    parts = []
    for c in range(4):
        tail = x[:, 128 + c // 2 * 8 : 136 + c // 2 * 8].reshape(n * 8, width)
        if c % 2:
            tail = swap_halves(tail)
        tail = jnp.where(low, tail, 0.0).reshape(n, 8, width)
        parts.append(jnp.concatenate([x[:, c * 32 : c * 32 + 32], tail], axis=1))
    return parts


def unfold_rows(x):
    parts = [p.reshape(LATS * CELL, 512) for p in unfold(x.astype(F32))]
    return jnp.concatenate(parts, axis=1).astype(BF16)


def unfold_one(x):
    return jnp.concatenate(unfold(x[None]), axis=0)


def fold_one(x):
    return fold([x[c : c + 1] for c in range(4)])[0]


class Flights:
    def __init__(self):
        self.open = {}

    def start(self, name, copies):
        self.open[name] = copies
        for copy in copies:
            copy.start()

    def wait(self, name):
        for copy in self.open.pop(name):
            copy.wait()


def spread(where, src_of, dst_of, sems):
    return [
        remote(
            src_of(where.lat_peer(k)), dst_of(where.lat), sems.at[0, k], sems.at[1, k], where.at_lat(k)
        )
        for k in range(1, LATS)
    ]


def halo_copies(where, step, src, dst, sems):
    copies = []
    for n, device in enumerate(where.halo(step)):
        rows = pl.ds(*HALO[n])
        copies.append(remote(src.at[rows], dst.at[rows], sems.at[0, n], sems.at[1, n], device))
    return copies


def sum_slots(ref):
    value = ref[0].astype(F32)
    for n in range(1, ref.shape[0]):
        value = value + ref[n].astype(F32)
    return value


def whole(
    cot_in, tokens_h, to_cells_h, in_send_h, in_own_h, in_halo_h,
    out_send_h, out_own_h, out_halo_h, to_grid_h, cot_fine_h,
    w_qkv_f_h, w_proj_f_h, w_merge_h, w_qkv_c_h, w_proj_c_h,
    grad_tokens, grad_qkv_f, grad_proj_f, grad_merge, grad_qkv_c, grad_proj_c,
    to_cells, in_send, in_own, in_halo, out_send, out_own, out_halo, to_grid, grid_in, w_qkv_f, w_proj_f, w_merge, w_qkv_c, w_proj_c,
    x, q, k, v, probs, mixed_f, tg, blended, merged, slices,
    send_in, got_in, send_out, got_out, got_in2, got_out2,
    cot, part, part_got, coarse_ref, packed, normed_got, rows, rows_t, cot_rows, qkv, d_mixed_c, mixed_c, d_qkv,
    d_packed, slices_t,
    share, core_a, z_a, line_a, y_a,
    core_b, z_b, line_b, y_b,
    fine_0, pair_0, lat_0, lon_0, piece_0, fine_1, pair_1, lat_1, lon_1, piece_1,
    load_sems, halo_sems, lat_sems, share_sems, z_sems, core_sems, lon_sems, pass_sems,
):
    where = Place()
    z, y, core = where.lon // 4, lax.rem(where.lon // 2, 2), lax.rem(where.lon, 2)
    chips = [(a, b) for a in range(4) for b in range(2)]
    around = [where.lon_at(lax.rem(z + a, 4), lax.rem(y + b, 2), core) for a, b in chips]
    sibling = where.lon_at(z, y, 1 - core)
    other_y = where.lon_at(z, 1 - y, core)
    flights = Flights()

    def body():
        barrier = pltpu.get_barrier_semaphore()
        friends = [where.at_lat(n) for n in range(1, LATS)] + around[1:] + [sibling]
        friends += list(where.halo(-1)[1:]) + list(where.halo(1)[1:])
        for device in friends:
            pl.semaphore_signal(barrier, inc=1, device_id=device, device_id_type=MESH)
        flights.start("tokens", [pltpu.make_async_copy(tokens_h, grid_in, load_sems.at[13])])
        loads = (
            ("to_cells", to_cells_h, to_cells), ("in_send", in_send_h, in_send),
            ("in_own", in_own_h, in_own), ("in_halo", in_halo_h, in_halo),
            ("w_qkv_f", w_qkv_f_h, w_qkv_f), ("w_proj_f", w_proj_f_h, w_proj_f),
            ("out_send", out_send_h, out_send), ("out_own", out_own_h, out_own),
            ("out_halo", out_halo_h, out_halo), ("w_merge", w_merge_h, w_merge),
            ("w_proj_c", w_proj_c_h, w_proj_c), ("w_qkv_c", w_qkv_c_h, w_qkv_c),
            ("to_grid", to_grid_h, to_grid),
        )
        for n, (name, far, near) in enumerate(loads):
            flights.start(name, [pltpu.make_async_copy(far, near, load_sems.at[n])])

        target = lax.broadcasted_iota(jnp.int32, (CELL, 12), 0)
        column = lax.broadcasted_iota(jnp.int32, (CELL, 12), 1)
        cot_wide = jnp.zeros((CELL, 2048), F32)
        for n in range(3):
            place = jnp.where(target == column + 12 * n, 1.0, 0.0).astype(BF16)
            cot_wide = cot_wide + mm(place, cot_in[n])
        cot[...] = fold([cot_wide[None, :, c * 512 : c * 512 + 512] for c in range(4)])[0].astype(BF16)
        flights.wait("tokens")
        flights.wait("to_cells")
        cells = mm(to_cells[...], grid_in[...])
        tg[...] = cells.astype(BF16)
        flights.start("cot_fine", [pltpu.make_async_copy(cot_fine_h, grid_in, load_sems.at[13])])
        normed = normalize(cells).astype(BF16)
        flights.wait("in_send")
        send_in[...] = mm(in_send[...], normed).astype(BF16)
        pl.semaphore_wait(barrier, len(friends))
        flights.start("halo1", halo_copies(where, -1, send_in, got_in, halo_sems.at[0]))
        flights.start("cots", spread(where, lambda peer: cot, lambda lat: normed_got.at[lat], lat_sems.at[0]))
        normed_got[where.lat] = cot[...]
        flights.wait("in_own")
        flights.wait("in_halo")
        own = mm(in_own[...], normed)
        flights.wait("halo1")
        x[...] = (own + mm(in_halo[...], got_in[...])).astype(BF16)
        flights.wait("w_qkv_f")
        for m, ref in enumerate((q, k, v)):
            ref[...] = mm(x[...], w_qkv_f[m]).astype(BF16)
        masks = head_masks()
        key = lax.broadcasted_iota(jnp.int32, (4 * WIN, WIN), 1)
        query = lax.broadcasted_iota(jnp.int32, (4 * WIN, WIN), 0) % WIN
        real = key < 72
        same = (key < 36) == (query < 36)
        last = where.lat == LATS - 1

        def window(w, carry):
            own_rows = pl.ds(pl.multiple_of(w * WIN, WIN), WIN)
            bound = jnp.logical_and(last, w >= 4)
            for g in range(2):
                lanes = slice(g * 256, g * 256 + 256)
                scores = mm_nt(stack_heads(q[own_rows, lanes], masks), k[own_rows, lanes]) * 0.125
                allowed = jnp.logical_and(real, jnp.logical_or(same, jnp.logical_not(bound)))
                weights = softmax_rows(jnp.where(allowed, scores, -1e30))
                probs[w * 2 + g] = weights
                mixed_f[own_rows, lanes] = pick_heads(
                    mm(weights.astype(BF16), v[own_rows, lanes]), masks
                ).astype(BF16)
            return carry

        lax.fori_loop(0, 8, window, 0, unroll=2)
        flights.wait("w_proj_f")
        out = mm(mixed_f[...], w_proj_f[...]).astype(BF16)
        flights.wait("out_send")
        send_out[...] = mm(out_send[...], out).astype(BF16)
        flights.start("halo2", halo_copies(where, 1, send_out, got_out, halo_sems.at[1]))
        flights.wait("out_own")
        flights.wait("out_halo")
        own = tg[...].astype(F32) + mm(out_own[...], out)
        flights.wait("halo2")
        blended[...] = own + mm(out_halo[...], got_out[...])
        merged[...] = (
            group_stats(blended[...].reshape(16, CELL, E), 0, 16 * E)[0]
            .reshape(LATS, WIN, E)
            .astype(BF16)
        )
        flights.start("merged", spread(where, lambda peer: merged.at[peer], lambda lat: slices.at[lat], lat_sems.at[1]))
        slices[where.lat] = merged[where.lat]
        flights.wait("cots")
        cot_rows[...] = unfold_rows(normed_got[...])
        flights.wait("w_proj_c")
        d_mixed_c[...] = mm_nt(cot_rows[...], w_proj_c[...]).astype(BF16)
        flights.wait("w_merge")
        flights.wait("merged")

        own_rows = unpack(slices[...])

        def merge(c, carry):
            quarters = []
            for n in range(4):
                lanes = pl.ds(pl.multiple_of(n * 512 + c * 256, 256), 256)
                quarters.append(mm(own_rows, w_merge[:, lanes]).reshape(LATS, CELL, 256))
            part[:, :, pl.ds(pl.multiple_of(c * 256, 256), 256)] = fold(quarters).astype(BF16)
            return carry

        def half(first, number):
            lanes = pl.ds(first * 256, 256)
            return spread(
                where,
                lambda peer: part.at[peer, :, lanes],
                lambda lat: part_got.at[lat, :, lanes],
                lat_sems.at[number],
            )

        merge(0, 0)
        flights.start("part_0", half(0, 2))
        merge(1, 0)
        flights.start("part_1", half(1, 3))
        part_got[where.lat] = part[where.lat]
        slices_t[...] = own_rows.astype(F32).T.astype(BF16)
        flights.wait("part_0")
        flights.wait("part_1")
        coarse_ref[...] = unfold_one(sum_slots(part_got))
        packed[...] = fold_one(group_stats(coarse_ref[...], 0, 2048)[0]).astype(BF16)

        def gather_half(src, first, number):
            lanes = pl.ds(first * 256, 256)
            return spread(
                where,
                lambda peer: src.at[:, lanes],
                lambda lat: normed_got.at[lat, :, lanes],
                lat_sems.at[number],
            )

        def rows_half(first):
            parts = unfold(normed_got[:, :, first * 256 : first * 256 + 256].astype(F32))
            for n in range(4):
                lanes = slice(n * 512 + first * 256, n * 512 + first * 256 + 256)
                rows[:, lanes] = parts[n].reshape(LATS * CELL, 256).astype(BF16)
                yield lanes

        for first in range(2):
            flights.start(f"normed_{first}", gather_half(packed, first, (4, 14)[first]))
        normed_got[where.lat] = packed[...]
        flights.wait("w_qkv_c")
        sums = [jnp.zeros((LATS * CELL, 256), F32)] * 3
        for first in range(2):
            flights.wait(f"normed_{first}")
            for lanes in rows_half(first):
                for m in range(3):
                    sums[m] = sums[m] + mm(rows[:, lanes], w_qkv_c[m, lanes])
        for m in range(3):
            qkv[m] = sums[m].astype(BF16)
        real_c = key % CELL < 36

        def window_c(w, carry):
            own_rows = pl.ds(pl.multiple_of(w * WIN, WIN), WIN)
            heads = stack_heads(qkv[0, own_rows], masks)
            d_heads = stack_heads(d_mixed_c[own_rows], masks)
            scores = mm_nt(heads, qkv[1, own_rows]) * 0.125
            weights = softmax_rows(jnp.where(real_c, scores, -1e30))
            weights_bf = weights.astype(BF16)
            mixed_c[own_rows] = pick_heads(mm(weights_bf, qkv[2, own_rows]), masks).astype(BF16)
            d_scores = scores_back(weights, mm_nt(d_heads, qkv[2, own_rows]))
            d_qkv[own_rows, :256] = pick_heads(mm(d_scores, qkv[1, own_rows]), masks).astype(BF16)
            d_qkv[own_rows, 256:512] = mm_tn(d_scores, heads).astype(BF16)
            d_qkv[own_rows, 512:] = mm_tn(weights_bf, d_heads).astype(BF16)
            return carry

        lax.fori_loop(0, 4, window_c, 0, unroll=2)

        def back(c, carry):
            quarters = []
            for n in range(4):
                part_rows = pl.ds(pl.multiple_of(n * 512 + c * 256, 256), 256)
                d_rows = mm_nt(d_qkv[:, :256], w_qkv_c[0, part_rows])
                d_rows = d_rows + mm_nt(d_qkv[:, 256:512], w_qkv_c[1, part_rows])
                d_rows = d_rows + mm_nt(d_qkv[:, 512:], w_qkv_c[2, part_rows])
                quarters.append(d_rows.reshape(LATS, CELL, 256))
            part[:, :, pl.ds(pl.multiple_of(c * 256, 256), 256)] = fold(quarters).astype(BF16)
            return carry

        back(0, 0)
        flights.start("d_part_0", half(0, 5))
        back(1, 0)
        flights.start("d_part_1", half(1, 6))
        part_got[where.lat] = part[where.lat]
        rows_t[...] = rows[...].astype(F32).T.astype(BF16)
        mixed_t = mixed_c[...].astype(F32).T.astype(BF16)

        def shares(m, carry):
            grad = mm(mixed_t, cot_rows[:, pl.ds(pl.multiple_of(m * 256, 256), 256)]).astype(BF16)
            for c in range(2):
                share[c, m // 2, m % 2, :256] = grad[:, c * 128 : c * 128 + 128]
                own_rows = pl.ds(pl.multiple_of(m * 256 + c * 128, 128), 128)
                grad_qkv = mm(rows_t[own_rows], d_qkv[...]).astype(BF16)
                for n in range(6):
                    share[c, m // 2, m % 2, 256 + 128 * n : 384 + 128 * n] = grad_qkv[
                        :, 128 * n : 128 * n + 128
                    ]
            return carry

        lax.fori_loop(0, 8, shares, 0)
        flights.start(
            "core_a",
            [remote(share.at[1 - core], core_a, share_sems.at[0, 0], share_sems.at[1, 0], sibling)],
        )

        def add_pairs(got):
            def add(n, carry):
                got[n] = (share[core, n].astype(F32) + got[n].astype(F32)).astype(BF16)
                return carry

            lax.fori_loop(0, 4, add, 0)

        def z_copies(src, dst, sems):
            copies = []
            for a in range(1, 4):
                there = lax.rem(z + a, 4)
                copies.append(
                    remote(
                        src.at[there], dst.at[a], sems.at[0, a], sems.at[1, a],
                        where.lon_at(there, y, core),
                    )
                )
            return copies

        flights.wait("d_part_0")
        flights.wait("d_part_1")
        d_normed = unfold_one(sum_slots(part_got).astype(BF16).astype(F32))
        d_coarse = fold_one(group_pullback(coarse_ref[...], d_normed, 0, 2048))
        d_packed[...] = (cot[...].astype(F32) + d_coarse).astype(BF16)
        for first in range(2):
            flights.start(f"d_coarse_{first}", gather_half(d_packed, first, (7, 15)[first]))
        normed_got[where.lat] = d_packed[...]
        flights.wait("core_a")
        add_pairs(core_a)
        flights.start("z_a", z_copies(core_a, z_a, z_sems.at[0]))
        sums = [jnp.zeros((LATS * CELL, 512), F32)] * 2
        for first in range(2):
            flights.wait(f"d_coarse_{first}")
            for lanes in rows_half(first):
                for n in range(2):
                    sums[n] = sums[n] + mm_nt(rows[:, lanes], w_merge[n * 512 : n * 512 + 512, lanes])
        merged[...] = pack(*sums)
        flights.start(
            "d_slices",
            spread(where, lambda peer: merged.at[peer], lambda lat: slices.at[lat], lat_sems.at[8]),
        )
        slices[where.lat] = merged[where.lat]

        def merge_shares(m, carry):
            grad = mm(slices_t[...], rows[:, pl.ds(pl.multiple_of(m * 256, 256), 256)]).astype(BF16)
            for c in range(2):
                share[c, m // 2, m % 2] = grad[:, c * 128 : c * 128 + 128]
            return carry

        lax.fori_loop(0, 8, merge_shares, 0)
        flights.start(
            "core_b",
            [remote(share.at[1 - core], core_b, share_sems.at[0, 1], share_sems.at[1, 1], sibling)],
        )
        flights.wait("d_slices")

        d_gathered = group_pullback(
            blended[...].reshape(16, CELL, E),
            slices[...].astype(F32).reshape(16, CELL, E),
            0,
            16 * E,
        )
        flights.wait("cot_fine")
        blended[...] = mm(to_cells[...], grid_in[...]) + d_gathered.reshape(16 * CELL, E)
        d_bf = blended[...].astype(BF16)
        send_in[...] = mm(in_send[...], d_bf).astype(BF16)
        flights.start("halo3", halo_copies(where, -1, send_in, got_in2, halo_sems.at[2]))
        own = mm(in_own[...], d_bf)
        flights.wait("core_b")
        add_pairs(core_b)
        flights.wait("z_a")
        z_a[0] = core_a[z]
        line_a[...] = sum_slots(z_a).astype(BF16)
        flights.start("z_b", z_copies(core_b, z_b, z_sems.at[1]))
        flights.start(
            "y_a", [remote(line_a.at[1 - y], y_a, share_sems.at[0, 2], share_sems.at[1, 2], other_y)]
        )
        flights.wait("halo3")
        d_out = (own + mm(in_halo[...], got_in2[...])).astype(BF16)
        grad = mm_tn(mixed_f[...], d_out).astype(BF16)
        for c in range(2):
            fine_0[:, :, c] = grad[:, c * 256 : c * 256 + 256].reshape(2, 8, 32, 256)
        mixed_f[...] = mm_nt(d_out, w_proj_f[...]).astype(BF16)

        def window_b(g):
            lanes = slice(g * 256, g * 256 + 256)

            def step(w, carry):
                own_rows = pl.ds(pl.multiple_of(w * WIN, WIN), WIN)
                weights = probs[w * 2 + g]
                heads = stack_heads(q[own_rows, lanes], masks)
                d_heads = stack_heads(mixed_f[own_rows, lanes], masks)
                d_scores = scores_back(weights, mm_nt(d_heads, v[own_rows, lanes]))
                new_q = pick_heads(mm(d_scores, k[own_rows, lanes]), masks).astype(BF16)
                new_k = mm_tn(d_scores, heads).astype(BF16)
                v[own_rows, lanes] = mm_tn(weights.astype(BF16), d_heads).astype(BF16)
                q[own_rows, lanes] = new_q
                k[own_rows, lanes] = new_k
                return carry

            return step

        def to_core(name, fine, pair, sems):
            flights.start(
                name, [remote(fine.at[1 - core], pair, sems.at[0], sems.at[1], sibling)]
            )

        def add_core(fine, pair):
            pair[...] = (fine[core].astype(F32) + pair[...].astype(F32)).astype(BF16)

        def to_lat(name, pair, got, sems):
            flights.start(name, spread(where, lambda peer: pair.at[peer], lambda lat: got.at[lat], sems))
            got[where.lat] = pair[where.lat]

        def to_lon(name, piece, got, sems):
            here = z * 2 + y
            copies = []
            for n in range(1, 8):
                copies.append(remote(piece, got.at[here], sems.at[0, n], sems.at[1, n], around[n]))
            flights.start(name, copies)
            got[here] = piece[...]

        def to_all(name, src, dst_of, sems, pass_sems):
            copies = spread(where, lambda peer: src, dst_of, sems)
            for copy in copies:
                copy.start()

            def to_sibling(n):
                rows_of = dst_of(lax.rem(where.lat - n + LATS, LATS))
                return remote(rows_of, rows_of, pass_sems.at[0, n], pass_sems.at[1, n], sibling)

            passed = [to_sibling(n) for n in range(LATS)]
            passed[0].start()

            def finish():
                for n in range(1, LATS):
                    copies[n - 1].wait()
                    passed[n].start()
                for copy in passed:
                    copy.wait()

            return finish

        def shard(lat):
            return pl.ds(pl.multiple_of(core * 256 + lat * 32, 32), 32)

        def qkv_half(g):
            return lambda lat: grad_qkv_f.at[:, shard(lat), pl.ds(g * 256, 256)]

        lax.fori_loop(0, 8, window_b(0), 0, unroll=2)
        x_t = x[...].astype(F32).T.astype(BF16)
        for m, ref in enumerate((q, k, v)):
            fine_0[:, :, 2 + m] = mm(x_t, ref[:, :256]).astype(BF16).reshape(2, 8, 32, 256)
        to_core("core_0", fine_0, pair_0, core_sems.at[0])
        lax.fori_loop(0, 4, window_b(1), 0, unroll=2)
        flights.wait("core_0")
        add_core(fine_0, pair_0)
        to_lat("lat_0", pair_0, lat_0, lat_sems.at[9])
        lax.fori_loop(4, 8, window_b(1), 0, unroll=2)
        for m, ref in enumerate((q, k, v)):
            fine_1[:, :, m] = mm(x_t, ref[:, 256:]).astype(BF16).reshape(2, 8, 32, 256)
        to_core("core_1", fine_1, pair_1, core_sems.at[1])
        d_shifted = mm_nt(q[...], w_qkv_f[0]) + mm_nt(k[...], w_qkv_f[1])
        d_shifted = (d_shifted + mm_nt(v[...], w_qkv_f[2])).astype(BF16)
        send_out[...] = mm(out_send[...], d_shifted).astype(BF16)
        flights.start("halo4", halo_copies(where, 1, send_out, got_out2, halo_sems.at[3]))
        flights.wait("lat_0")
        piece_0[...] = sum_slots(lat_0).astype(BF16)
        to_lon("lon_0", piece_0, lon_0, lon_sems.at[0])
        flights.wait("core_1")
        add_core(fine_1, pair_1)
        to_lat("lat_1", pair_1, lat_1, lat_sems.at[10])
        own = mm(out_own[...], d_shifted)
        flights.wait("halo4")
        flights.wait("lon_0")
        piece_0[...] = sum_slots(lon_0).astype(BF16)
        grad_qkv_f[:, shard(where.lat), :256] = piece_0[2:]
        grad_proj_f[:, shard(where.lat)] = piece_0[:2]
        ends = [
            to_all("qkv_0", piece_0.at[pl.ds(2, 3)], qkv_half(0), lat_sems.at[11], pass_sems.at[0]),
            to_all(
                "proj", piece_0.at[pl.ds(0, 2)], lambda lat: grad_proj_f.at[:, shard(lat)],
                lat_sems.at[12], pass_sems.at[1],
            ),
        ]
        d_normed = (own + mm(out_halo[...], got_out2[...])).astype(BF16).astype(F32)
        grad = blended[...] + pullback(tg[...].astype(F32), d_normed)
        flights.wait("to_grid")
        grad_tokens[...] = mm(to_grid[...], grad.astype(BF16)).astype(BF16)
        flights.wait("lat_1")
        piece_1[...] = sum_slots(lat_1).astype(BF16)
        to_lon("lon_1", piece_1, lon_1, lon_sems.at[1])
        flights.wait("lon_1")
        piece_1[...] = sum_slots(lon_1).astype(BF16)
        grad_qkv_f[:, shard(where.lat), 256:] = piece_1[...]
        ends.append(to_all("qkv_1", piece_1, qkv_half(1), lat_sems.at[13], pass_sems.at[2]))
        flights.wait("z_b")
        z_b[0] = core_b[z]
        line_b[...] = sum_slots(z_b).astype(BF16)
        flights.start(
            "y_b", [remote(line_b.at[1 - y], y_b, share_sems.at[0, 3], share_sems.at[1, 3], other_y)]
        )
        flights.wait("y_a")
        grad_proj_c[...] = line_a[y, :256].astype(F32) + y_a[:256].astype(F32)
        for n in range(6):
            own_rows = slice(256 + 128 * n, 384 + 128 * n)
            grad_qkv_c[n // 2, :, (n % 2) * 128 : (n % 2) * 128 + 128] = line_a[y, own_rows].astype(
                F32
            ) + y_a[own_rows].astype(F32)
        flights.wait("y_b")
        grad_merge[...] = line_b[y].astype(F32) + y_b[...].astype(F32)
        for end in ends:
            end()

    body()


def dma(*shape):
    return pltpu.SemaphoreType.DMA(shape)


def bf(*shape):
    return pltpu.VMEM(shape, BF16)


def f32(*shape):
    return pltpu.VMEM(shape, F32)


def per_device(tokens, w_qkv_f, w_proj_f, w_merge, w_qkv_c, w_proj_c, cot_fine, cot_coarse):
    to_cells, in_send, in_own, in_halo, out_send, out_own, out_halo, to_grid = tables()
    flat = tokens.reshape(ROWS * COLS, E)
    cot_flat = cot_fine.reshape(ROWS * COLS, E)
    size = 16 * CELL
    wide = (LATS, 144, E)
    slim = (LATS, WIN, E)
    near = pl.BlockSpec(memory_space=pltpu.VMEM)
    far = pl.BlockSpec(memory_space=pl.ANY)
    shares = [bf(4, 2, 1024, 128)] * 2 + [bf(2, 1024, 128), bf(1024, 128)]
    grad_tokens, grad_qkv_f, grad_proj_f, grad_merge, grad_qkv_c, grad_proj_c = pl.pallas_call(
        whole,
        out_shape=[
            jax.ShapeDtypeStruct((ROWS * COLS, E), BF16),
            jax.ShapeDtypeStruct((3, E, E), BF16),
            jax.ShapeDtypeStruct((2, E, 256), BF16),
            jax.ShapeDtypeStruct((1024, 128), F32),
            jax.ShapeDtypeStruct((3, 128, 256), F32),
            jax.ShapeDtypeStruct((256, 128), F32),
        ],
        in_specs=[near] + [far] * 15,
        out_specs=[near] * 6,
        scratch_shapes=[
            *[bf(*t.shape) for t in (to_cells, in_send, in_own, in_halo)],
            *[bf(*t.shape) for t in (out_send, out_own, out_halo, to_grid, cot_flat)],
            *[bf(*t.shape) for t in (w_qkv_f, w_proj_f, w_merge, w_qkv_c, w_proj_c)],
            *[bf(size, E)] * 4, f32(16, 4 * WIN, WIN), bf(size, E), bf(size, E), f32(size, E),
            bf(*slim), bf(*slim),
            *[bf(224, E)] * 6,
            bf(144, E), bf(*wide), bf(*wide), f32(4, CELL, E), bf(144, E), bf(*wide), bf(320, 2048), bf(2048, 320),
            bf(320, 2048), bf(3, 320, 256), bf(320, 256), bf(320, 256), bf(320, 768),
            bf(144, E), bf(1024, 320),
            bf(2, 4, 2, 1024, 128), *shares, *shares,
            bf(2, 8, 5, 32, 256), *[bf(8, 5, 32, 256)] * 3, bf(5, 32, 256),
            bf(2, 8, 3, 32, 256), *[bf(8, 3, 32, 256)] * 3, bf(3, 32, 256),
            dma(14), dma(4, 2, 3), dma(16, 2, LATS), dma(2, 4), dma(2, 2, 4), dma(2, 2), dma(2, 2, 8),
            dma(3, 2, LATS),
        ],
        compiler_params=pltpu.CompilerParams(
            collective_id=1, has_side_effects=True, vmem_limit_bytes=VMEM_BYTES
        ),
    )(
        cot_coarse[0], flat, to_cells, in_send, in_own, in_halo, out_send, out_own, out_halo, to_grid, cot_flat,
        w_qkv_f, w_proj_f, w_merge, w_qkv_c, w_proj_c,
    )
    arrays = (grad_tokens, grad_qkv_f, grad_proj_f, grad_merge, grad_qkv_c, grad_proj_c)
    outs = [(ROWS * COLS, E), (3, E, E), (E, E), (1024, 128), (3, 128, 256), (256, 128)]
    steps = 4

    def cut(shape, dim):
        size = tuple(s // steps if d == dim else s for d, s in enumerate(shape))
        return pl.BlockSpec(size, lambda i: tuple(i if d == dim else 0 for d in range(len(shape))))

    dims = (0, 1, 0, 0, 1, 0)
    results = pl.pallas_call(
        finish,
        grid=(steps,),
        out_shape=[jax.ShapeDtypeStruct(s, F32 if n else BF16) for n, s in enumerate(outs)],
        in_specs=[cut(t.shape, 1 if n == 2 else d) for n, (t, d) in enumerate(zip(arrays, dims))],
        out_specs=[cut(s, d) for s, d in zip(outs, dims)],
    )(*arrays)
    return (results[0].reshape(tokens.shape), *results[1:])


def finish(tokens, qkv_f, proj_f, merge, qkv_c, proj_c, *outs):
    fine_scale, coarse_scale = 73728**-0.5, 4608**-0.5
    outs[0][...] = tokens[...]
    outs[1][...] = qkv_f[...].astype(F32) * fine_scale
    outs[2][:, :256] = proj_f[0].astype(F32) * fine_scale
    outs[2][:, 256:] = proj_f[1].astype(F32) * fine_scale
    for source, out in zip((merge, qkv_c, proj_c), outs[3:]):
        out[...] = source[...] * coarse_scale


def solution(mesh):
    return jax.shard_map(
        per_device,
        mesh=mesh,
        in_specs=(
            P(None, "lat", "lon", None),
            P(),
            P(),
            P("lat", None),
            P(None, None, "lat"),
            P("lat", None),
            P(None, "lat", "lon", None),
            P(None, "lat", "lon", None),
        ),
        out_specs=(
            P(None, "lat", "lon", None),
            P(),
            P(),
            P("lat", "lon"),
            P(None, "lon", "lat"),
            P("lat", "lon"),
        ),
        check_vma=False,
    )
```

```python
import jax
import jax.numpy as jnp
import numpy as np
from jax import lax
from jax.experimental import pallas as pl
from jax.experimental.pallas import tpu as pltpu
from jax.sharding import PartitionSpec as P

MESH = pl.DeviceIdType.MESH
F32 = jnp.float32
BF16 = jnp.bfloat16
EPS = 1e-05
LATS = 8
ROWS, COLS = 12, 48
WL, WC = 6, 12
CELL = 40
WIN = 80
E = 512
HALO = ((0, 128), (128, 64), (192, 32))
VMEM_BYTES = 63 * 1024 * 1024


def tables():
    win = np.zeros((ROWS, COLS), np.int64)
    cell = np.zeros((ROWS, COLS), np.int64)
    for i in range(ROWS):
        for j in range(COLS):
            win[i, j] = ((i // WL) * 4 + j // WC) * WIN + (i % WL) * WC + j % WC
            cell[i, j] = ((i % 4) * 4 + j % 4) * CELL + (i // 4) * 12 + j // 4
    size = 16 * CELL
    to_cells = np.zeros((size, ROWS * COLS), np.float32)
    in_send = np.zeros((224, size), np.float32)
    in_own = np.zeros((size, size), np.float32)
    in_halo = np.zeros((size, 224), np.float32)
    out_send = np.zeros((224, size), np.float32)
    out_own = np.zeros((size, size), np.float32)
    out_halo = np.zeros((size, 224), np.float32)
    for i in range(ROWS):
        for j in range(COLS):
            to_cells[cell[i, j], i * COLS + j] = 1
            r, c = i + 3, j + 6
            if r < ROWS and c < COLS:
                in_own[win[i, j], cell[r, c]] = 1
                out_own[cell[r, c], win[i, j]] = 1
            else:
                if c < COLS:
                    slot = (r - ROWS) * 42 + c - 6
                elif r < ROWS:
                    slot = 128 + (r - 3) * 6 + c - COLS
                else:
                    slot = 192 + (r - ROWS) * 6 + c - COLS
                in_send[slot, cell[r % ROWS, c % COLS]] = 1
                in_halo[win[i, j], slot] = 1
                out_send[slot, win[i, j]] = 1
                out_halo[cell[r % ROWS, c % COLS], slot] = 1
    return [
        jnp.asarray(t, BF16)
        for t in (to_cells, in_send, in_own, in_halo, out_send, out_own, out_halo, to_cells.T)
    ]


def mm(a, b):
    return jnp.dot(a, b, preferred_element_type=F32)


def mm_nt(a, b):
    return lax.dot_general(a, b, (((1,), (1,)), ((), ())), preferred_element_type=F32)


def mm_tn(a, b):
    return lax.dot_general(a, b, (((0,), (0,)), ((), ())), preferred_element_type=F32)


def normalize(x):
    centred = x - jnp.mean(x, axis=-1, keepdims=True)
    return centred * lax.rsqrt(jnp.mean(centred * centred, axis=-1, keepdims=True) + EPS)


def pullback(x, dy):
    centred = x - jnp.mean(x, axis=-1, keepdims=True)
    rate = lax.rsqrt(jnp.mean(centred * centred, axis=-1, keepdims=True) + EPS)
    y = centred * rate
    inner = jnp.mean(dy * y, axis=-1, keepdims=True)
    return rate * (dy - jnp.mean(dy, axis=-1, keepdims=True) - y * inner)


def total(x, axes):
    s = jnp.sum(x, axis=-1, keepdims=True)
    return jnp.sum(s, axis=axes, keepdims=True)


def group_stats(x, axis, count):
    mean = total(x, axis) * (1.0 / count)
    centred = x - mean
    rate = lax.rsqrt(total(centred * centred, axis) * (1.0 / count) + EPS)
    return centred * rate, rate


def group_pullback(x, dy, axis, count):
    y, rate = group_stats(x, axis, count)
    inner = total(dy * y, axis) * (1.0 / count)
    return rate * (dy - total(dy, axis) * (1.0 / count) - y * inner)


def head_masks():
    lane = lax.broadcasted_iota(jnp.int32, (1, 256), 1) // 64
    return [jnp.where(lane == h, 1.0, 0.0) for h in range(4)]


def stack_heads(x, masks):
    return jnp.concatenate([x * m.astype(BF16) for m in masks], axis=0)


def pick_heads(x, masks):
    out = x[:WIN] * masks[0]
    for h in range(1, 4):
        out = out + x[h * WIN : (h + 1) * WIN] * masks[h]
    return out


def softmax_rows(scores):
    weights = jnp.exp(scores - jnp.max(scores, axis=-1, keepdims=True))
    return weights / jnp.sum(weights, axis=-1, keepdims=True)


def scores_back(probs, d_probs):
    d_probs = d_probs.astype(BF16).astype(F32)
    inner = jnp.sum(d_probs * probs, axis=-1, keepdims=True)
    return (probs * (d_probs - inner) * 0.125).astype(BF16)


def greet(devices):
    barrier = pltpu.get_barrier_semaphore()
    for device in devices:
        pl.semaphore_signal(barrier, inc=1, device_id=device, device_id_type=MESH)
    pl.semaphore_wait(barrier, len(devices))


def remote(src, dst, send, recv, device):
    return pltpu.make_async_remote_copy(
        src_ref=src, dst_ref=dst, send_sem=send, recv_sem=recv, device_id=device, device_id_type=MESH
    )


class Place:
    def __init__(self):
        self.lat = lax.axis_index("lat")
        self.lon = lax.axis_index("lon")

    def lat_peer(self, k):
        return lax.rem(self.lat + k, LATS)

    def at_lat(self, k):
        return (self.lat_peer(k), self.lon)

    def halo(self, step):
        up = lax.rem(self.lat + step + LATS, LATS)
        side = lax.rem(self.lon + step + 16, 16)
        return ((up, self.lon), (self.lat, side), (up, side))

    def lon_at(self, z, y, core):
        return (self.lat, z * 4 + y * 2 + core)


def start_halo(where, step, src, dst, sems):
    copies = []
    for n, device in enumerate(where.halo(step)):
        first, count = HALO[n]
        copies.append(
            remote(
                src.at[pl.ds(first, count)],
                dst.at[pl.ds(first, count)],
                sems.at[0, n],
                sems.at[1, n],
                device,
            )
        )
        copies[-1].start()
    return copies


def wait_all(copies):
    for copy in copies:
        copy.wait()


def start_spread(where, src_of, dst, sems):
    copies = []
    for k in range(1, LATS):
        copies.append(
            remote(
                src_of(where.lat_peer(k)),
                dst.at[where.lat],
                sems.at[0, k],
                sems.at[1, k],
                where.at_lat(k),
            )
        )
        copies[-1].start()
    return copies


def finish_spread(where, src_of, dst, sems):
    for k in range(1, LATS):
        source = where.lat_peer(LATS - k)
        remote(src_of(source), dst.at[source], sems.at[0, k], sems.at[1, k], where.at_lat(k)).wait()


def unpack(x):
    x = x.astype(F32)
    width = x.shape[-1]
    halves = [x[:, :CELL].reshape(LATS * CELL, width), x[:, CELL:].reshape(LATS * CELL, width)]
    return jnp.concatenate(halves, axis=1).astype(BF16)


def pack(top, bottom):
    width = top.shape[-1]
    halves = [top.reshape(LATS, CELL, width), bottom.reshape(LATS, CELL, width)]
    return jnp.concatenate(halves, axis=1).astype(BF16)


def swap_halves(x):
    low = lax.broadcasted_iota(jnp.int32, x.shape, 0) % 8 < 4
    count = x.shape[0]
    return jnp.where(low, pltpu.roll(x, count - 4, 0), pltpu.roll(x, 4, 0))


def fold(parts):
    n, _, width = parts[0].shape
    low = lax.broadcasted_iota(jnp.int32, (n * 8, width), 0) % 8 < 4
    pieces = [p[:, :32] for p in parts]
    for c in (0, 2):
        first = parts[c][:, 32:].reshape(n * 8, width)
        second = swap_halves(parts[c + 1][:, 32:].reshape(n * 8, width))
        pieces.append(jnp.where(low, first, second).reshape(n, 8, width))
    return jnp.concatenate(pieces, axis=1)


def unfold(x):
    n, _, width = x.shape
    low = lax.broadcasted_iota(jnp.int32, (n * 8, width), 0) % 8 < 4
    parts = []
    for c in range(4):
        tail = x[:, 128 + c // 2 * 8 : 136 + c // 2 * 8].reshape(n * 8, width)
        if c % 2:
            tail = swap_halves(tail)
        tail = jnp.where(low, tail, 0.0).reshape(n, 8, width)
        parts.append(jnp.concatenate([x[:, c * 32 : c * 32 + 32], tail], axis=1))
    return parts


def unfold_rows(x):
    parts = [p.reshape(LATS * CELL, 512) for p in unfold(x.astype(F32))]
    return jnp.concatenate(parts, axis=1).astype(BF16)


def unfold_one(x):
    return jnp.concatenate(unfold(x[None]), axis=0)


def fold_one(x):
    return fold([x[c : c + 1] for c in range(4)])[0]


class Flights:
    def __init__(self):
        self.open = {}

    def start(self, name, copies):
        self.open[name] = copies
        for copy in copies:
            copy.start()

    def wait(self, name):
        for copy in self.open.pop(name):
            copy.wait()


def spread(where, src_of, dst_of, sems):
    return [
        remote(
            src_of(where.lat_peer(k)), dst_of(where.lat), sems.at[0, k], sems.at[1, k], where.at_lat(k)
        )
        for k in range(1, LATS)
    ]


def halo_copies(where, step, src, dst, sems):
    copies = []
    for n, device in enumerate(where.halo(step)):
        rows = pl.ds(*HALO[n])
        copies.append(remote(src.at[rows], dst.at[rows], sems.at[0, n], sems.at[1, n], device))
    return copies


def sum_slots(ref):
    value = ref[0].astype(F32)
    for n in range(1, ref.shape[0]):
        value = value + ref[n].astype(F32)
    return value


def whole(
    cot_in, tokens_h, to_cells_h, in_send_h, in_own_h, in_halo_h,
    out_send_h, out_own_h, out_halo_h, to_grid_h, cot_fine_h,
    w_qkv_f_h, w_proj_f_h, w_merge_h, w_qkv_c_h, w_proj_c_h,
    grad_tokens, grad_qkv_f, grad_proj_f, grad_merge, grad_qkv_c, grad_proj_c,
    to_cells, in_send, in_own, in_halo, out_send, out_own, out_halo, to_grid, grid_in, w_qkv_f, w_proj_f, w_merge, w_qkv_c, w_proj_c,
    x, q, k, v, probs, mixed_f, tg, blended, merged, slices,
    send_in, got_in, send_out, got_out, got_in2, got_out2,
    cot, part, part_got, coarse_ref, packed, normed_got, rows, rows_t, cot_rows, qkv, d_mixed_c, mixed_c, d_qkv,
    d_packed, slices_t,
    share, core_a, z_a, line_a, y_a,
    core_b, z_b, line_b, y_b,
    fine_0, pair_0, lat_0, lon_0, piece_0, half_0, fine_1, pair_1, lat_1, lon_1, piece_1, half_1,
    load_sems, halo_sems, lat_sems, share_sems, z_sems, core_sems, lon_sems, pass_sems,
):
    where = Place()
    z, y, core = where.lon // 4, lax.rem(where.lon // 2, 2), lax.rem(where.lon, 2)
    chips = [(a, b) for a in range(4) for b in range(2)]
    around = [where.lon_at(lax.rem(z + a, 4), lax.rem(y + b, 2), core) for a, b in chips]
    sibling = where.lon_at(z, y, 1 - core)
    other_y = where.lon_at(z, 1 - y, core)
    flights = Flights()

    def body():
        barrier = pltpu.get_barrier_semaphore()
        friends = [where.at_lat(n) for n in range(1, LATS)] + around[1:] + [sibling]
        friends += list(where.halo(-1)[1:]) + list(where.halo(1)[1:])
        for device in friends:
            pl.semaphore_signal(barrier, inc=1, device_id=device, device_id_type=MESH)
        flights.start("tokens", [pltpu.make_async_copy(tokens_h, grid_in, load_sems.at[13])])
        loads = (
            ("to_cells", to_cells_h, to_cells), ("in_send", in_send_h, in_send),
            ("in_own", in_own_h, in_own), ("in_halo", in_halo_h, in_halo),
            ("w_qkv_f", w_qkv_f_h, w_qkv_f), ("w_proj_f", w_proj_f_h, w_proj_f),
            ("out_send", out_send_h, out_send), ("out_own", out_own_h, out_own),
            ("out_halo", out_halo_h, out_halo), ("w_merge", w_merge_h, w_merge),
            ("w_proj_c", w_proj_c_h, w_proj_c), ("w_qkv_c", w_qkv_c_h, w_qkv_c),
            ("to_grid", to_grid_h, to_grid),
        )
        for n, (name, far, near) in enumerate(loads):
            flights.start(name, [pltpu.make_async_copy(far, near, load_sems.at[n])])

        target = lax.broadcasted_iota(jnp.int32, (CELL, 12), 0)
        column = lax.broadcasted_iota(jnp.int32, (CELL, 12), 1)
        cot_wide = jnp.zeros((CELL, 2048), F32)
        for n in range(3):
            place = jnp.where(target == column + 12 * n, 1.0, 0.0).astype(BF16)
            cot_wide = cot_wide + mm(place, cot_in[n])
        cot[...] = fold([cot_wide[None, :, c * 512 : c * 512 + 512] for c in range(4)])[0].astype(BF16)
        flights.wait("tokens")
        flights.wait("to_cells")
        cells = mm(to_cells[...], grid_in[...])
        tg[...] = cells.astype(BF16)
        flights.start("cot_fine", [pltpu.make_async_copy(cot_fine_h, grid_in, load_sems.at[13])])
        normed = normalize(cells).astype(BF16)
        flights.wait("in_send")
        send_in[...] = mm(in_send[...], normed).astype(BF16)
        pl.semaphore_wait(barrier, len(friends))
        flights.start("halo1", halo_copies(where, -1, send_in, got_in, halo_sems.at[0]))
        flights.start("cots", spread(where, lambda peer: cot, lambda lat: normed_got.at[lat], lat_sems.at[0]))
        normed_got[where.lat] = cot[...]
        flights.wait("in_own")
        flights.wait("in_halo")
        own = mm(in_own[...], normed)
        flights.wait("halo1")
        x[...] = (own + mm(in_halo[...], got_in[...])).astype(BF16)
        flights.wait("w_qkv_f")
        for m, ref in enumerate((q, k, v)):
            ref[...] = mm(x[...], w_qkv_f[m]).astype(BF16)
        masks = head_masks()
        key = lax.broadcasted_iota(jnp.int32, (4 * WIN, WIN), 1)
        query = lax.broadcasted_iota(jnp.int32, (4 * WIN, WIN), 0) % WIN
        real = key < 72
        same = (key < 36) == (query < 36)
        last = where.lat == LATS - 1

        def window(w, carry):
            own_rows = pl.ds(pl.multiple_of(w * WIN, WIN), WIN)
            bound = jnp.logical_and(last, w >= 4)
            for g in range(2):
                lanes = slice(g * 256, g * 256 + 256)
                scores = mm_nt(stack_heads(q[own_rows, lanes], masks), k[own_rows, lanes]) * 0.125
                allowed = jnp.logical_and(real, jnp.logical_or(same, jnp.logical_not(bound)))
                weights = softmax_rows(jnp.where(allowed, scores, -1e30))
                probs[w * 2 + g] = weights
                mixed_f[own_rows, lanes] = pick_heads(
                    mm(weights.astype(BF16), v[own_rows, lanes]), masks
                ).astype(BF16)
            return carry

        lax.fori_loop(0, 8, window, 0, unroll=2)
        flights.wait("w_proj_f")
        out = mm(mixed_f[...], w_proj_f[...]).astype(BF16)
        flights.wait("out_send")
        send_out[...] = mm(out_send[...], out).astype(BF16)
        flights.start("halo2", halo_copies(where, 1, send_out, got_out, halo_sems.at[1]))
        flights.wait("out_own")
        flights.wait("out_halo")
        own = tg[...].astype(F32) + mm(out_own[...], out)
        flights.wait("halo2")
        blended[...] = own + mm(out_halo[...], got_out[...])
        merged[...] = (
            group_stats(blended[...].reshape(16, CELL, E), 0, 16 * E)[0]
            .reshape(LATS, WIN, E)
            .astype(BF16)
        )
        flights.start("merged", spread(where, lambda peer: merged.at[peer], lambda lat: slices.at[lat], lat_sems.at[1]))
        slices[where.lat] = merged[where.lat]
        flights.wait("cots")
        cot_rows[...] = unfold_rows(normed_got[...])
        flights.wait("w_proj_c")
        d_mixed_c[...] = mm_nt(cot_rows[...], w_proj_c[...]).astype(BF16)
        flights.wait("w_merge")
        flights.wait("merged")

        own_rows = unpack(slices[...])

        def merge(c, carry):
            quarters = []
            for n in range(4):
                lanes = pl.ds(pl.multiple_of(n * 512 + c * 256, 256), 256)
                quarters.append(mm(own_rows, w_merge[:, lanes]).reshape(LATS, CELL, 256))
            part[:, :, pl.ds(pl.multiple_of(c * 256, 256), 256)] = fold(quarters).astype(BF16)
            return carry

        def half(first, number):
            lanes = pl.ds(first * 256, 256)
            return spread(
                where,
                lambda peer: part.at[peer, :, lanes],
                lambda lat: part_got.at[lat, :, lanes],
                lat_sems.at[number],
            )

        merge(0, 0)
        flights.start("part_0", half(0, 2))
        merge(1, 0)
        flights.start("part_1", half(1, 3))
        part_got[where.lat] = part[where.lat]
        slices_t[...] = own_rows.astype(F32).T.astype(BF16)
        flights.wait("part_0")
        flights.wait("part_1")
        coarse_ref[...] = unfold_one(sum_slots(part_got))
        packed[...] = fold_one(group_stats(coarse_ref[...], 0, 2048)[0]).astype(BF16)

        def gather_half(src, first, number):
            lanes = pl.ds(first * 256, 256)
            return spread(
                where,
                lambda peer: src.at[:, lanes],
                lambda lat: normed_got.at[lat, :, lanes],
                lat_sems.at[number],
            )

        def rows_half(first):
            parts = unfold(normed_got[:, :, first * 256 : first * 256 + 256].astype(F32))
            for n in range(4):
                lanes = slice(n * 512 + first * 256, n * 512 + first * 256 + 256)
                rows[:, lanes] = parts[n].reshape(LATS * CELL, 256).astype(BF16)
                yield lanes

        for first in range(2):
            flights.start(f"normed_{first}", gather_half(packed, first, (4, 14)[first]))
        normed_got[where.lat] = packed[...]
        flights.wait("w_qkv_c")
        sums = [jnp.zeros((LATS * CELL, 256), F32)] * 3
        for first in range(2):
            flights.wait(f"normed_{first}")
            for lanes in rows_half(first):
                for m in range(3):
                    sums[m] = sums[m] + mm(rows[:, lanes], w_qkv_c[m, lanes])
        for m in range(3):
            qkv[m] = sums[m].astype(BF16)
        real_c = key % CELL < 36

        def window_c(w, carry):
            own_rows = pl.ds(pl.multiple_of(w * WIN, WIN), WIN)
            heads = stack_heads(qkv[0, own_rows], masks)
            d_heads = stack_heads(d_mixed_c[own_rows], masks)
            scores = mm_nt(heads, qkv[1, own_rows]) * 0.125
            weights = softmax_rows(jnp.where(real_c, scores, -1e30))
            weights_bf = weights.astype(BF16)
            mixed_c[own_rows] = pick_heads(mm(weights_bf, qkv[2, own_rows]), masks).astype(BF16)
            d_scores = scores_back(weights, mm_nt(d_heads, qkv[2, own_rows]))
            d_qkv[own_rows, :256] = pick_heads(mm(d_scores, qkv[1, own_rows]), masks).astype(BF16)
            d_qkv[own_rows, 256:512] = mm_tn(d_scores, heads).astype(BF16)
            d_qkv[own_rows, 512:] = mm_tn(weights_bf, d_heads).astype(BF16)
            return carry

        lax.fori_loop(0, 4, window_c, 0, unroll=2)

        def back(c, carry):
            quarters = []
            for n in range(4):
                part_rows = pl.ds(pl.multiple_of(n * 512 + c * 256, 256), 256)
                d_rows = mm_nt(d_qkv[:, :256], w_qkv_c[0, part_rows])
                d_rows = d_rows + mm_nt(d_qkv[:, 256:512], w_qkv_c[1, part_rows])
                d_rows = d_rows + mm_nt(d_qkv[:, 512:], w_qkv_c[2, part_rows])
                quarters.append(d_rows.reshape(LATS, CELL, 256))
            part[:, :, pl.ds(pl.multiple_of(c * 256, 256), 256)] = fold(quarters).astype(BF16)
            return carry

        back(0, 0)
        flights.start("d_part_0", half(0, 5))
        back(1, 0)
        flights.start("d_part_1", half(1, 6))
        part_got[where.lat] = part[where.lat]
        rows_t[...] = rows[...].astype(F32).T.astype(BF16)
        mixed_t = mixed_c[...].astype(F32).T.astype(BF16)

        def shares(m, carry):
            grad = mm(mixed_t, cot_rows[:, pl.ds(pl.multiple_of(m * 256, 256), 256)]).astype(BF16)
            for c in range(2):
                share[c, m // 2, m % 2, :256] = grad[:, c * 128 : c * 128 + 128]
                own_rows = pl.ds(pl.multiple_of(m * 256 + c * 128, 128), 128)
                grad_qkv = mm(rows_t[own_rows], d_qkv[...]).astype(BF16)
                for n in range(6):
                    share[c, m // 2, m % 2, 256 + 128 * n : 384 + 128 * n] = grad_qkv[
                        :, 128 * n : 128 * n + 128
                    ]
            return carry

        lax.fori_loop(0, 8, shares, 0)
        flights.start(
            "core_a",
            [remote(share.at[1 - core], core_a, share_sems.at[0, 0], share_sems.at[1, 0], sibling)],
        )

        def add_pairs(got):
            def add(n, carry):
                got[n] = (share[core, n].astype(F32) + got[n].astype(F32)).astype(BF16)
                return carry

            lax.fori_loop(0, 4, add, 0)

        def z_copies(src, dst, sems):
            copies = []
            for a in range(1, 4):
                there = lax.rem(z + a, 4)
                copies.append(
                    remote(
                        src.at[there], dst.at[a], sems.at[0, a], sems.at[1, a],
                        where.lon_at(there, y, core),
                    )
                )
            return copies

        flights.wait("d_part_0")
        flights.wait("d_part_1")
        d_normed = unfold_one(sum_slots(part_got).astype(BF16).astype(F32))
        d_coarse = fold_one(group_pullback(coarse_ref[...], d_normed, 0, 2048))
        d_packed[...] = (cot[...].astype(F32) + d_coarse).astype(BF16)
        for first in range(2):
            flights.start(f"d_coarse_{first}", gather_half(d_packed, first, (7, 15)[first]))
        normed_got[where.lat] = d_packed[...]
        flights.wait("core_a")
        add_pairs(core_a)
        flights.start("z_a", z_copies(core_a, z_a, z_sems.at[0]))
        sums = [jnp.zeros((LATS * CELL, 512), F32)] * 2
        for first in range(2):
            flights.wait(f"d_coarse_{first}")
            for lanes in rows_half(first):
                for n in range(2):
                    sums[n] = sums[n] + mm_nt(rows[:, lanes], w_merge[n * 512 : n * 512 + 512, lanes])
        merged[...] = pack(*sums)
        flights.start(
            "d_slices",
            spread(where, lambda peer: merged.at[peer], lambda lat: slices.at[lat], lat_sems.at[8]),
        )
        slices[where.lat] = merged[where.lat]

        def merge_shares(m, carry):
            grad = mm(slices_t[...], rows[:, pl.ds(pl.multiple_of(m * 256, 256), 256)]).astype(BF16)
            for c in range(2):
                share[c, m // 2, m % 2] = grad[:, c * 128 : c * 128 + 128]
            return carry

        lax.fori_loop(0, 8, merge_shares, 0)
        flights.start(
            "core_b",
            [remote(share.at[1 - core], core_b, share_sems.at[0, 1], share_sems.at[1, 1], sibling)],
        )
        flights.wait("d_slices")

        d_gathered = group_pullback(
            blended[...].reshape(16, CELL, E),
            slices[...].astype(F32).reshape(16, CELL, E),
            0,
            16 * E,
        )
        flights.wait("cot_fine")
        blended[...] = mm(to_cells[...], grid_in[...]) + d_gathered.reshape(16 * CELL, E)
        d_bf = blended[...].astype(BF16)
        send_in[...] = mm(in_send[...], d_bf).astype(BF16)
        flights.start("halo3", halo_copies(where, -1, send_in, got_in2, halo_sems.at[2]))
        own = mm(in_own[...], d_bf)
        flights.wait("core_b")
        add_pairs(core_b)
        flights.wait("z_a")
        z_a[0] = core_a[z]
        line_a[...] = sum_slots(z_a).astype(BF16)
        flights.start("z_b", z_copies(core_b, z_b, z_sems.at[1]))
        flights.start(
            "y_a", [remote(line_a.at[1 - y], y_a, share_sems.at[0, 2], share_sems.at[1, 2], other_y)]
        )
        flights.wait("halo3")
        d_out = (own + mm(in_halo[...], got_in2[...])).astype(BF16)
        grad = mm_tn(mixed_f[...], d_out).astype(BF16)
        for c in range(2):
            fine_0[:, :, c] = grad[:, c * 256 : c * 256 + 256].reshape(2, 8, 32, 256)
        mixed_f[...] = mm_nt(d_out, w_proj_f[...]).astype(BF16)

        def window_b(g):
            lanes = slice(g * 256, g * 256 + 256)

            def step(w, carry):
                own_rows = pl.ds(pl.multiple_of(w * WIN, WIN), WIN)
                weights = probs[w * 2 + g]
                heads = stack_heads(q[own_rows, lanes], masks)
                d_heads = stack_heads(mixed_f[own_rows, lanes], masks)
                d_scores = scores_back(weights, mm_nt(d_heads, v[own_rows, lanes]))
                new_q = pick_heads(mm(d_scores, k[own_rows, lanes]), masks).astype(BF16)
                new_k = mm_tn(d_scores, heads).astype(BF16)
                v[own_rows, lanes] = mm_tn(weights.astype(BF16), d_heads).astype(BF16)
                q[own_rows, lanes] = new_q
                k[own_rows, lanes] = new_k
                return carry

            return step

        def to_core(name, fine, pair, sems):
            flights.start(
                name, [remote(fine.at[1 - core], pair, sems.at[0], sems.at[1], sibling)]
            )

        def add_core(fine, pair):
            pair[...] = (fine[core].astype(F32) + pair[...].astype(F32)).astype(BF16)

        def to_lat(name, pair, got, sems):
            flights.start(name, spread(where, lambda peer: pair.at[peer], lambda lat: got.at[lat], sems))
            got[where.lat] = pair[where.lat]

        def to_y(name, piece, half, sems):
            flights.start(name, [remote(piece, half, sems.at[0], sems.at[1], other_y)])

        def to_z(name, piece, half, got, sems):
            half[...] = (piece[...].astype(F32) + half[...].astype(F32)).astype(BF16)
            copies = []
            for n in range(1, 4):
                there = where.lon_at(lax.rem(z + n, 4), y, core)
                copies.append(remote(half, got.at[z], sems.at[0, n], sems.at[1, n], there))
            flights.start(name, copies)
            got[z] = half[...]

        def to_all(name, src, dst_of, sems, pass_sems):
            copies = spread(where, lambda peer: src, dst_of, sems)
            for copy in copies:
                copy.start()

            def to_sibling(n):
                rows_of = dst_of(lax.rem(where.lat - n + LATS, LATS))
                return remote(rows_of, rows_of, pass_sems.at[0, n], pass_sems.at[1, n], sibling)

            passed = [to_sibling(n) for n in range(LATS)]
            passed[0].start()

            def finish():
                for n in range(1, LATS):
                    copies[n - 1].wait()
                    passed[n].start()
                for copy in passed:
                    copy.wait()

            return finish

        def shard(lat):
            return pl.ds(pl.multiple_of(core * 256 + lat * 32, 32), 32)

        def qkv_half(g):
            return lambda lat: grad_qkv_f.at[:, shard(lat), pl.ds(g * 256, 256)]

        lax.fori_loop(0, 8, window_b(0), 0, unroll=2)
        x_t = x[...].astype(F32).T.astype(BF16)
        for m, ref in enumerate((q, k, v)):
            fine_0[:, :, 2 + m] = mm(x_t, ref[:, :256]).astype(BF16).reshape(2, 8, 32, 256)
        to_core("core_0", fine_0, pair_0, core_sems.at[0])
        lax.fori_loop(0, 4, window_b(1), 0, unroll=2)
        flights.wait("core_0")
        add_core(fine_0, pair_0)
        to_lat("lat_0", pair_0, lat_0, lat_sems.at[9])
        lax.fori_loop(4, 8, window_b(1), 0, unroll=2)
        for m, ref in enumerate((q, k, v)):
            fine_1[:, :, m] = mm(x_t, ref[:, 256:]).astype(BF16).reshape(2, 8, 32, 256)
        to_core("core_1", fine_1, pair_1, core_sems.at[1])
        d_shifted = mm_nt(q[...], w_qkv_f[0]) + mm_nt(k[...], w_qkv_f[1])
        d_shifted = (d_shifted + mm_nt(v[...], w_qkv_f[2])).astype(BF16)
        send_out[...] = mm(out_send[...], d_shifted).astype(BF16)
        flights.start("halo4", halo_copies(where, 1, send_out, got_out2, halo_sems.at[3]))
        flights.wait("core_1")
        add_core(fine_1, pair_1)
        to_lat("lat_1", pair_1, lat_1, lat_sems.at[10])
        flights.wait("lat_0")
        piece_0[...] = sum_slots(lat_0).astype(BF16)
        to_y("y_0", piece_0, half_0, core_sems.at[2])
        own = mm(out_own[...], d_shifted)
        flights.wait("y_0")
        to_z("lon_0", piece_0, half_0, lon_0, lon_sems.at[0])
        flights.wait("halo4")
        d_normed = (own + mm(out_halo[...], got_out2[...])).astype(BF16).astype(F32)
        grad = blended[...] + pullback(tg[...].astype(F32), d_normed)
        flights.wait("to_grid")
        grad_tokens[...] = mm(to_grid[...], grad.astype(BF16)).astype(BF16)
        flights.wait("lat_1")
        piece_1[...] = sum_slots(lat_1).astype(BF16)
        to_y("y_1", piece_1, half_1, core_sems.at[3])
        flights.wait("lon_0")
        piece_0[...] = sum_slots(lon_0).astype(BF16)
        grad_qkv_f[:, shard(where.lat), :256] = piece_0[2:]
        grad_proj_f[:, shard(where.lat)] = piece_0[:2]
        ends = [
            to_all("qkv_0", piece_0.at[pl.ds(2, 3)], qkv_half(0), lat_sems.at[11], pass_sems.at[0]),
            to_all(
                "proj", piece_0.at[pl.ds(0, 2)], lambda lat: grad_proj_f.at[:, shard(lat)],
                lat_sems.at[12], pass_sems.at[1],
            ),
        ]
        flights.wait("y_1")
        to_z("lon_1", piece_1, half_1, lon_1, lon_sems.at[1])
        flights.wait("z_b")
        z_b[0] = core_b[z]
        line_b[...] = sum_slots(z_b).astype(BF16)
        flights.start(
            "y_b", [remote(line_b.at[1 - y], y_b, share_sems.at[0, 3], share_sems.at[1, 3], other_y)]
        )
        flights.wait("lon_1")
        piece_1[...] = sum_slots(lon_1).astype(BF16)
        grad_qkv_f[:, shard(where.lat), 256:] = piece_1[...]
        ends.append(to_all("qkv_1", piece_1, qkv_half(1), lat_sems.at[13], pass_sems.at[2]))
        flights.wait("y_a")
        grad_proj_c[...] = line_a[y, :256].astype(F32) + y_a[:256].astype(F32)
        for n in range(6):
            own_rows = slice(256 + 128 * n, 384 + 128 * n)
            grad_qkv_c[n // 2, :, (n % 2) * 128 : (n % 2) * 128 + 128] = line_a[y, own_rows].astype(
                F32
            ) + y_a[own_rows].astype(F32)
        flights.wait("y_b")
        grad_merge[...] = line_b[y].astype(F32) + y_b[...].astype(F32)
        for end in ends:
            end()

    body()


def dma(*shape):
    return pltpu.SemaphoreType.DMA(shape)


def bf(*shape):
    return pltpu.VMEM(shape, BF16)


def f32(*shape):
    return pltpu.VMEM(shape, F32)


def per_device(tokens, w_qkv_f, w_proj_f, w_merge, w_qkv_c, w_proj_c, cot_fine, cot_coarse):
    to_cells, in_send, in_own, in_halo, out_send, out_own, out_halo, to_grid = tables()
    flat = tokens.reshape(ROWS * COLS, E)
    cot_flat = cot_fine.reshape(ROWS * COLS, E)
    size = 16 * CELL
    wide = (LATS, 144, E)
    slim = (LATS, WIN, E)
    near = pl.BlockSpec(memory_space=pltpu.VMEM)
    far = pl.BlockSpec(memory_space=pl.ANY)
    shares = [bf(4, 2, 1024, 128)] * 2 + [bf(2, 1024, 128), bf(1024, 128)]
    grad_tokens, grad_qkv_f, grad_proj_f, grad_merge, grad_qkv_c, grad_proj_c = pl.pallas_call(
        whole,
        out_shape=[
            jax.ShapeDtypeStruct((ROWS * COLS, E), BF16),
            jax.ShapeDtypeStruct((3, E, E), BF16),
            jax.ShapeDtypeStruct((2, E, 256), BF16),
            jax.ShapeDtypeStruct((1024, 128), F32),
            jax.ShapeDtypeStruct((3, 128, 256), F32),
            jax.ShapeDtypeStruct((256, 128), F32),
        ],
        in_specs=[near] + [far] * 15,
        out_specs=[near] * 6,
        scratch_shapes=[
            *[bf(*t.shape) for t in (to_cells, in_send, in_own, in_halo)],
            *[bf(*t.shape) for t in (out_send, out_own, out_halo, to_grid, cot_flat)],
            *[bf(*t.shape) for t in (w_qkv_f, w_proj_f, w_merge, w_qkv_c, w_proj_c)],
            *[bf(size, E)] * 4, f32(16, 4 * WIN, WIN), bf(size, E), bf(size, E), f32(size, E),
            bf(*slim), bf(*slim),
            *[bf(224, E)] * 6,
            bf(144, E), bf(*wide), bf(*wide), f32(4, CELL, E), bf(144, E), bf(*wide), bf(320, 2048), bf(2048, 320),
            bf(320, 2048), bf(3, 320, 256), bf(320, 256), bf(320, 256), bf(320, 768),
            bf(144, E), bf(1024, 320),
            bf(2, 4, 2, 1024, 128), *shares, *shares,
            bf(2, 8, 5, 32, 256), *[bf(8, 5, 32, 256)] * 2, bf(4, 5, 32, 256), *[bf(5, 32, 256)] * 2,
            bf(2, 8, 3, 32, 256), *[bf(8, 3, 32, 256)] * 2, bf(4, 3, 32, 256), *[bf(3, 32, 256)] * 2,
            dma(14), dma(4, 2, 3), dma(16, 2, LATS), dma(2, 4), dma(2, 2, 4), dma(4, 2), dma(2, 2, 4),
            dma(3, 2, LATS),
        ],
        compiler_params=pltpu.CompilerParams(
            collective_id=1, has_side_effects=True, vmem_limit_bytes=VMEM_BYTES
        ),
    )(
        cot_coarse[0], flat, to_cells, in_send, in_own, in_halo, out_send, out_own, out_halo, to_grid, cot_flat,
        w_qkv_f, w_proj_f, w_merge, w_qkv_c, w_proj_c,
    )
    arrays = (grad_tokens, grad_qkv_f, grad_proj_f, grad_merge, grad_qkv_c, grad_proj_c)
    outs = [(ROWS * COLS, E), (3, E, E), (E, E), (1024, 128), (3, 128, 256), (256, 128)]
    steps = 4

    def cut(shape, dim):
        size = tuple(s // steps if d == dim else s for d, s in enumerate(shape))
        return pl.BlockSpec(size, lambda i: tuple(i if d == dim else 0 for d in range(len(shape))))

    dims = (0, 1, 0, 0, 1, 0)
    results = pl.pallas_call(
        finish,
        grid=(steps,),
        out_shape=[jax.ShapeDtypeStruct(s, F32 if n else BF16) for n, s in enumerate(outs)],
        in_specs=[cut(t.shape, 1 if n == 2 else d) for n, (t, d) in enumerate(zip(arrays, dims))],
        out_specs=[cut(s, d) for s, d in zip(outs, dims)],
    )(*arrays)
    return (results[0].reshape(tokens.shape), *results[1:])


def finish(tokens, qkv_f, proj_f, merge, qkv_c, proj_c, *outs):
    fine_scale, coarse_scale = 73728**-0.5, 4608**-0.5
    outs[0][...] = tokens[...]
    outs[1][...] = qkv_f[...].astype(F32) * fine_scale
    outs[2][:, :256] = proj_f[0].astype(F32) * fine_scale
    outs[2][:, 256:] = proj_f[1].astype(F32) * fine_scale
    for source, out in zip((merge, qkv_c, proj_c), outs[3:]):
        out[...] = source[...] * coarse_scale


def solution(mesh):
    return jax.shard_map(
        per_device,
        mesh=mesh,
        in_specs=(
            P(None, "lat", "lon", None),
            P(),
            P(),
            P("lat", None),
            P(None, None, "lat"),
            P("lat", None),
            P(None, "lat", "lon", None),
            P(None, "lat", "lon", None),
        ),
        out_specs=(
            P(None, "lat", "lon", None),
            P(),
            P(),
            P("lat", "lon"),
            P(None, "lon", "lat"),
            P("lat", "lon"),
        ),
        check_vma=False,
    )
```

```python
import jax
import jax.numpy as jnp
import numpy as np
from jax import lax
from jax.experimental import pallas as pl
from jax.experimental.pallas import tpu as pltpu
from jax.sharding import PartitionSpec as P

MESH = pl.DeviceIdType.MESH
F32 = jnp.float32
BF16 = jnp.bfloat16
EPS = 1e-05
LATS = 8
ROWS, COLS = 12, 48
WL, WC = 6, 12
CELL = 40
WIN = 80
E = 512
HALO = ((0, 128), (128, 64), (192, 32))
VMEM_BYTES = 63 * 1024 * 1024


def tables():
    win = np.zeros((ROWS, COLS), np.int64)
    cell = np.zeros((ROWS, COLS), np.int64)
    for i in range(ROWS):
        for j in range(COLS):
            win[i, j] = ((i // WL) * 4 + j // WC) * WIN + (i % WL) * WC + j % WC
            cell[i, j] = ((i % 4) * 4 + j % 4) * CELL + (i // 4) * 12 + j // 4
    size = 16 * CELL
    to_cells = np.zeros((size, ROWS * COLS), np.float32)
    in_send = np.zeros((224, size), np.float32)
    in_own = np.zeros((size, size), np.float32)
    in_halo = np.zeros((size, 224), np.float32)
    out_send = np.zeros((224, size), np.float32)
    out_own = np.zeros((size, size), np.float32)
    out_halo = np.zeros((size, 224), np.float32)
    for i in range(ROWS):
        for j in range(COLS):
            to_cells[cell[i, j], i * COLS + j] = 1
            r, c = i + 3, j + 6
            if r < ROWS and c < COLS:
                in_own[win[i, j], cell[r, c]] = 1
                out_own[cell[r, c], win[i, j]] = 1
            else:
                if c < COLS:
                    slot = (r - ROWS) * 42 + c - 6
                elif r < ROWS:
                    slot = 128 + (r - 3) * 6 + c - COLS
                else:
                    slot = 192 + (r - ROWS) * 6 + c - COLS
                in_send[slot, cell[r % ROWS, c % COLS]] = 1
                in_halo[win[i, j], slot] = 1
                out_send[slot, win[i, j]] = 1
                out_halo[cell[r % ROWS, c % COLS], slot] = 1
    return [
        jnp.asarray(t, BF16)
        for t in (to_cells, in_send, in_own, in_halo, out_send, out_own, out_halo, to_cells.T)
    ]


def mm(a, b):
    return jnp.dot(a, b, preferred_element_type=F32)


def mm_nt(a, b):
    return lax.dot_general(a, b, (((1,), (1,)), ((), ())), preferred_element_type=F32)


def mm_tn(a, b):
    return lax.dot_general(a, b, (((0,), (0,)), ((), ())), preferred_element_type=F32)


def normalize(x):
    centred = x - jnp.mean(x, axis=-1, keepdims=True)
    return centred * lax.rsqrt(jnp.mean(centred * centred, axis=-1, keepdims=True) + EPS)


def pullback(x, dy):
    centred = x - jnp.mean(x, axis=-1, keepdims=True)
    rate = lax.rsqrt(jnp.mean(centred * centred, axis=-1, keepdims=True) + EPS)
    y = centred * rate
    inner = jnp.mean(dy * y, axis=-1, keepdims=True)
    return rate * (dy - jnp.mean(dy, axis=-1, keepdims=True) - y * inner)


def total(x, axes):
    s = jnp.sum(x, axis=-1, keepdims=True)
    return jnp.sum(s, axis=axes, keepdims=True)


def group_stats(x, axis, count):
    mean = total(x, axis) * (1.0 / count)
    centred = x - mean
    rate = lax.rsqrt(total(centred * centred, axis) * (1.0 / count) + EPS)
    return centred * rate, rate


def group_pullback(x, dy, axis, count):
    y, rate = group_stats(x, axis, count)
    inner = total(dy * y, axis) * (1.0 / count)
    return rate * (dy - total(dy, axis) * (1.0 / count) - y * inner)


def head_masks():
    lane = lax.broadcasted_iota(jnp.int32, (1, 256), 1) // 64
    return [jnp.where(lane == h, 1.0, 0.0) for h in range(4)]


def stack_heads(x, masks):
    return jnp.concatenate([x * m.astype(BF16) for m in masks], axis=0)


def pick_heads(x, masks):
    out = x[:WIN] * masks[0]
    for h in range(1, 4):
        out = out + x[h * WIN : (h + 1) * WIN] * masks[h]
    return out


def softmax_rows(scores):
    weights = jnp.exp(scores - jnp.max(scores, axis=-1, keepdims=True))
    return weights / jnp.sum(weights, axis=-1, keepdims=True)


def scores_back(probs, d_probs):
    d_probs = d_probs.astype(BF16).astype(F32)
    inner = jnp.sum(d_probs * probs, axis=-1, keepdims=True)
    return (probs * (d_probs - inner) * 0.125).astype(BF16)


def greet(devices):
    barrier = pltpu.get_barrier_semaphore()
    for device in devices:
        pl.semaphore_signal(barrier, inc=1, device_id=device, device_id_type=MESH)
    pl.semaphore_wait(barrier, len(devices))


def remote(src, dst, send, recv, device):
    return pltpu.make_async_remote_copy(
        src_ref=src, dst_ref=dst, send_sem=send, recv_sem=recv, device_id=device, device_id_type=MESH
    )


class Place:
    def __init__(self):
        self.lat = lax.axis_index("lat")
        self.lon = lax.axis_index("lon")

    def lat_peer(self, k):
        return lax.rem(self.lat + k, LATS)

    def at_lat(self, k):
        return (self.lat_peer(k), self.lon)

    def halo(self, step):
        up = lax.rem(self.lat + step + LATS, LATS)
        side = lax.rem(self.lon + step + 16, 16)
        return ((up, self.lon), (self.lat, side), (up, side))

    def lon_at(self, z, y, core):
        return (self.lat, z * 4 + y * 2 + core)


def start_halo(where, step, src, dst, sems):
    copies = []
    for n, device in enumerate(where.halo(step)):
        first, count = HALO[n]
        copies.append(
            remote(
                src.at[pl.ds(first, count)],
                dst.at[pl.ds(first, count)],
                sems.at[0, n],
                sems.at[1, n],
                device,
            )
        )
        copies[-1].start()
    return copies


def wait_all(copies):
    for copy in copies:
        copy.wait()


def start_spread(where, src_of, dst, sems):
    copies = []
    for k in range(1, LATS):
        copies.append(
            remote(
                src_of(where.lat_peer(k)),
                dst.at[where.lat],
                sems.at[0, k],
                sems.at[1, k],
                where.at_lat(k),
            )
        )
        copies[-1].start()
    return copies


def finish_spread(where, src_of, dst, sems):
    for k in range(1, LATS):
        source = where.lat_peer(LATS - k)
        remote(src_of(source), dst.at[source], sems.at[0, k], sems.at[1, k], where.at_lat(k)).wait()


def unpack(x):
    x = x.astype(F32)
    width = x.shape[-1]
    halves = [x[:, :CELL].reshape(LATS * CELL, width), x[:, CELL:].reshape(LATS * CELL, width)]
    return jnp.concatenate(halves, axis=1).astype(BF16)


def pack(top, bottom):
    width = top.shape[-1]
    halves = [top.reshape(LATS, CELL, width), bottom.reshape(LATS, CELL, width)]
    return jnp.concatenate(halves, axis=1).astype(BF16)


def swap_halves(x):
    low = lax.broadcasted_iota(jnp.int32, x.shape, 0) % 8 < 4
    count = x.shape[0]
    return jnp.where(low, pltpu.roll(x, count - 4, 0), pltpu.roll(x, 4, 0))


def fold(parts):
    n, _, width = parts[0].shape
    low = lax.broadcasted_iota(jnp.int32, (n * 8, width), 0) % 8 < 4
    pieces = [p[:, :32] for p in parts]
    for c in (0, 2):
        first = parts[c][:, 32:].reshape(n * 8, width)
        second = swap_halves(parts[c + 1][:, 32:].reshape(n * 8, width))
        pieces.append(jnp.where(low, first, second).reshape(n, 8, width))
    return jnp.concatenate(pieces, axis=1)


def unfold(x):
    n, _, width = x.shape
    low = lax.broadcasted_iota(jnp.int32, (n * 8, width), 0) % 8 < 4
    parts = []
    for c in range(4):
        tail = x[:, 128 + c // 2 * 8 : 136 + c // 2 * 8].reshape(n * 8, width)
        if c % 2:
            tail = swap_halves(tail)
        tail = jnp.where(low, tail, 0.0).reshape(n, 8, width)
        parts.append(jnp.concatenate([x[:, c * 32 : c * 32 + 32], tail], axis=1))
    return parts


def unfold_rows(x):
    parts = [p.reshape(LATS * CELL, 512) for p in unfold(x.astype(F32))]
    return jnp.concatenate(parts, axis=1).astype(BF16)


def unfold_one(x):
    return jnp.concatenate(unfold(x[None]), axis=0)


def fold_one(x):
    return fold([x[c : c + 1] for c in range(4)])[0]


class Flights:
    def __init__(self):
        self.open = {}

    def start(self, name, copies):
        self.open[name] = copies
        for copy in copies:
            copy.start()

    def wait(self, name):
        for copy in self.open.pop(name):
            copy.wait()


def spread(where, src_of, dst_of, sems):
    return [
        remote(
            src_of(where.lat_peer(k)), dst_of(where.lat), sems.at[0, k], sems.at[1, k], where.at_lat(k)
        )
        for k in range(1, LATS)
    ]


def halo_copies(where, step, src, dst, sems):
    copies = []
    for n, device in enumerate(where.halo(step)):
        rows = pl.ds(*HALO[n])
        copies.append(remote(src.at[rows], dst.at[rows], sems.at[0, n], sems.at[1, n], device))
    return copies


def sum_slots(ref):
    value = ref[0].astype(F32)
    for n in range(1, ref.shape[0]):
        value = value + ref[n].astype(F32)
    return value


def whole(
    cot_in, tokens_h, to_cells_h, in_send_h, in_own_h, in_halo_h,
    out_send_h, out_own_h, out_halo_h, to_grid_h, cot_fine_h,
    w_qkv_f_h, w_proj_f_h, w_merge_h, w_qkv_c_h, w_proj_c_h,
    grad_tokens, grad_qkv_f, grad_proj_f, grad_merge, grad_qkv_c, grad_proj_c,
    to_cells, in_send, in_own, in_halo, out_send, out_own, out_halo, to_grid, grid_in, w_qkv_f, w_proj_f, w_merge, w_qkv_c, w_proj_c,
    x, q, k, v, probs, mixed_f, tg, blended, merged, slices,
    send_in, got_in, send_out, got_out, got_in2, got_out2,
    cot, part, part_got, coarse_ref, packed, normed_got, rows, rows_t, cot_rows, qkv, d_mixed_c, mixed_c, d_qkv,
    d_packed, slices_t,
    share, core_a, z_a, line_a, y_a,
    core_b, z_b, line_b, y_b,
    fine_p, pair_p, lat_p, lon_p, piece_p, half_p,
    fine_0, pair_0, lat_0, lon_0, piece_0, half_0, fine_1, pair_1, lat_1, lon_1, piece_1, half_1,
    load_sems, halo_sems, lat_sems, share_sems, z_sems, core_sems, lon_sems, pass_sems,
):
    where = Place()
    z, y, core = where.lon // 4, lax.rem(where.lon // 2, 2), lax.rem(where.lon, 2)
    chips = [(a, b) for a in range(4) for b in range(2)]
    around = [where.lon_at(lax.rem(z + a, 4), lax.rem(y + b, 2), core) for a, b in chips]
    sibling = where.lon_at(z, y, 1 - core)
    other_y = where.lon_at(z, 1 - y, core)
    flights = Flights()

    def body():
        barrier = pltpu.get_barrier_semaphore()
        friends = [where.at_lat(n) for n in range(1, LATS)] + around[1:] + [sibling]
        friends += list(where.halo(-1)[1:]) + list(where.halo(1)[1:])
        for device in friends:
            pl.semaphore_signal(barrier, inc=1, device_id=device, device_id_type=MESH)
        flights.start("tokens", [pltpu.make_async_copy(tokens_h, grid_in, load_sems.at[13])])
        loads = (
            ("to_cells", to_cells_h, to_cells), ("in_send", in_send_h, in_send),
            ("in_own", in_own_h, in_own), ("in_halo", in_halo_h, in_halo),
            ("w_qkv_f", w_qkv_f_h, w_qkv_f), ("w_proj_f", w_proj_f_h, w_proj_f),
            ("out_send", out_send_h, out_send), ("out_own", out_own_h, out_own),
            ("out_halo", out_halo_h, out_halo), ("w_merge", w_merge_h, w_merge),
            ("w_proj_c", w_proj_c_h, w_proj_c), ("w_qkv_c", w_qkv_c_h, w_qkv_c),
            ("to_grid", to_grid_h, to_grid),
        )
        for n, (name, far, near) in enumerate(loads):
            flights.start(name, [pltpu.make_async_copy(far, near, load_sems.at[n])])

        target = lax.broadcasted_iota(jnp.int32, (CELL, 12), 0)
        column = lax.broadcasted_iota(jnp.int32, (CELL, 12), 1)
        cot_wide = jnp.zeros((CELL, 2048), F32)
        for n in range(3):
            place = jnp.where(target == column + 12 * n, 1.0, 0.0).astype(BF16)
            cot_wide = cot_wide + mm(place, cot_in[n])
        cot[...] = fold([cot_wide[None, :, c * 512 : c * 512 + 512] for c in range(4)])[0].astype(BF16)
        flights.wait("tokens")
        flights.wait("to_cells")
        cells = mm(to_cells[...], grid_in[...])
        tg[...] = cells.astype(BF16)
        flights.start("cot_fine", [pltpu.make_async_copy(cot_fine_h, grid_in, load_sems.at[13])])
        normed = normalize(cells).astype(BF16)
        flights.wait("in_send")
        send_in[...] = mm(in_send[...], normed).astype(BF16)
        pl.semaphore_wait(barrier, len(friends))
        flights.start("halo1", halo_copies(where, -1, send_in, got_in, halo_sems.at[0]))
        flights.start("cots", spread(where, lambda peer: cot, lambda lat: normed_got.at[lat], lat_sems.at[0]))
        normed_got[where.lat] = cot[...]
        flights.wait("in_own")
        flights.wait("in_halo")
        own = mm(in_own[...], normed)
        flights.wait("halo1")
        x[...] = (own + mm(in_halo[...], got_in[...])).astype(BF16)
        flights.wait("w_qkv_f")
        for m, ref in enumerate((q, k, v)):
            ref[...] = mm(x[...], w_qkv_f[m]).astype(BF16)
        masks = head_masks()
        key = lax.broadcasted_iota(jnp.int32, (4 * WIN, WIN), 1)
        query = lax.broadcasted_iota(jnp.int32, (4 * WIN, WIN), 0) % WIN
        real = key < 72
        same = (key < 36) == (query < 36)
        last = where.lat == LATS - 1

        def window(w, carry):
            own_rows = pl.ds(pl.multiple_of(w * WIN, WIN), WIN)
            bound = jnp.logical_and(last, w >= 4)
            for g in range(2):
                lanes = slice(g * 256, g * 256 + 256)
                scores = mm_nt(stack_heads(q[own_rows, lanes], masks), k[own_rows, lanes]) * 0.125
                allowed = jnp.logical_and(real, jnp.logical_or(same, jnp.logical_not(bound)))
                weights = softmax_rows(jnp.where(allowed, scores, -1e30))
                probs[w * 2 + g] = weights
                mixed_f[own_rows, lanes] = pick_heads(
                    mm(weights.astype(BF16), v[own_rows, lanes]), masks
                ).astype(BF16)
            return carry

        lax.fori_loop(0, 8, window, 0, unroll=2)
        flights.wait("w_proj_f")
        out = mm(mixed_f[...], w_proj_f[...]).astype(BF16)
        flights.wait("out_send")
        send_out[...] = mm(out_send[...], out).astype(BF16)
        flights.start("halo2", halo_copies(where, 1, send_out, got_out, halo_sems.at[1]))
        flights.wait("out_own")
        flights.wait("out_halo")
        own = tg[...].astype(F32) + mm(out_own[...], out)
        flights.wait("halo2")
        blended[...] = own + mm(out_halo[...], got_out[...])
        merged[...] = (
            group_stats(blended[...].reshape(16, CELL, E), 0, 16 * E)[0]
            .reshape(LATS, WIN, E)
            .astype(BF16)
        )
        flights.start("merged", spread(where, lambda peer: merged.at[peer], lambda lat: slices.at[lat], lat_sems.at[1]))
        slices[where.lat] = merged[where.lat]
        flights.wait("cots")
        cot_rows[...] = unfold_rows(normed_got[...])
        flights.wait("w_proj_c")
        d_mixed_c[...] = mm_nt(cot_rows[...], w_proj_c[...]).astype(BF16)
        flights.wait("w_merge")
        flights.wait("merged")

        own_rows = unpack(slices[...])

        def merge(c, carry):
            quarters = []
            for n in range(4):
                lanes = pl.ds(pl.multiple_of(n * 512 + c * 256, 256), 256)
                quarters.append(mm(own_rows, w_merge[:, lanes]).reshape(LATS, CELL, 256))
            part[:, :, pl.ds(pl.multiple_of(c * 256, 256), 256)] = fold(quarters).astype(BF16)
            return carry

        def half(first, number):
            lanes = pl.ds(first * 256, 256)
            return spread(
                where,
                lambda peer: part.at[peer, :, lanes],
                lambda lat: part_got.at[lat, :, lanes],
                lat_sems.at[number],
            )

        merge(0, 0)
        flights.start("part_0", half(0, 2))
        merge(1, 0)
        flights.start("part_1", half(1, 3))
        part_got[where.lat] = part[where.lat]
        slices_t[...] = own_rows.astype(F32).T.astype(BF16)
        flights.wait("part_0")
        flights.wait("part_1")
        coarse_ref[...] = unfold_one(sum_slots(part_got))
        packed[...] = fold_one(group_stats(coarse_ref[...], 0, 2048)[0]).astype(BF16)

        def gather_half(src, first, number):
            lanes = pl.ds(first * 256, 256)
            return spread(
                where,
                lambda peer: src.at[:, lanes],
                lambda lat: normed_got.at[lat, :, lanes],
                lat_sems.at[number],
            )

        def rows_half(first):
            parts = unfold(normed_got[:, :, first * 256 : first * 256 + 256].astype(F32))
            for n in range(4):
                lanes = slice(n * 512 + first * 256, n * 512 + first * 256 + 256)
                rows[:, lanes] = parts[n].reshape(LATS * CELL, 256).astype(BF16)
                yield lanes

        for first in range(2):
            flights.start(f"normed_{first}", gather_half(packed, first, (4, 14)[first]))
        normed_got[where.lat] = packed[...]
        flights.wait("w_qkv_c")
        sums = [jnp.zeros((LATS * CELL, 256), F32)] * 3
        for first in range(2):
            flights.wait(f"normed_{first}")
            for lanes in rows_half(first):
                for m in range(3):
                    sums[m] = sums[m] + mm(rows[:, lanes], w_qkv_c[m, lanes])
        for m in range(3):
            qkv[m] = sums[m].astype(BF16)
        real_c = key % CELL < 36

        def window_c(w, carry):
            own_rows = pl.ds(pl.multiple_of(w * WIN, WIN), WIN)
            heads = stack_heads(qkv[0, own_rows], masks)
            d_heads = stack_heads(d_mixed_c[own_rows], masks)
            scores = mm_nt(heads, qkv[1, own_rows]) * 0.125
            weights = softmax_rows(jnp.where(real_c, scores, -1e30))
            weights_bf = weights.astype(BF16)
            mixed_c[own_rows] = pick_heads(mm(weights_bf, qkv[2, own_rows]), masks).astype(BF16)
            d_scores = scores_back(weights, mm_nt(d_heads, qkv[2, own_rows]))
            d_qkv[own_rows, :256] = pick_heads(mm(d_scores, qkv[1, own_rows]), masks).astype(BF16)
            d_qkv[own_rows, 256:512] = mm_tn(d_scores, heads).astype(BF16)
            d_qkv[own_rows, 512:] = mm_tn(weights_bf, d_heads).astype(BF16)
            return carry

        lax.fori_loop(0, 4, window_c, 0, unroll=2)

        def back(c, carry):
            quarters = []
            for n in range(4):
                part_rows = pl.ds(pl.multiple_of(n * 512 + c * 256, 256), 256)
                d_rows = mm_nt(d_qkv[:, :256], w_qkv_c[0, part_rows])
                d_rows = d_rows + mm_nt(d_qkv[:, 256:512], w_qkv_c[1, part_rows])
                d_rows = d_rows + mm_nt(d_qkv[:, 512:], w_qkv_c[2, part_rows])
                quarters.append(d_rows.reshape(LATS, CELL, 256))
            part[:, :, pl.ds(pl.multiple_of(c * 256, 256), 256)] = fold(quarters).astype(BF16)
            return carry

        back(0, 0)
        flights.start("d_part_0", half(0, 5))
        back(1, 0)
        flights.start("d_part_1", half(1, 6))
        part_got[where.lat] = part[where.lat]
        rows_t[...] = rows[...].astype(F32).T.astype(BF16)
        mixed_t = mixed_c[...].astype(F32).T.astype(BF16)

        def shares(m, carry):
            grad = mm(mixed_t, cot_rows[:, pl.ds(pl.multiple_of(m * 256, 256), 256)]).astype(BF16)
            for c in range(2):
                share[c, m // 2, m % 2, :256] = grad[:, c * 128 : c * 128 + 128]
                own_rows = pl.ds(pl.multiple_of(m * 256 + c * 128, 128), 128)
                grad_qkv = mm(rows_t[own_rows], d_qkv[...]).astype(BF16)
                for n in range(6):
                    share[c, m // 2, m % 2, 256 + 128 * n : 384 + 128 * n] = grad_qkv[
                        :, 128 * n : 128 * n + 128
                    ]
            return carry

        lax.fori_loop(0, 8, shares, 0)
        flights.start(
            "core_a",
            [remote(share.at[1 - core], core_a, share_sems.at[0, 0], share_sems.at[1, 0], sibling)],
        )

        def add_pairs(got):
            def add(n, carry):
                got[n] = (share[core, n].astype(F32) + got[n].astype(F32)).astype(BF16)
                return carry

            lax.fori_loop(0, 4, add, 0)

        def z_copies(src, dst, sems):
            copies = []
            for a in range(1, 4):
                there = lax.rem(z + a, 4)
                copies.append(
                    remote(
                        src.at[there], dst.at[a], sems.at[0, a], sems.at[1, a],
                        where.lon_at(there, y, core),
                    )
                )
            return copies

        flights.wait("d_part_0")
        flights.wait("d_part_1")
        d_normed = unfold_one(sum_slots(part_got).astype(BF16).astype(F32))
        d_coarse = fold_one(group_pullback(coarse_ref[...], d_normed, 0, 2048))
        d_packed[...] = (cot[...].astype(F32) + d_coarse).astype(BF16)
        for first in range(2):
            flights.start(f"d_coarse_{first}", gather_half(d_packed, first, (7, 15)[first]))
        normed_got[where.lat] = d_packed[...]
        flights.wait("core_a")
        add_pairs(core_a)
        flights.start("z_a", z_copies(core_a, z_a, z_sems.at[0]))
        sums = [jnp.zeros((LATS * CELL, 512), F32)] * 2
        for first in range(2):
            flights.wait(f"d_coarse_{first}")
            for lanes in rows_half(first):
                for n in range(2):
                    sums[n] = sums[n] + mm_nt(rows[:, lanes], w_merge[n * 512 : n * 512 + 512, lanes])
        merged[...] = pack(*sums)
        flights.start(
            "d_slices",
            spread(where, lambda peer: merged.at[peer], lambda lat: slices.at[lat], lat_sems.at[8]),
        )
        slices[where.lat] = merged[where.lat]

        def merge_shares(m, carry):
            grad = mm(slices_t[...], rows[:, pl.ds(pl.multiple_of(m * 256, 256), 256)]).astype(BF16)
            for c in range(2):
                share[c, m // 2, m % 2] = grad[:, c * 128 : c * 128 + 128]
            return carry

        lax.fori_loop(0, 8, merge_shares, 0)
        flights.start(
            "core_b",
            [remote(share.at[1 - core], core_b, share_sems.at[0, 1], share_sems.at[1, 1], sibling)],
        )
        flights.wait("d_slices")

        d_gathered = group_pullback(
            blended[...].reshape(16, CELL, E),
            slices[...].astype(F32).reshape(16, CELL, E),
            0,
            16 * E,
        )
        flights.wait("cot_fine")
        blended[...] = mm(to_cells[...], grid_in[...]) + d_gathered.reshape(16 * CELL, E)
        d_bf = blended[...].astype(BF16)
        send_in[...] = mm(in_send[...], d_bf).astype(BF16)
        flights.start("halo3", halo_copies(where, -1, send_in, got_in2, halo_sems.at[2]))
        own = mm(in_own[...], d_bf)
        flights.wait("core_b")
        add_pairs(core_b)
        flights.wait("z_a")
        z_a[0] = core_a[z]
        line_a[...] = sum_slots(z_a).astype(BF16)
        flights.start("z_b", z_copies(core_b, z_b, z_sems.at[1]))
        flights.start(
            "y_a", [remote(line_a.at[1 - y], y_a, share_sems.at[0, 2], share_sems.at[1, 2], other_y)]
        )
        flights.wait("halo3")
        d_out = (own + mm(in_halo[...], got_in2[...])).astype(BF16)
        grad = mm_tn(mixed_f[...], d_out).astype(BF16)
        for c in range(2):
            fine_p[:, :, c] = grad[:, c * 256 : c * 256 + 256].reshape(2, 8, 32, 256)
        mixed_f[...] = mm_nt(d_out, w_proj_f[...]).astype(BF16)

        def window_b(g):
            lanes = slice(g * 256, g * 256 + 256)

            def step(w, carry):
                own_rows = pl.ds(pl.multiple_of(w * WIN, WIN), WIN)
                weights = probs[w * 2 + g]
                heads = stack_heads(q[own_rows, lanes], masks)
                d_heads = stack_heads(mixed_f[own_rows, lanes], masks)
                d_scores = scores_back(weights, mm_nt(d_heads, v[own_rows, lanes]))
                new_q = pick_heads(mm(d_scores, k[own_rows, lanes]), masks).astype(BF16)
                new_k = mm_tn(d_scores, heads).astype(BF16)
                v[own_rows, lanes] = mm_tn(weights.astype(BF16), d_heads).astype(BF16)
                q[own_rows, lanes] = new_q
                k[own_rows, lanes] = new_k
                return carry

            return step

        def to_core(name, fine, pair, sems):
            flights.start(
                name, [remote(fine.at[1 - core], pair, sems.at[0], sems.at[1], sibling)]
            )

        def add_core(fine, pair):
            pair[...] = (fine[core].astype(F32) + pair[...].astype(F32)).astype(BF16)

        def to_lat(name, pair, got, sems):
            flights.start(name, spread(where, lambda peer: pair.at[peer], lambda lat: got.at[lat], sems))
            got[where.lat] = pair[where.lat]

        def to_y(name, piece, half, sems):
            flights.start(name, [remote(piece, half, sems.at[0], sems.at[1], other_y)])

        def to_z(name, piece, half, got, sems):
            half[...] = (piece[...].astype(F32) + half[...].astype(F32)).astype(BF16)
            copies = []
            for n in range(1, 4):
                there = where.lon_at(lax.rem(z + n, 4), y, core)
                copies.append(remote(half, got.at[z], sems.at[0, n], sems.at[1, n], there))
            flights.start(name, copies)
            got[z] = half[...]

        def to_all(name, src, dst_of, sems, pass_sems):
            copies = spread(where, lambda peer: src, dst_of, sems)
            for copy in copies:
                copy.start()

            def to_sibling(n):
                rows_of = dst_of(lax.rem(where.lat - n + LATS, LATS))
                return remote(rows_of, rows_of, pass_sems.at[0, n], pass_sems.at[1, n], sibling)

            passed = [to_sibling(n) for n in range(LATS)]
            passed[0].start()

            def finish():
                for n in range(1, LATS):
                    copies[n - 1].wait()
                    passed[n].start()
                for copy in passed:
                    copy.wait()

            return finish

        def shard(lat):
            return pl.ds(pl.multiple_of(core * 256 + lat * 32, 32), 32)

        def qkv_half(g):
            return lambda lat: grad_qkv_f.at[:, shard(lat), pl.ds(g * 256, 256)]

        to_core("core_p", fine_p, pair_p, core_sems.at[4])
        lax.fori_loop(0, 8, window_b(0), 0, unroll=2)
        flights.wait("core_p")
        add_core(fine_p, pair_p)
        to_lat("lat_p", pair_p, lat_p, lat_sems.at[16])
        x_t = x[...].astype(F32).T.astype(BF16)
        for m, ref in enumerate((q, k, v)):
            fine_0[:, :, m] = mm(x_t, ref[:, :256]).astype(BF16).reshape(2, 8, 32, 256)
        to_core("core_0", fine_0, pair_0, core_sems.at[0])
        lax.fori_loop(0, 4, window_b(1), 0, unroll=2)
        flights.wait("core_0")
        add_core(fine_0, pair_0)
        to_lat("lat_0", pair_0, lat_0, lat_sems.at[9])
        lax.fori_loop(4, 8, window_b(1), 0, unroll=2)
        flights.wait("lat_p")
        piece_p[...] = sum_slots(lat_p).astype(BF16)
        to_y("y_p", piece_p, half_p, core_sems.at[5])
        for m, ref in enumerate((q, k, v)):
            fine_1[:, :, m] = mm(x_t, ref[:, 256:]).astype(BF16).reshape(2, 8, 32, 256)
        to_core("core_1", fine_1, pair_1, core_sems.at[1])
        d_shifted = mm_nt(q[...], w_qkv_f[0]) + mm_nt(k[...], w_qkv_f[1])
        d_shifted = (d_shifted + mm_nt(v[...], w_qkv_f[2])).astype(BF16)
        send_out[...] = mm(out_send[...], d_shifted).astype(BF16)
        flights.start("halo4", halo_copies(where, 1, send_out, got_out2, halo_sems.at[3]))
        flights.wait("core_1")
        add_core(fine_1, pair_1)
        to_lat("lat_1", pair_1, lat_1, lat_sems.at[10])
        flights.wait("y_p")
        to_z("lon_p", piece_p, half_p, lon_p, lon_sems.at[2])
        flights.wait("lat_0")
        piece_0[...] = sum_slots(lat_0).astype(BF16)
        to_y("y_0", piece_0, half_0, core_sems.at[2])
        own = mm(out_own[...], d_shifted)
        flights.wait("y_0")
        to_z("lon_0", piece_0, half_0, lon_0, lon_sems.at[0])
        flights.wait("lon_p")
        piece_p[...] = sum_slots(lon_p).astype(BF16)
        grad_proj_f[:, shard(where.lat)] = piece_p[...]
        ends = [
            to_all(
                "proj", piece_p, lambda lat: grad_proj_f.at[:, shard(lat)],
                lat_sems.at[12], pass_sems.at[1],
            )
        ]
        flights.wait("halo4")
        d_normed = (own + mm(out_halo[...], got_out2[...])).astype(BF16).astype(F32)
        grad = blended[...] + pullback(tg[...].astype(F32), d_normed)
        flights.wait("to_grid")
        grad_tokens[...] = mm(to_grid[...], grad.astype(BF16)).astype(BF16)
        flights.wait("lat_1")
        piece_1[...] = sum_slots(lat_1).astype(BF16)
        to_y("y_1", piece_1, half_1, core_sems.at[3])
        flights.wait("lon_0")
        piece_0[...] = sum_slots(lon_0).astype(BF16)
        grad_qkv_f[:, shard(where.lat), :256] = piece_0[...]
        ends.append(to_all("qkv_0", piece_0, qkv_half(0), lat_sems.at[11], pass_sems.at[0]))
        flights.wait("y_1")
        to_z("lon_1", piece_1, half_1, lon_1, lon_sems.at[1])
        flights.wait("z_b")
        z_b[0] = core_b[z]
        line_b[...] = sum_slots(z_b).astype(BF16)
        flights.start(
            "y_b", [remote(line_b.at[1 - y], y_b, share_sems.at[0, 3], share_sems.at[1, 3], other_y)]
        )
        flights.wait("lon_1")
        piece_1[...] = sum_slots(lon_1).astype(BF16)
        grad_qkv_f[:, shard(where.lat), 256:] = piece_1[...]
        ends.append(to_all("qkv_1", piece_1, qkv_half(1), lat_sems.at[13], pass_sems.at[2]))
        flights.wait("y_a")
        grad_proj_c[...] = line_a[y, :256].astype(F32) + y_a[:256].astype(F32)
        for n in range(6):
            own_rows = slice(256 + 128 * n, 384 + 128 * n)
            grad_qkv_c[n // 2, :, (n % 2) * 128 : (n % 2) * 128 + 128] = line_a[y, own_rows].astype(
                F32
            ) + y_a[own_rows].astype(F32)
        flights.wait("y_b")
        grad_merge[...] = line_b[y].astype(F32) + y_b[...].astype(F32)
        for end in ends:
            end()

    body()


def dma(*shape):
    return pltpu.SemaphoreType.DMA(shape)


def bf(*shape):
    return pltpu.VMEM(shape, BF16)


def f32(*shape):
    return pltpu.VMEM(shape, F32)


def per_device(tokens, w_qkv_f, w_proj_f, w_merge, w_qkv_c, w_proj_c, cot_fine, cot_coarse):
    to_cells, in_send, in_own, in_halo, out_send, out_own, out_halo, to_grid = tables()
    flat = tokens.reshape(ROWS * COLS, E)
    cot_flat = cot_fine.reshape(ROWS * COLS, E)
    size = 16 * CELL
    wide = (LATS, 144, E)
    slim = (LATS, WIN, E)
    near = pl.BlockSpec(memory_space=pltpu.VMEM)
    far = pl.BlockSpec(memory_space=pl.ANY)
    shares = [bf(4, 2, 1024, 128)] * 2 + [bf(2, 1024, 128), bf(1024, 128)]
    grad_tokens, grad_qkv_f, grad_proj_f, grad_merge, grad_qkv_c, grad_proj_c = pl.pallas_call(
        whole,
        out_shape=[
            jax.ShapeDtypeStruct((ROWS * COLS, E), BF16),
            jax.ShapeDtypeStruct((3, E, E), BF16),
            jax.ShapeDtypeStruct((2, E, 256), BF16),
            jax.ShapeDtypeStruct((1024, 128), F32),
            jax.ShapeDtypeStruct((3, 128, 256), F32),
            jax.ShapeDtypeStruct((256, 128), F32),
        ],
        in_specs=[near] + [far] * 15,
        out_specs=[near] * 6,
        scratch_shapes=[
            *[bf(*t.shape) for t in (to_cells, in_send, in_own, in_halo)],
            *[bf(*t.shape) for t in (out_send, out_own, out_halo, to_grid, cot_flat)],
            *[bf(*t.shape) for t in (w_qkv_f, w_proj_f, w_merge, w_qkv_c, w_proj_c)],
            *[bf(size, E)] * 4, f32(16, 4 * WIN, WIN), bf(size, E), bf(size, E), f32(size, E),
            bf(*slim), bf(*slim),
            *[bf(224, E)] * 6,
            bf(144, E), bf(*wide), bf(*wide), f32(4, CELL, E), bf(144, E), bf(*wide), bf(320, 2048), bf(2048, 320),
            bf(320, 2048), bf(3, 320, 256), bf(320, 256), bf(320, 256), bf(320, 768),
            bf(144, E), bf(1024, 320),
            bf(2, 4, 2, 1024, 128), *shares, *shares,
            bf(2, 8, 2, 32, 256), *[bf(8, 2, 32, 256)] * 2, bf(4, 2, 32, 256), *[bf(2, 32, 256)] * 2,
            bf(2, 8, 3, 32, 256), *[bf(8, 3, 32, 256)] * 2, bf(4, 3, 32, 256), *[bf(3, 32, 256)] * 2,
            bf(2, 8, 3, 32, 256), *[bf(8, 3, 32, 256)] * 2, bf(4, 3, 32, 256), *[bf(3, 32, 256)] * 2,
            dma(14), dma(4, 2, 3), dma(17, 2, LATS), dma(2, 4), dma(2, 2, 4), dma(6, 2), dma(3, 2, 4),
            dma(3, 2, LATS),
        ],
        compiler_params=pltpu.CompilerParams(
            collective_id=1, has_side_effects=True, vmem_limit_bytes=VMEM_BYTES
        ),
    )(
        cot_coarse[0], flat, to_cells, in_send, in_own, in_halo, out_send, out_own, out_halo, to_grid, cot_flat,
        w_qkv_f, w_proj_f, w_merge, w_qkv_c, w_proj_c,
    )
    arrays = (grad_tokens, grad_qkv_f, grad_proj_f, grad_merge, grad_qkv_c, grad_proj_c)
    outs = [(ROWS * COLS, E), (3, E, E), (E, E), (1024, 128), (3, 128, 256), (256, 128)]
    steps = 4

    def cut(shape, dim):
        size = tuple(s // steps if d == dim else s for d, s in enumerate(shape))
        return pl.BlockSpec(size, lambda i: tuple(i if d == dim else 0 for d in range(len(shape))))

    dims = (0, 1, 0, 0, 1, 0)
    results = pl.pallas_call(
        finish,
        grid=(steps,),
        out_shape=[jax.ShapeDtypeStruct(s, F32 if n else BF16) for n, s in enumerate(outs)],
        in_specs=[cut(t.shape, 1 if n == 2 else d) for n, (t, d) in enumerate(zip(arrays, dims))],
        out_specs=[cut(s, d) for s, d in zip(outs, dims)],
    )(*arrays)
    return (results[0].reshape(tokens.shape), *results[1:])


def finish(tokens, qkv_f, proj_f, merge, qkv_c, proj_c, *outs):
    fine_scale, coarse_scale = 73728**-0.5, 4608**-0.5
    outs[0][...] = tokens[...]
    outs[1][...] = qkv_f[...].astype(F32) * fine_scale
    outs[2][:, :256] = proj_f[0].astype(F32) * fine_scale
    outs[2][:, 256:] = proj_f[1].astype(F32) * fine_scale
    for source, out in zip((merge, qkv_c, proj_c), outs[3:]):
        out[...] = source[...] * coarse_scale


def solution(mesh):
    return jax.shard_map(
        per_device,
        mesh=mesh,
        in_specs=(
            P(None, "lat", "lon", None),
            P(),
            P(),
            P("lat", None),
            P(None, None, "lat"),
            P("lat", None),
            P(None, "lat", "lon", None),
            P(None, "lat", "lon", None),
        ),
        out_specs=(
            P(None, "lat", "lon", None),
            P(),
            P(),
            P("lat", "lon"),
            P(None, "lon", "lat"),
            P("lat", "lon"),
        ),
        check_vma=False,
    )
```

```python
import jax
import jax.numpy as jnp
import numpy as np
from jax import lax
from jax.experimental import pallas as pl
from jax.experimental.pallas import tpu as pltpu
from jax.sharding import PartitionSpec as P

MESH = pl.DeviceIdType.MESH
F32 = jnp.float32
BF16 = jnp.bfloat16
EPS = 1e-05
LATS = 8
ROWS, COLS = 12, 48
WL, WC = 6, 12
CELL = 40
WIN = 80
E = 512
HALO = ((0, 128), (128, 64), (192, 32))
VMEM_BYTES = 63 * 1024 * 1024


def tables():
    win = np.zeros((ROWS, COLS), np.int64)
    cell = np.zeros((ROWS, COLS), np.int64)
    for i in range(ROWS):
        for j in range(COLS):
            win[i, j] = ((i // WL) * 4 + j // WC) * WIN + (i % WL) * WC + j % WC
            cell[i, j] = ((i % 4) * 4 + j % 4) * CELL + (i // 4) * 12 + j // 4
    size = 16 * CELL
    to_cells = np.zeros((size, ROWS * COLS), np.float32)
    in_send = np.zeros((224, size), np.float32)
    in_own = np.zeros((size, size), np.float32)
    in_halo = np.zeros((size, 224), np.float32)
    out_send = np.zeros((224, size), np.float32)
    out_own = np.zeros((size, size), np.float32)
    out_halo = np.zeros((size, 224), np.float32)
    for i in range(ROWS):
        for j in range(COLS):
            to_cells[cell[i, j], i * COLS + j] = 1
            r, c = i + 3, j + 6
            if r < ROWS and c < COLS:
                in_own[win[i, j], cell[r, c]] = 1
                out_own[cell[r, c], win[i, j]] = 1
            else:
                if c < COLS:
                    slot = (r - ROWS) * 42 + c - 6
                elif r < ROWS:
                    slot = 128 + (r - 3) * 6 + c - COLS
                else:
                    slot = 192 + (r - ROWS) * 6 + c - COLS
                in_send[slot, cell[r % ROWS, c % COLS]] = 1
                in_halo[win[i, j], slot] = 1
                out_send[slot, win[i, j]] = 1
                out_halo[cell[r % ROWS, c % COLS], slot] = 1
    return [
        jnp.asarray(t, BF16)
        for t in (to_cells, in_send, in_own, in_halo, out_send, out_own, out_halo, to_cells.T)
    ]


def mm(a, b):
    return jnp.dot(a, b, preferred_element_type=F32)


def mm_nt(a, b):
    return lax.dot_general(a, b, (((1,), (1,)), ((), ())), preferred_element_type=F32)


def mm_tn(a, b):
    return lax.dot_general(a, b, (((0,), (0,)), ((), ())), preferred_element_type=F32)


def normalize(x):
    centred = x - jnp.mean(x, axis=-1, keepdims=True)
    return centred * lax.rsqrt(jnp.mean(centred * centred, axis=-1, keepdims=True) + EPS)


def pullback(x, dy):
    centred = x - jnp.mean(x, axis=-1, keepdims=True)
    rate = lax.rsqrt(jnp.mean(centred * centred, axis=-1, keepdims=True) + EPS)
    y = centred * rate
    inner = jnp.mean(dy * y, axis=-1, keepdims=True)
    return rate * (dy - jnp.mean(dy, axis=-1, keepdims=True) - y * inner)


def total(x, axes):
    s = jnp.sum(x, axis=-1, keepdims=True)
    return jnp.sum(s, axis=axes, keepdims=True)


def group_stats(x, axis, count):
    mean = total(x, axis) * (1.0 / count)
    centred = x - mean
    rate = lax.rsqrt(total(centred * centred, axis) * (1.0 / count) + EPS)
    return centred * rate, rate


def group_pullback(x, dy, axis, count):
    y, rate = group_stats(x, axis, count)
    inner = total(dy * y, axis) * (1.0 / count)
    return rate * (dy - total(dy, axis) * (1.0 / count) - y * inner)


def head_masks():
    lane = lax.broadcasted_iota(jnp.int32, (1, 256), 1) // 64
    return [jnp.where(lane == h, 1.0, 0.0) for h in range(4)]


def stack_heads(x, masks):
    return jnp.concatenate([x * m.astype(BF16) for m in masks], axis=0)


def pick_heads(x, masks):
    out = x[:WIN] * masks[0]
    for h in range(1, 4):
        out = out + x[h * WIN : (h + 1) * WIN] * masks[h]
    return out


def softmax_rows(scores):
    weights = jnp.exp(scores - jnp.max(scores, axis=-1, keepdims=True))
    return weights / jnp.sum(weights, axis=-1, keepdims=True)


def scores_back(probs, d_probs):
    d_probs = d_probs.astype(BF16).astype(F32)
    inner = jnp.sum(d_probs * probs, axis=-1, keepdims=True)
    return (probs * (d_probs - inner) * 0.125).astype(BF16)


def greet(devices):
    barrier = pltpu.get_barrier_semaphore()
    for device in devices:
        pl.semaphore_signal(barrier, inc=1, device_id=device, device_id_type=MESH)
    pl.semaphore_wait(barrier, len(devices))


def remote(src, dst, send, recv, device):
    return pltpu.make_async_remote_copy(
        src_ref=src, dst_ref=dst, send_sem=send, recv_sem=recv, device_id=device, device_id_type=MESH
    )


class Place:
    def __init__(self):
        self.lat = lax.axis_index("lat")
        self.lon = lax.axis_index("lon")

    def lat_peer(self, k):
        return lax.rem(self.lat + k, LATS)

    def at_lat(self, k):
        return (self.lat_peer(k), self.lon)

    def halo(self, step):
        up = lax.rem(self.lat + step + LATS, LATS)
        side = lax.rem(self.lon + step + 16, 16)
        return ((up, self.lon), (self.lat, side), (up, side))

    def lon_at(self, z, y, core):
        return (self.lat, z * 4 + y * 2 + core)


def start_halo(where, step, src, dst, sems):
    copies = []
    for n, device in enumerate(where.halo(step)):
        first, count = HALO[n]
        copies.append(
            remote(
                src.at[pl.ds(first, count)],
                dst.at[pl.ds(first, count)],
                sems.at[0, n],
                sems.at[1, n],
                device,
            )
        )
        copies[-1].start()
    return copies


def wait_all(copies):
    for copy in copies:
        copy.wait()


def start_spread(where, src_of, dst, sems):
    copies = []
    for k in range(1, LATS):
        copies.append(
            remote(
                src_of(where.lat_peer(k)),
                dst.at[where.lat],
                sems.at[0, k],
                sems.at[1, k],
                where.at_lat(k),
            )
        )
        copies[-1].start()
    return copies


def finish_spread(where, src_of, dst, sems):
    for k in range(1, LATS):
        source = where.lat_peer(LATS - k)
        remote(src_of(source), dst.at[source], sems.at[0, k], sems.at[1, k], where.at_lat(k)).wait()


def unpack(x):
    x = x.astype(F32)
    width = x.shape[-1]
    halves = [x[:, :CELL].reshape(LATS * CELL, width), x[:, CELL:].reshape(LATS * CELL, width)]
    return jnp.concatenate(halves, axis=1).astype(BF16)


def pack(top, bottom):
    width = top.shape[-1]
    halves = [top.reshape(LATS, CELL, width), bottom.reshape(LATS, CELL, width)]
    return jnp.concatenate(halves, axis=1).astype(BF16)


def swap_halves(x):
    low = lax.broadcasted_iota(jnp.int32, x.shape, 0) % 8 < 4
    count = x.shape[0]
    return jnp.where(low, pltpu.roll(x, count - 4, 0), pltpu.roll(x, 4, 0))


def fold(parts):
    n, _, width = parts[0].shape
    low = lax.broadcasted_iota(jnp.int32, (n * 8, width), 0) % 8 < 4
    pieces = [p[:, :32] for p in parts]
    for c in (0, 2):
        first = parts[c][:, 32:].reshape(n * 8, width)
        second = swap_halves(parts[c + 1][:, 32:].reshape(n * 8, width))
        pieces.append(jnp.where(low, first, second).reshape(n, 8, width))
    return jnp.concatenate(pieces, axis=1)


def unfold(x):
    n, _, width = x.shape
    low = lax.broadcasted_iota(jnp.int32, (n * 8, width), 0) % 8 < 4
    parts = []
    for c in range(4):
        tail = x[:, 128 + c // 2 * 8 : 136 + c // 2 * 8].reshape(n * 8, width)
        if c % 2:
            tail = swap_halves(tail)
        tail = jnp.where(low, tail, 0.0).reshape(n, 8, width)
        parts.append(jnp.concatenate([x[:, c * 32 : c * 32 + 32], tail], axis=1))
    return parts


def unfold_rows(x):
    parts = [p.reshape(LATS * CELL, 512) for p in unfold(x.astype(F32))]
    return jnp.concatenate(parts, axis=1).astype(BF16)


def unfold_one(x):
    return jnp.concatenate(unfold(x[None]), axis=0)


def fold_one(x):
    return fold([x[c : c + 1] for c in range(4)])[0]


class Flights:
    def __init__(self):
        self.open = {}

    def start(self, name, copies):
        self.open[name] = copies
        for copy in copies:
            copy.start()

    def wait(self, name):
        for copy in self.open.pop(name):
            copy.wait()


def spread(where, src_of, dst_of, sems):
    return [
        remote(
            src_of(where.lat_peer(k)), dst_of(where.lat), sems.at[0, k], sems.at[1, k], where.at_lat(k)
        )
        for k in range(1, LATS)
    ]


def halo_copies(where, step, src, dst, sems):
    copies = []
    for n, device in enumerate(where.halo(step)):
        rows = pl.ds(*HALO[n])
        copies.append(remote(src.at[rows], dst.at[rows], sems.at[0, n], sems.at[1, n], device))
    return copies


def sum_slots(ref):
    value = ref[0].astype(F32)
    for n in range(1, ref.shape[0]):
        value = value + ref[n].astype(F32)
    return value


def whole(
    cot_in, tokens_h, to_cells_h, in_send_h, in_own_h, in_halo_h,
    out_send_h, out_own_h, out_halo_h, to_grid_h, cot_fine_h,
    w_qkv_f_h, w_proj_f_h, w_merge_h, w_qkv_c_h, w_proj_c_h,
    grad_tokens, grad_qkv_f, grad_proj_f, grad_merge, grad_qkv_c, grad_proj_c,
    to_cells, in_send, in_own, in_halo, out_send, out_own, out_halo, to_grid, grid_in, w_qkv_f, w_proj_f, w_merge, w_qkv_c, w_proj_c,
    x, q, k, v, probs, mixed_f, tg, blended, merged, slices,
    send_in, got_in, send_out, got_out, got_in2, got_out2,
    cot, part, part_got, coarse_ref, packed, normed_got, rows, rows_t, cot_rows, qkv, d_mixed_c, mixed_c, d_qkv,
    d_packed, slices_t,
    share, core_a, z_a, line_a, y_a,
    core_b, z_b, line_b, y_b,
    fine_p, pair_p, lat_p, lon_p, piece_p, half_p,
    fine_0, pair_0, lat_0, lon_0, piece_0, half_0, fine_1, pair_1, lat_1, lon_1, piece_1, half_1,
    load_sems, halo_sems, lat_sems, share_sems, z_sems, core_sems, lon_sems, pass_sems,
):
    where = Place()
    z, y, core = where.lon // 4, lax.rem(where.lon // 2, 2), lax.rem(where.lon, 2)
    chips = [(a, b) for a in range(4) for b in range(2)]
    around = [where.lon_at(lax.rem(z + a, 4), lax.rem(y + b, 2), core) for a, b in chips]
    sibling = where.lon_at(z, y, 1 - core)
    other_y = where.lon_at(z, 1 - y, core)
    flights = Flights()

    def body():
        barrier = pltpu.get_barrier_semaphore()
        friends = [where.at_lat(n) for n in range(1, LATS)] + around[1:] + [sibling]
        friends += list(where.halo(-1)[1:]) + list(where.halo(1)[1:])
        for device in friends:
            pl.semaphore_signal(barrier, inc=1, device_id=device, device_id_type=MESH)
        flights.start("tokens", [pltpu.make_async_copy(tokens_h, grid_in, load_sems.at[13])])
        loads = (
            ("to_cells", to_cells_h, to_cells), ("in_send", in_send_h, in_send),
            ("in_own", in_own_h, in_own), ("in_halo", in_halo_h, in_halo),
            ("w_qkv_f", w_qkv_f_h, w_qkv_f), ("w_proj_f", w_proj_f_h, w_proj_f),
            ("out_send", out_send_h, out_send), ("out_own", out_own_h, out_own),
            ("out_halo", out_halo_h, out_halo), ("w_merge", w_merge_h, w_merge),
            ("w_proj_c", w_proj_c_h, w_proj_c), ("w_qkv_c", w_qkv_c_h, w_qkv_c),
            ("to_grid", to_grid_h, to_grid),
        )
        for n, (name, far, near) in enumerate(loads):
            flights.start(name, [pltpu.make_async_copy(far, near, load_sems.at[n])])

        target = lax.broadcasted_iota(jnp.int32, (CELL, 12), 0)
        column = lax.broadcasted_iota(jnp.int32, (CELL, 12), 1)
        cot_wide = jnp.zeros((CELL, 2048), F32)
        for n in range(3):
            place = jnp.where(target == column + 12 * n, 1.0, 0.0).astype(BF16)
            cot_wide = cot_wide + mm(place, cot_in[n])
        cot[...] = fold([cot_wide[None, :, c * 512 : c * 512 + 512] for c in range(4)])[0].astype(BF16)
        flights.wait("tokens")
        flights.wait("to_cells")
        cells = mm(to_cells[...], grid_in[...])
        tg[...] = cells.astype(BF16)
        flights.start("cot_fine", [pltpu.make_async_copy(cot_fine_h, grid_in, load_sems.at[13])])
        normed = normalize(cells).astype(BF16)
        flights.wait("in_send")
        send_in[...] = mm(in_send[...], normed).astype(BF16)
        pl.semaphore_wait(barrier, len(friends))
        flights.start("halo1", halo_copies(where, -1, send_in, got_in, halo_sems.at[0]))
        flights.start("cots", spread(where, lambda peer: cot, lambda lat: normed_got.at[lat], lat_sems.at[0]))
        normed_got[where.lat] = cot[...]
        flights.wait("in_own")
        flights.wait("in_halo")
        own = mm(in_own[...], normed)
        flights.wait("halo1")
        x[...] = (own + mm(in_halo[...], got_in[...])).astype(BF16)
        flights.wait("w_qkv_f")
        for m, ref in enumerate((q, k, v)):
            ref[...] = mm(x[...], w_qkv_f[m]).astype(BF16)
        masks = head_masks()
        key = lax.broadcasted_iota(jnp.int32, (4 * WIN, WIN), 1)
        query = lax.broadcasted_iota(jnp.int32, (4 * WIN, WIN), 0) % WIN
        real = key < 72
        same = (key < 36) == (query < 36)
        last = where.lat == LATS - 1

        def window(w, carry):
            own_rows = pl.ds(pl.multiple_of(w * WIN, WIN), WIN)
            bound = jnp.logical_and(last, w >= 4)
            for g in range(2):
                lanes = slice(g * 256, g * 256 + 256)
                scores = mm_nt(stack_heads(q[own_rows, lanes], masks), k[own_rows, lanes]) * 0.125
                allowed = jnp.logical_and(real, jnp.logical_or(same, jnp.logical_not(bound)))
                weights = softmax_rows(jnp.where(allowed, scores, -1e30))
                probs[w * 2 + g] = weights
                mixed_f[own_rows, lanes] = pick_heads(
                    mm(weights.astype(BF16), v[own_rows, lanes]), masks
                ).astype(BF16)
            return carry

        lax.fori_loop(0, 8, window, 0, unroll=2)
        flights.wait("w_proj_f")
        out = mm(mixed_f[...], w_proj_f[...]).astype(BF16)
        flights.wait("out_send")
        send_out[...] = mm(out_send[...], out).astype(BF16)
        flights.start("halo2", halo_copies(where, 1, send_out, got_out, halo_sems.at[1]))
        flights.wait("out_own")
        flights.wait("out_halo")
        own = tg[...].astype(F32) + mm(out_own[...], out)
        flights.wait("halo2")
        blended[...] = own + mm(out_halo[...], got_out[...])
        merged[...] = (
            group_stats(blended[...].reshape(16, CELL, E), 0, 16 * E)[0]
            .reshape(LATS, WIN, E)
            .astype(BF16)
        )
        flights.start("merged", spread(where, lambda peer: merged.at[peer], lambda lat: slices.at[lat], lat_sems.at[1]))
        slices[where.lat] = merged[where.lat]
        flights.wait("cots")
        cot_rows[...] = unfold_rows(normed_got[...])
        flights.wait("w_proj_c")
        d_mixed_c[...] = mm_nt(cot_rows[...], w_proj_c[...]).astype(BF16)
        flights.wait("w_merge")
        flights.wait("merged")

        own_rows = unpack(slices[...])

        def merge(c, carry):
            quarters = []
            for n in range(4):
                lanes = pl.ds(pl.multiple_of(n * 512 + c * 256, 256), 256)
                quarters.append(mm(own_rows, w_merge[:, lanes]).reshape(LATS, CELL, 256))
            part[:, :, pl.ds(pl.multiple_of(c * 256, 256), 256)] = fold(quarters).astype(BF16)
            return carry

        def half(first, number):
            lanes = pl.ds(first * 256, 256)
            return spread(
                where,
                lambda peer: part.at[peer, :, lanes],
                lambda lat: part_got.at[lat, :, lanes],
                lat_sems.at[number],
            )

        merge(0, 0)
        flights.start("part_0", half(0, 2))
        merge(1, 0)
        flights.start("part_1", half(1, 3))
        part_got[where.lat] = part[where.lat]
        slices_t[...] = own_rows.astype(F32).T.astype(BF16)
        flights.wait("part_0")
        flights.wait("part_1")
        coarse_ref[...] = unfold_one(sum_slots(part_got))
        packed[...] = fold_one(group_stats(coarse_ref[...], 0, 2048)[0]).astype(BF16)

        def gather_half(src, first, number):
            lanes = pl.ds(first * 256, 256)
            return spread(
                where,
                lambda peer: src.at[:, lanes],
                lambda lat: normed_got.at[lat, :, lanes],
                lat_sems.at[number],
            )

        def rows_half(first):
            parts = unfold(normed_got[:, :, first * 256 : first * 256 + 256].astype(F32))
            for n in range(4):
                lanes = slice(n * 512 + first * 256, n * 512 + first * 256 + 256)
                rows[:, lanes] = parts[n].reshape(LATS * CELL, 256).astype(BF16)
                yield lanes

        for first in range(2):
            flights.start(f"normed_{first}", gather_half(packed, first, (4, 14)[first]))
        normed_got[where.lat] = packed[...]
        flights.wait("w_qkv_c")
        sums = [jnp.zeros((LATS * CELL, 256), F32)] * 3
        for first in range(2):
            flights.wait(f"normed_{first}")
            for lanes in rows_half(first):
                for m in range(3):
                    sums[m] = sums[m] + mm(rows[:, lanes], w_qkv_c[m, lanes])
        for m in range(3):
            qkv[m] = sums[m].astype(BF16)
        real_c = key % CELL < 36

        def window_c(w, carry):
            own_rows = pl.ds(pl.multiple_of(w * WIN, WIN), WIN)
            heads = stack_heads(qkv[0, own_rows], masks)
            d_heads = stack_heads(d_mixed_c[own_rows], masks)
            scores = mm_nt(heads, qkv[1, own_rows]) * 0.125
            weights = softmax_rows(jnp.where(real_c, scores, -1e30))
            weights_bf = weights.astype(BF16)
            mixed_c[own_rows] = pick_heads(mm(weights_bf, qkv[2, own_rows]), masks).astype(BF16)
            d_scores = scores_back(weights, mm_nt(d_heads, qkv[2, own_rows]))
            d_qkv[own_rows, :256] = pick_heads(mm(d_scores, qkv[1, own_rows]), masks).astype(BF16)
            d_qkv[own_rows, 256:512] = mm_tn(d_scores, heads).astype(BF16)
            d_qkv[own_rows, 512:] = mm_tn(weights_bf, d_heads).astype(BF16)
            return carry

        lax.fori_loop(0, 4, window_c, 0, unroll=2)

        def back(c, carry):
            quarters = []
            for n in range(4):
                part_rows = pl.ds(pl.multiple_of(n * 512 + c * 256, 256), 256)
                d_rows = mm_nt(d_qkv[:, :256], w_qkv_c[0, part_rows])
                d_rows = d_rows + mm_nt(d_qkv[:, 256:512], w_qkv_c[1, part_rows])
                d_rows = d_rows + mm_nt(d_qkv[:, 512:], w_qkv_c[2, part_rows])
                quarters.append(d_rows.reshape(LATS, CELL, 256))
            part[:, :, pl.ds(pl.multiple_of(c * 256, 256), 256)] = fold(quarters).astype(BF16)
            return carry

        back(0, 0)
        flights.start("d_part_0", half(0, 5))
        back(1, 0)
        flights.start("d_part_1", half(1, 6))
        part_got[where.lat] = part[where.lat]
        rows_t[...] = rows[...].astype(F32).T.astype(BF16)
        mixed_t = mixed_c[...].astype(F32).T.astype(BF16)

        def shares(m, carry):
            grad = mm(mixed_t, cot_rows[:, pl.ds(pl.multiple_of(m * 256, 256), 256)]).astype(BF16)
            for c in range(2):
                share[c, m // 2, m % 2, :256] = grad[:, c * 128 : c * 128 + 128]
                own_rows = pl.ds(pl.multiple_of(m * 256 + c * 128, 128), 128)
                grad_qkv = mm(rows_t[own_rows], d_qkv[...]).astype(BF16)
                for n in range(6):
                    share[c, m // 2, m % 2, 256 + 128 * n : 384 + 128 * n] = grad_qkv[
                        :, 128 * n : 128 * n + 128
                    ]
            return carry

        lax.fori_loop(0, 8, shares, 0)
        flights.start(
            "core_a",
            [remote(share.at[1 - core], core_a, share_sems.at[0, 0], share_sems.at[1, 0], sibling)],
        )

        def add_pairs(got):
            def add(n, carry):
                got[n] = (share[core, n].astype(F32) + got[n].astype(F32)).astype(BF16)
                return carry

            lax.fori_loop(0, 4, add, 0)

        def z_copies(src, dst, sems):
            copies = []
            for a in range(1, 4):
                there = lax.rem(z + a, 4)
                copies.append(
                    remote(
                        src.at[there], dst.at[a], sems.at[0, a], sems.at[1, a],
                        where.lon_at(there, y, core),
                    )
                )
            return copies

        flights.wait("d_part_0")
        flights.wait("d_part_1")
        d_normed = unfold_one(sum_slots(part_got).astype(BF16).astype(F32))
        d_coarse = fold_one(group_pullback(coarse_ref[...], d_normed, 0, 2048))
        d_packed[...] = (cot[...].astype(F32) + d_coarse).astype(BF16)
        for first in range(2):
            flights.start(f"d_coarse_{first}", gather_half(d_packed, first, (7, 15)[first]))
        normed_got[where.lat] = d_packed[...]
        flights.wait("core_a")
        add_pairs(core_a)
        flights.start("z_a", z_copies(core_a, z_a, z_sems.at[0]))
        sums = [jnp.zeros((LATS * CELL, 512), F32)] * 2
        for first in range(2):
            flights.wait(f"d_coarse_{first}")
            for lanes in rows_half(first):
                for n in range(2):
                    sums[n] = sums[n] + mm_nt(rows[:, lanes], w_merge[n * 512 : n * 512 + 512, lanes])
        merged[...] = pack(*sums)
        flights.start(
            "d_slices",
            spread(where, lambda peer: merged.at[peer], lambda lat: slices.at[lat], lat_sems.at[8]),
        )
        slices[where.lat] = merged[where.lat]

        def merge_shares(m, carry):
            grad = mm(slices_t[...], rows[:, pl.ds(pl.multiple_of(m * 256, 256), 256)]).astype(BF16)
            for c in range(2):
                share[c, m // 2, m % 2] = grad[:, c * 128 : c * 128 + 128]
            return carry

        lax.fori_loop(0, 8, merge_shares, 0)
        flights.start(
            "core_b",
            [remote(share.at[1 - core], core_b, share_sems.at[0, 1], share_sems.at[1, 1], sibling)],
        )
        flights.wait("d_slices")

        d_gathered = group_pullback(
            blended[...].reshape(16, CELL, E),
            slices[...].astype(F32).reshape(16, CELL, E),
            0,
            16 * E,
        )
        flights.wait("cot_fine")
        blended[...] = mm(to_cells[...], grid_in[...]) + d_gathered.reshape(16 * CELL, E)
        d_bf = blended[...].astype(BF16)
        send_in[...] = mm(in_send[...], d_bf).astype(BF16)
        flights.start("halo3", halo_copies(where, -1, send_in, got_in2, halo_sems.at[2]))
        own = mm(in_own[...], d_bf)
        flights.wait("core_b")
        add_pairs(core_b)
        flights.wait("z_a")
        z_a[0] = core_a[z]
        line_a[...] = sum_slots(z_a).astype(BF16)
        flights.start("z_b", z_copies(core_b, z_b, z_sems.at[1]))
        flights.start(
            "y_a", [remote(line_a.at[1 - y], y_a, share_sems.at[0, 2], share_sems.at[1, 2], other_y)]
        )
        flights.wait("halo3")
        d_out = (own + mm(in_halo[...], got_in2[...])).astype(BF16)
        grad = mm_tn(mixed_f[...], d_out).astype(BF16)
        for c in range(2):
            fine_p[:, :, c] = grad[:, c * 256 : c * 256 + 256].reshape(2, 8, 32, 256)
        mixed_f[...] = mm_nt(d_out, w_proj_f[...]).astype(BF16)

        def window_b(g):
            lanes = slice(g * 256, g * 256 + 256)

            def step(batch, carry):
                done = []
                for n in range(4):
                    w = batch * 4 + n
                    own_rows = pl.ds(pl.multiple_of(w * WIN, WIN), WIN)
                    weights = probs[w * 2 + g]
                    heads = stack_heads(q[own_rows, lanes], masks)
                    d_heads = stack_heads(mixed_f[own_rows, lanes], masks)
                    d_scores = scores_back(weights, mm_nt(d_heads, v[own_rows, lanes]))
                    new_q = pick_heads(mm(d_scores, k[own_rows, lanes]), masks).astype(BF16)
                    new_k = mm_tn(d_scores, heads).astype(BF16)
                    new_v = mm_tn(weights.astype(BF16), d_heads).astype(BF16)
                    done.append((own_rows, new_q, new_k, new_v))
                for own_rows, new_q, new_k, new_v in done:
                    q[own_rows, lanes] = new_q
                    k[own_rows, lanes] = new_k
                    v[own_rows, lanes] = new_v
                return carry

            return step

        def to_core(name, fine, pair, sems):
            flights.start(
                name, [remote(fine.at[1 - core], pair, sems.at[0], sems.at[1], sibling)]
            )

        def add_core(fine, pair):
            pair[...] = (fine[core].astype(F32) + pair[...].astype(F32)).astype(BF16)

        def to_lat(name, pair, got, sems):
            flights.start(name, spread(where, lambda peer: pair.at[peer], lambda lat: got.at[lat], sems))
            got[where.lat] = pair[where.lat]

        def to_y(name, piece, half, sems):
            flights.start(name, [remote(piece, half, sems.at[0], sems.at[1], other_y)])

        def to_z(name, piece, half, got, sems):
            half[...] = (piece[...].astype(F32) + half[...].astype(F32)).astype(BF16)
            copies = []
            for n in range(1, 4):
                there = where.lon_at(lax.rem(z + n, 4), y, core)
                copies.append(remote(half, got.at[z], sems.at[0, n], sems.at[1, n], there))
            flights.start(name, copies)
            got[z] = half[...]

        def to_all(name, src, dst_of, sems, pass_sems):
            copies = spread(where, lambda peer: src, dst_of, sems)
            for copy in copies:
                copy.start()

            def to_sibling(n):
                rows_of = dst_of(lax.rem(where.lat - n + LATS, LATS))
                return remote(rows_of, rows_of, pass_sems.at[0, n], pass_sems.at[1, n], sibling)

            passed = [to_sibling(n) for n in range(LATS)]
            passed[0].start()

            def finish():
                for n in range(1, LATS):
                    copies[n - 1].wait()
                    passed[n].start()
                for copy in passed:
                    copy.wait()

            return finish

        def shard(lat):
            return pl.ds(pl.multiple_of(core * 256 + lat * 32, 32), 32)

        def qkv_half(g):
            return lambda lat: grad_qkv_f.at[:, shard(lat), pl.ds(g * 256, 256)]

        to_core("core_p", fine_p, pair_p, core_sems.at[4])
        lax.fori_loop(0, 2, window_b(0), 0)
        flights.wait("core_p")
        add_core(fine_p, pair_p)
        to_lat("lat_p", pair_p, lat_p, lat_sems.at[16])
        x_t = x[...].astype(F32).T.astype(BF16)
        for m, ref in enumerate((q, k, v)):
            fine_0[:, :, m] = mm(x_t, ref[:, :256]).astype(BF16).reshape(2, 8, 32, 256)
        to_core("core_0", fine_0, pair_0, core_sems.at[0])
        window_b(1)(0, 0)
        flights.wait("core_0")
        add_core(fine_0, pair_0)
        to_lat("lat_0", pair_0, lat_0, lat_sems.at[9])
        window_b(1)(1, 0)
        flights.wait("lat_p")
        piece_p[...] = sum_slots(lat_p).astype(BF16)
        to_y("y_p", piece_p, half_p, core_sems.at[5])
        for m, ref in enumerate((q, k, v)):
            fine_1[:, :, m] = mm(x_t, ref[:, 256:]).astype(BF16).reshape(2, 8, 32, 256)
        to_core("core_1", fine_1, pair_1, core_sems.at[1])
        d_shifted = mm_nt(q[...], w_qkv_f[0]) + mm_nt(k[...], w_qkv_f[1])
        d_shifted = (d_shifted + mm_nt(v[...], w_qkv_f[2])).astype(BF16)
        send_out[...] = mm(out_send[...], d_shifted).astype(BF16)
        flights.start("halo4", halo_copies(where, 1, send_out, got_out2, halo_sems.at[3]))
        flights.wait("core_1")
        add_core(fine_1, pair_1)
        to_lat("lat_1", pair_1, lat_1, lat_sems.at[10])
        flights.wait("y_p")
        to_z("lon_p", piece_p, half_p, lon_p, lon_sems.at[2])
        own = mm(out_own[...], d_shifted)
        flights.wait("lat_0")
        piece_0[...] = sum_slots(lat_0).astype(BF16)
        to_y("y_0", piece_0, half_0, core_sems.at[2])
        flights.wait("y_0")
        to_z("lon_0", piece_0, half_0, lon_0, lon_sems.at[0])
        flights.wait("lon_p")
        piece_p[...] = sum_slots(lon_p).astype(BF16)
        grad_proj_f[:, shard(where.lat)] = piece_p[...]
        ends = [
            to_all(
                "proj", piece_p, lambda lat: grad_proj_f.at[:, shard(lat)],
                lat_sems.at[12], pass_sems.at[1],
            )
        ]
        flights.wait("halo4")
        d_normed = (own + mm(out_halo[...], got_out2[...])).astype(BF16).astype(F32)
        grad = blended[...] + pullback(tg[...].astype(F32), d_normed)
        flights.wait("to_grid")
        grad_tokens[...] = mm(to_grid[...], grad.astype(BF16)).astype(BF16)
        flights.wait("lat_1")
        piece_1[...] = sum_slots(lat_1).astype(BF16)
        to_y("y_1", piece_1, half_1, core_sems.at[3])
        flights.wait("lon_0")
        piece_0[...] = sum_slots(lon_0).astype(BF16)
        grad_qkv_f[:, shard(where.lat), :256] = piece_0[...]
        ends.append(to_all("qkv_0", piece_0, qkv_half(0), lat_sems.at[11], pass_sems.at[0]))
        flights.wait("y_1")
        to_z("lon_1", piece_1, half_1, lon_1, lon_sems.at[1])
        flights.wait("z_b")
        z_b[0] = core_b[z]
        line_b[...] = sum_slots(z_b).astype(BF16)
        flights.start(
            "y_b", [remote(line_b.at[1 - y], y_b, share_sems.at[0, 3], share_sems.at[1, 3], other_y)]
        )
        flights.wait("lon_1")
        piece_1[...] = sum_slots(lon_1).astype(BF16)
        grad_qkv_f[:, shard(where.lat), 256:] = piece_1[...]
        ends.append(to_all("qkv_1", piece_1, qkv_half(1), lat_sems.at[13], pass_sems.at[2]))
        flights.wait("y_a")
        grad_proj_c[...] = line_a[y, :256].astype(F32) + y_a[:256].astype(F32)
        for n in range(6):
            own_rows = slice(256 + 128 * n, 384 + 128 * n)
            grad_qkv_c[n // 2, :, (n % 2) * 128 : (n % 2) * 128 + 128] = line_a[y, own_rows].astype(
                F32
            ) + y_a[own_rows].astype(F32)
        flights.wait("y_b")
        grad_merge[...] = line_b[y].astype(F32) + y_b[...].astype(F32)
        for end in ends:
            end()

    body()


def dma(*shape):
    return pltpu.SemaphoreType.DMA(shape)


def bf(*shape):
    return pltpu.VMEM(shape, BF16)


def f32(*shape):
    return pltpu.VMEM(shape, F32)


def per_device(tokens, w_qkv_f, w_proj_f, w_merge, w_qkv_c, w_proj_c, cot_fine, cot_coarse):
    to_cells, in_send, in_own, in_halo, out_send, out_own, out_halo, to_grid = tables()
    flat = tokens.reshape(ROWS * COLS, E)
    cot_flat = cot_fine.reshape(ROWS * COLS, E)
    size = 16 * CELL
    wide = (LATS, 144, E)
    slim = (LATS, WIN, E)
    near = pl.BlockSpec(memory_space=pltpu.VMEM)
    far = pl.BlockSpec(memory_space=pl.ANY)
    shares = [bf(4, 2, 1024, 128)] * 2 + [bf(2, 1024, 128), bf(1024, 128)]
    grad_tokens, grad_qkv_f, grad_proj_f, grad_merge, grad_qkv_c, grad_proj_c = pl.pallas_call(
        whole,
        out_shape=[
            jax.ShapeDtypeStruct((ROWS * COLS, E), BF16),
            jax.ShapeDtypeStruct((3, E, E), BF16),
            jax.ShapeDtypeStruct((2, E, 256), BF16),
            jax.ShapeDtypeStruct((1024, 128), F32),
            jax.ShapeDtypeStruct((3, 128, 256), F32),
            jax.ShapeDtypeStruct((256, 128), F32),
        ],
        in_specs=[near] + [far] * 15,
        out_specs=[near] * 6,
        scratch_shapes=[
            *[bf(*t.shape) for t in (to_cells, in_send, in_own, in_halo)],
            *[bf(*t.shape) for t in (out_send, out_own, out_halo, to_grid, cot_flat)],
            *[bf(*t.shape) for t in (w_qkv_f, w_proj_f, w_merge, w_qkv_c, w_proj_c)],
            *[bf(size, E)] * 4, f32(16, 4 * WIN, WIN), bf(size, E), bf(size, E), f32(size, E),
            bf(*slim), bf(*slim),
            *[bf(224, E)] * 6,
            bf(144, E), bf(*wide), bf(*wide), f32(4, CELL, E), bf(144, E), bf(*wide), bf(320, 2048), bf(2048, 320),
            bf(320, 2048), bf(3, 320, 256), bf(320, 256), bf(320, 256), bf(320, 768),
            bf(144, E), bf(1024, 320),
            bf(2, 4, 2, 1024, 128), *shares, *shares,
            bf(2, 8, 2, 32, 256), *[bf(8, 2, 32, 256)] * 2, bf(4, 2, 32, 256), *[bf(2, 32, 256)] * 2,
            bf(2, 8, 3, 32, 256), *[bf(8, 3, 32, 256)] * 2, bf(4, 3, 32, 256), *[bf(3, 32, 256)] * 2,
            bf(2, 8, 3, 32, 256), *[bf(8, 3, 32, 256)] * 2, bf(4, 3, 32, 256), *[bf(3, 32, 256)] * 2,
            dma(14), dma(4, 2, 3), dma(17, 2, LATS), dma(2, 4), dma(2, 2, 4), dma(6, 2), dma(3, 2, 4),
            dma(3, 2, LATS),
        ],
        compiler_params=pltpu.CompilerParams(
            collective_id=1, has_side_effects=True, vmem_limit_bytes=VMEM_BYTES
        ),
    )(
        cot_coarse[0], flat, to_cells, in_send, in_own, in_halo, out_send, out_own, out_halo, to_grid, cot_flat,
        w_qkv_f, w_proj_f, w_merge, w_qkv_c, w_proj_c,
    )
    arrays = (grad_tokens, grad_qkv_f, grad_proj_f, grad_merge, grad_qkv_c, grad_proj_c)
    outs = [(ROWS * COLS, E), (3, E, E), (E, E), (1024, 128), (3, 128, 256), (256, 128)]
    steps = 4

    def cut(shape, dim):
        size = tuple(s // steps if d == dim else s for d, s in enumerate(shape))
        return pl.BlockSpec(size, lambda i: tuple(i if d == dim else 0 for d in range(len(shape))))

    dims = (0, 1, 0, 0, 1, 0)
    results = pl.pallas_call(
        finish,
        grid=(steps,),
        out_shape=[jax.ShapeDtypeStruct(s, F32 if n else BF16) for n, s in enumerate(outs)],
        in_specs=[cut(t.shape, 1 if n == 2 else d) for n, (t, d) in enumerate(zip(arrays, dims))],
        out_specs=[cut(s, d) for s, d in zip(outs, dims)],
    )(*arrays)
    return (results[0].reshape(tokens.shape), *results[1:])


def finish(tokens, qkv_f, proj_f, merge, qkv_c, proj_c, *outs):
    fine_scale, coarse_scale = 73728**-0.5, 4608**-0.5
    outs[0][...] = tokens[...]
    outs[1][...] = qkv_f[...].astype(F32) * fine_scale
    outs[2][:, :256] = proj_f[0].astype(F32) * fine_scale
    outs[2][:, 256:] = proj_f[1].astype(F32) * fine_scale
    for source, out in zip((merge, qkv_c, proj_c), outs[3:]):
        out[...] = source[...] * coarse_scale


def solution(mesh):
    return jax.shard_map(
        per_device,
        mesh=mesh,
        in_specs=(
            P(None, "lat", "lon", None),
            P(),
            P(),
            P("lat", None),
            P(None, None, "lat"),
            P("lat", None),
            P(None, "lat", "lon", None),
            P(None, "lat", "lon", None),
        ),
        out_specs=(
            P(None, "lat", "lon", None),
            P(),
            P(),
            P("lat", "lon"),
            P(None, "lon", "lat"),
            P("lat", "lon"),
        ),
        check_vma=False,
    )
```

```python
import jax
import jax.numpy as jnp
import numpy as np
from jax import lax
from jax.experimental import pallas as pl
from jax.experimental.pallas import tpu as pltpu
from jax.sharding import PartitionSpec as P

MESH = pl.DeviceIdType.MESH
F32 = jnp.float32
BF16 = jnp.bfloat16
EPS = 1e-05
LATS = 8
ROWS, COLS = 12, 48
WL, WC = 6, 12
CELL = 40
WIN = 80
E = 512
HALO = ((0, 128), (128, 64), (192, 32))
VMEM_BYTES = 63 * 1024 * 1024


def tables():
    win = np.zeros((ROWS, COLS), np.int64)
    cell = np.zeros((ROWS, COLS), np.int64)
    for i in range(ROWS):
        for j in range(COLS):
            win[i, j] = ((i // WL) * 4 + j // WC) * WIN + (i % WL) * WC + j % WC
            cell[i, j] = ((i % 4) * 4 + j % 4) * CELL + (i // 4) * 12 + j // 4
    size = 16 * CELL
    to_cells = np.zeros((size, ROWS * COLS), np.float32)
    in_send = np.zeros((224, size), np.float32)
    in_own = np.zeros((size, size), np.float32)
    in_halo = np.zeros((size, 224), np.float32)
    out_send = np.zeros((224, size), np.float32)
    out_own = np.zeros((size, size), np.float32)
    out_halo = np.zeros((size, 224), np.float32)
    for i in range(ROWS):
        for j in range(COLS):
            to_cells[cell[i, j], i * COLS + j] = 1
            r, c = i + 3, j + 6
            if r < ROWS and c < COLS:
                in_own[win[i, j], cell[r, c]] = 1
                out_own[cell[r, c], win[i, j]] = 1
            else:
                if c < COLS:
                    slot = (r - ROWS) * 42 + c - 6
                elif r < ROWS:
                    slot = 128 + (r - 3) * 6 + c - COLS
                else:
                    slot = 192 + (r - ROWS) * 6 + c - COLS
                in_send[slot, cell[r % ROWS, c % COLS]] = 1
                in_halo[win[i, j], slot] = 1
                out_send[slot, win[i, j]] = 1
                out_halo[cell[r % ROWS, c % COLS], slot] = 1
    return [
        jnp.asarray(t, BF16)
        for t in (to_cells, in_send, in_own, in_halo, out_send, out_own, out_halo, to_cells.T)
    ]


def mm(a, b):
    return jnp.dot(a, b, preferred_element_type=F32)


def mm_nt(a, b):
    return lax.dot_general(a, b, (((1,), (1,)), ((), ())), preferred_element_type=F32)


def mm_tn(a, b):
    return lax.dot_general(a, b, (((0,), (0,)), ((), ())), preferred_element_type=F32)


def normalize(x):
    centred = x - jnp.mean(x, axis=-1, keepdims=True)
    return centred * lax.rsqrt(jnp.mean(centred * centred, axis=-1, keepdims=True) + EPS)


def pullback(x, dy):
    centred = x - jnp.mean(x, axis=-1, keepdims=True)
    rate = lax.rsqrt(jnp.mean(centred * centred, axis=-1, keepdims=True) + EPS)
    y = centred * rate
    inner = jnp.mean(dy * y, axis=-1, keepdims=True)
    return rate * (dy - jnp.mean(dy, axis=-1, keepdims=True) - y * inner)


def total(x, axes):
    s = jnp.sum(x, axis=-1, keepdims=True)
    return jnp.sum(s, axis=axes, keepdims=True)


def group_stats(x, axis, count):
    mean = total(x, axis) * (1.0 / count)
    centred = x - mean
    rate = lax.rsqrt(total(centred * centred, axis) * (1.0 / count) + EPS)
    return centred * rate, rate


def group_pullback(x, dy, axis, count):
    y, rate = group_stats(x, axis, count)
    inner = total(dy * y, axis) * (1.0 / count)
    return rate * (dy - total(dy, axis) * (1.0 / count) - y * inner)


def head_masks():
    lane = lax.broadcasted_iota(jnp.int32, (1, 256), 1) // 64
    return [jnp.where(lane == h, 1.0, 0.0) for h in range(4)]


def stack_heads(x, masks):
    return jnp.concatenate([x * m.astype(BF16) for m in masks], axis=0)


def pick_heads(x, masks):
    out = x[:WIN] * masks[0]
    for h in range(1, 4):
        out = out + x[h * WIN : (h + 1) * WIN] * masks[h]
    return out


def softmax_rows(scores):
    weights = jnp.exp(scores - jnp.max(scores, axis=-1, keepdims=True))
    return weights / jnp.sum(weights, axis=-1, keepdims=True)


def scores_back(probs, d_probs):
    d_probs = d_probs.astype(BF16).astype(F32)
    inner = jnp.sum(d_probs * probs, axis=-1, keepdims=True)
    return (probs * (d_probs - inner) * 0.125).astype(BF16)


def greet(devices):
    barrier = pltpu.get_barrier_semaphore()
    for device in devices:
        pl.semaphore_signal(barrier, inc=1, device_id=device, device_id_type=MESH)
    pl.semaphore_wait(barrier, len(devices))


def remote(src, dst, send, recv, device):
    return pltpu.make_async_remote_copy(
        src_ref=src, dst_ref=dst, send_sem=send, recv_sem=recv, device_id=device, device_id_type=MESH
    )


class Place:
    def __init__(self):
        self.lat = lax.axis_index("lat")
        self.lon = lax.axis_index("lon")

    def lat_peer(self, k):
        return lax.rem(self.lat + k, LATS)

    def at_lat(self, k):
        return (self.lat_peer(k), self.lon)

    def halo(self, step):
        up = lax.rem(self.lat + step + LATS, LATS)
        side = lax.rem(self.lon + step + 16, 16)
        return ((up, self.lon), (self.lat, side), (up, side))

    def lon_at(self, z, y, core):
        return (self.lat, z * 4 + y * 2 + core)


def start_halo(where, step, src, dst, sems):
    copies = []
    for n, device in enumerate(where.halo(step)):
        first, count = HALO[n]
        copies.append(
            remote(
                src.at[pl.ds(first, count)],
                dst.at[pl.ds(first, count)],
                sems.at[0, n],
                sems.at[1, n],
                device,
            )
        )
        copies[-1].start()
    return copies


def wait_all(copies):
    for copy in copies:
        copy.wait()


def start_spread(where, src_of, dst, sems):
    copies = []
    for k in range(1, LATS):
        copies.append(
            remote(
                src_of(where.lat_peer(k)),
                dst.at[where.lat],
                sems.at[0, k],
                sems.at[1, k],
                where.at_lat(k),
            )
        )
        copies[-1].start()
    return copies


def finish_spread(where, src_of, dst, sems):
    for k in range(1, LATS):
        source = where.lat_peer(LATS - k)
        remote(src_of(source), dst.at[source], sems.at[0, k], sems.at[1, k], where.at_lat(k)).wait()


def unpack(x):
    x = x.astype(F32)
    width = x.shape[-1]
    halves = [x[:, :CELL].reshape(LATS * CELL, width), x[:, CELL:].reshape(LATS * CELL, width)]
    return jnp.concatenate(halves, axis=1).astype(BF16)


def pack(top, bottom):
    width = top.shape[-1]
    halves = [top.reshape(LATS, CELL, width), bottom.reshape(LATS, CELL, width)]
    return jnp.concatenate(halves, axis=1).astype(BF16)


def swap_halves(x):
    low = lax.broadcasted_iota(jnp.int32, x.shape, 0) % 8 < 4
    count = x.shape[0]
    return jnp.where(low, pltpu.roll(x, count - 4, 0), pltpu.roll(x, 4, 0))


def fold(parts):
    n, _, width = parts[0].shape
    low = lax.broadcasted_iota(jnp.int32, (n * 8, width), 0) % 8 < 4
    pieces = [p[:, :32] for p in parts]
    for c in (0, 2):
        first = parts[c][:, 32:].reshape(n * 8, width)
        second = swap_halves(parts[c + 1][:, 32:].reshape(n * 8, width))
        pieces.append(jnp.where(low, first, second).reshape(n, 8, width))
    return jnp.concatenate(pieces, axis=1)


def unfold(x):
    n, _, width = x.shape
    low = lax.broadcasted_iota(jnp.int32, (n * 8, width), 0) % 8 < 4
    parts = []
    for c in range(4):
        tail = x[:, 128 + c // 2 * 8 : 136 + c // 2 * 8].reshape(n * 8, width)
        if c % 2:
            tail = swap_halves(tail)
        tail = jnp.where(low, tail, 0.0).reshape(n, 8, width)
        parts.append(jnp.concatenate([x[:, c * 32 : c * 32 + 32], tail], axis=1))
    return parts


def unfold_rows(x):
    parts = [p.reshape(LATS * CELL, 512) for p in unfold(x.astype(F32))]
    return jnp.concatenate(parts, axis=1).astype(BF16)


def unfold_one(x):
    return jnp.concatenate(unfold(x[None]), axis=0)


def fold_one(x):
    return fold([x[c : c + 1] for c in range(4)])[0]


class Flights:
    def __init__(self):
        self.open = {}

    def start(self, name, copies):
        self.open[name] = copies
        for copy in copies:
            copy.start()

    def wait(self, name):
        for copy in self.open.pop(name):
            copy.wait()


def spread(where, src_of, dst_of, sems):
    return [
        remote(
            src_of(where.lat_peer(k)), dst_of(where.lat), sems.at[0, k], sems.at[1, k], where.at_lat(k)
        )
        for k in range(1, LATS)
    ]


def halo_copies(where, step, src, dst, sems):
    copies = []
    for n, device in enumerate(where.halo(step)):
        rows = pl.ds(*HALO[n])
        copies.append(remote(src.at[rows], dst.at[rows], sems.at[0, n], sems.at[1, n], device))
    return copies


def sum_slots(ref):
    value = ref[0].astype(F32)
    for n in range(1, ref.shape[0]):
        value = value + ref[n].astype(F32)
    return value


def whole(
    cot_in, tokens_h, to_cells_h, in_send_h, in_own_h, in_halo_h,
    out_send_h, out_own_h, out_halo_h, to_grid_h, cot_fine_h,
    w_qkv_f_h, w_proj_f_h, w_merge_h, w_qkv_c_h, w_proj_c_h,
    grad_tokens, grad_qkv_f, grad_proj_f, grad_merge, grad_qkv_c, grad_proj_c,
    to_cells, in_send, in_own, in_halo, out_send, out_own, out_halo, to_grid, grid_in, w_qkv_f, w_proj_f, w_merge, w_qkv_c, w_proj_c,
    x, q, k, v, probs, mixed_f, tg, blended, merged, slices,
    send_in, got_in, send_out, got_out, got_in2, got_out2,
    cot, part, part_got, coarse_ref, packed, normed_got, rows, rows_t, cot_rows, qkv, d_mixed_c, mixed_c, d_qkv,
    d_packed, slices_t,
    share, core_a, z_a, line_a, y_a,
    core_b, z_b, line_b, y_b,
    fine_p, pair_p, lat_p, lon_p, piece_p, half_p,
    fine_0, pair_0, lat_0, lon_0, piece_0, half_0, fine_1, pair_1, lat_1, lon_1, piece_1, half_1,
    load_sems, halo_sems, lat_sems, share_sems, z_sems, core_sems, lon_sems, pass_sems,
):
    where = Place()
    z, y, core = where.lon // 4, lax.rem(where.lon // 2, 2), lax.rem(where.lon, 2)
    chips = [(a, b) for a in range(4) for b in range(2)]
    around = [where.lon_at(lax.rem(z + a, 4), lax.rem(y + b, 2), core) for a, b in chips]
    sibling = where.lon_at(z, y, 1 - core)
    other_y = where.lon_at(z, 1 - y, core)
    flights = Flights()

    def body():
        barrier = pltpu.get_barrier_semaphore()
        friends = [where.at_lat(n) for n in range(1, LATS)] + around[1:] + [sibling]
        friends += list(where.halo(-1)[1:]) + list(where.halo(1)[1:])
        for device in friends:
            pl.semaphore_signal(barrier, inc=1, device_id=device, device_id_type=MESH)
        flights.start("tokens", [pltpu.make_async_copy(tokens_h, grid_in, load_sems.at[13])])
        loads = (
            ("to_cells", to_cells_h, to_cells), ("in_send", in_send_h, in_send),
            ("in_own", in_own_h, in_own), ("in_halo", in_halo_h, in_halo),
            ("w_qkv_f", w_qkv_f_h, w_qkv_f), ("w_proj_f", w_proj_f_h, w_proj_f),
            ("out_send", out_send_h, out_send), ("out_own", out_own_h, out_own),
            ("out_halo", out_halo_h, out_halo), ("w_merge", w_merge_h, w_merge),
            ("w_proj_c", w_proj_c_h, w_proj_c), ("w_qkv_c", w_qkv_c_h, w_qkv_c),
            ("to_grid", to_grid_h, to_grid),
        )
        for n, (name, far, near) in enumerate(loads):
            flights.start(name, [pltpu.make_async_copy(far, near, load_sems.at[n])])

        target = lax.broadcasted_iota(jnp.int32, (CELL, 12), 0)
        column = lax.broadcasted_iota(jnp.int32, (CELL, 12), 1)
        cot_wide = jnp.zeros((CELL, 2048), F32)
        for n in range(3):
            place = jnp.where(target == column + 12 * n, 1.0, 0.0).astype(BF16)
            cot_wide = cot_wide + mm(place, cot_in[n])
        cot[...] = fold([cot_wide[None, :, c * 512 : c * 512 + 512] for c in range(4)])[0].astype(BF16)
        flights.wait("tokens")
        flights.wait("to_cells")
        cells = mm(to_cells[...], grid_in[...])
        tg[...] = cells.astype(BF16)
        flights.start("cot_fine", [pltpu.make_async_copy(cot_fine_h, grid_in, load_sems.at[13])])
        normed = normalize(cells).astype(BF16)
        flights.wait("in_send")
        send_in[...] = mm(in_send[...], normed).astype(BF16)
        pl.semaphore_wait(barrier, len(friends))
        flights.start("halo1", halo_copies(where, -1, send_in, got_in, halo_sems.at[0]))
        flights.start("cots", spread(where, lambda peer: cot, lambda lat: normed_got.at[lat], lat_sems.at[0]))
        normed_got[where.lat] = cot[...]
        flights.wait("in_own")
        flights.wait("in_halo")
        own = mm(in_own[...], normed)
        flights.wait("halo1")
        x[...] = (own + mm(in_halo[...], got_in[...])).astype(BF16)
        flights.wait("w_qkv_f")
        for m, ref in enumerate((q, k, v)):
            ref[...] = mm(x[...], w_qkv_f[m]).astype(BF16)
        masks = head_masks()
        key = lax.broadcasted_iota(jnp.int32, (4 * WIN, WIN), 1)
        query = lax.broadcasted_iota(jnp.int32, (4 * WIN, WIN), 0) % WIN
        real = key < 72
        same = (key < 36) == (query < 36)
        last = where.lat == LATS - 1

        def window(w, carry):
            own_rows = pl.ds(pl.multiple_of(w * WIN, WIN), WIN)
            bound = jnp.logical_and(last, w >= 4)
            for g in range(2):
                lanes = slice(g * 256, g * 256 + 256)
                scores = mm_nt(stack_heads(q[own_rows, lanes], masks), k[own_rows, lanes]) * 0.125
                allowed = jnp.logical_and(real, jnp.logical_or(same, jnp.logical_not(bound)))
                weights = softmax_rows(jnp.where(allowed, scores, -1e30))
                probs[w * 2 + g] = weights
                mixed_f[own_rows, lanes] = pick_heads(
                    mm(weights.astype(BF16), v[own_rows, lanes]), masks
                ).astype(BF16)
            return carry

        lax.fori_loop(0, 8, window, 0, unroll=2)
        flights.wait("w_proj_f")
        out = mm(mixed_f[...], w_proj_f[...]).astype(BF16)
        flights.wait("out_send")
        send_out[...] = mm(out_send[...], out).astype(BF16)
        flights.start("halo2", halo_copies(where, 1, send_out, got_out, halo_sems.at[1]))
        flights.wait("out_own")
        flights.wait("out_halo")
        own = tg[...].astype(F32) + mm(out_own[...], out)
        flights.wait("halo2")
        blended[...] = own + mm(out_halo[...], got_out[...])
        merged[...] = (
            group_stats(blended[...].reshape(16, CELL, E), 0, 16 * E)[0]
            .reshape(LATS, WIN, E)
            .astype(BF16)
        )
        flights.start("merged", spread(where, lambda peer: merged.at[peer], lambda lat: slices.at[lat], lat_sems.at[1]))
        slices[where.lat] = merged[where.lat]
        flights.wait("cots")
        cot_rows[...] = unfold_rows(normed_got[...])
        flights.wait("w_proj_c")
        d_mixed_c[...] = mm_nt(cot_rows[...], w_proj_c[...]).astype(BF16)
        flights.wait("w_merge")
        flights.wait("merged")

        own_rows = unpack(slices[...])

        def merge(c, carry):
            quarters = []
            for n in range(4):
                lanes = pl.ds(pl.multiple_of(n * 512 + c * 256, 256), 256)
                quarters.append(mm(own_rows, w_merge[:, lanes]).reshape(LATS, CELL, 256))
            part[:, :, pl.ds(pl.multiple_of(c * 256, 256), 256)] = fold(quarters).astype(BF16)
            return carry

        def half(first, number):
            lanes = pl.ds(first * 256, 256)
            return spread(
                where,
                lambda peer: part.at[peer, :, lanes],
                lambda lat: part_got.at[lat, :, lanes],
                lat_sems.at[number],
            )

        merge(0, 0)
        flights.start("part_0", half(0, 2))
        merge(1, 0)
        flights.start("part_1", half(1, 3))
        part_got[where.lat] = part[where.lat]
        slices_t[...] = own_rows.astype(F32).T.astype(BF16)
        flights.wait("part_0")
        flights.wait("part_1")
        coarse_ref[...] = unfold_one(sum_slots(part_got))
        packed[...] = fold_one(group_stats(coarse_ref[...], 0, 2048)[0]).astype(BF16)

        def gather_half(src, first, number):
            lanes = pl.ds(first * 256, 256)
            return spread(
                where,
                lambda peer: src.at[:, lanes],
                lambda lat: normed_got.at[lat, :, lanes],
                lat_sems.at[number],
            )

        def rows_half(first):
            parts = unfold(normed_got[:, :, first * 256 : first * 256 + 256].astype(F32))
            for n in range(4):
                lanes = slice(n * 512 + first * 256, n * 512 + first * 256 + 256)
                rows[:, lanes] = parts[n].reshape(LATS * CELL, 256).astype(BF16)
                yield lanes

        for first in range(2):
            flights.start(f"normed_{first}", gather_half(packed, first, (4, 14)[first]))
        normed_got[where.lat] = packed[...]
        flights.wait("w_qkv_c")
        sums = [jnp.zeros((LATS * CELL, 256), F32)] * 3
        for first in range(2):
            flights.wait(f"normed_{first}")
            for lanes in rows_half(first):
                for m in range(3):
                    sums[m] = sums[m] + mm(rows[:, lanes], w_qkv_c[m, lanes])
        for m in range(3):
            qkv[m] = sums[m].astype(BF16)
        real_c = key % CELL < 36

        def window_c(w, carry):
            own_rows = pl.ds(pl.multiple_of(w * WIN, WIN), WIN)
            heads = stack_heads(qkv[0, own_rows], masks)
            d_heads = stack_heads(d_mixed_c[own_rows], masks)
            scores = mm_nt(heads, qkv[1, own_rows]) * 0.125
            weights = softmax_rows(jnp.where(real_c, scores, -1e30))
            weights_bf = weights.astype(BF16)
            mixed_c[own_rows] = pick_heads(mm(weights_bf, qkv[2, own_rows]), masks).astype(BF16)
            d_scores = scores_back(weights, mm_nt(d_heads, qkv[2, own_rows]))
            d_qkv[own_rows, :256] = pick_heads(mm(d_scores, qkv[1, own_rows]), masks).astype(BF16)
            d_qkv[own_rows, 256:512] = mm_tn(d_scores, heads).astype(BF16)
            d_qkv[own_rows, 512:] = mm_tn(weights_bf, d_heads).astype(BF16)
            return carry

        lax.fori_loop(0, 4, window_c, 0, unroll=2)

        def back(c, carry):
            quarters = []
            for n in range(4):
                part_rows = pl.ds(pl.multiple_of(n * 512 + c * 256, 256), 256)
                d_rows = mm_nt(d_qkv[:, :256], w_qkv_c[0, part_rows])
                d_rows = d_rows + mm_nt(d_qkv[:, 256:512], w_qkv_c[1, part_rows])
                d_rows = d_rows + mm_nt(d_qkv[:, 512:], w_qkv_c[2, part_rows])
                quarters.append(d_rows.reshape(LATS, CELL, 256))
            part[:, :, pl.ds(pl.multiple_of(c * 256, 256), 256)] = fold(quarters).astype(BF16)
            return carry

        back(0, 0)
        flights.start("d_part_0", half(0, 5))
        back(1, 0)
        flights.start("d_part_1", half(1, 6))
        part_got[where.lat] = part[where.lat]
        rows_t[...] = rows[...].astype(F32).T.astype(BF16)
        mixed_t = mixed_c[...].astype(F32).T.astype(BF16)

        def shares(m, carry):
            grad = mm(mixed_t, cot_rows[:, pl.ds(pl.multiple_of(m * 256, 256), 256)]).astype(BF16)
            for c in range(2):
                share[c, m // 2, m % 2, :256] = grad[:, c * 128 : c * 128 + 128]
                own_rows = pl.ds(pl.multiple_of(m * 256 + c * 128, 128), 128)
                grad_qkv = mm(rows_t[own_rows], d_qkv[...]).astype(BF16)
                for n in range(6):
                    share[c, m // 2, m % 2, 256 + 128 * n : 384 + 128 * n] = grad_qkv[
                        :, 128 * n : 128 * n + 128
                    ]
            return carry

        lax.fori_loop(0, 8, shares, 0)
        flights.start(
            "core_a",
            [remote(share.at[1 - core], core_a, share_sems.at[0, 0], share_sems.at[1, 0], sibling)],
        )

        def add_pairs(got):
            def add(n, carry):
                got[n] = (share[core, n].astype(F32) + got[n].astype(F32)).astype(BF16)
                return carry

            lax.fori_loop(0, 4, add, 0)

        def z_copies(src, dst, sems):
            copies = []
            for a in range(1, 4):
                there = lax.rem(z + a, 4)
                copies.append(
                    remote(
                        src.at[there], dst.at[a], sems.at[0, a], sems.at[1, a],
                        where.lon_at(there, y, core),
                    )
                )
            return copies

        flights.wait("d_part_0")
        flights.wait("d_part_1")
        d_normed = unfold_one(sum_slots(part_got).astype(BF16).astype(F32))
        d_coarse = fold_one(group_pullback(coarse_ref[...], d_normed, 0, 2048))
        d_packed[...] = (cot[...].astype(F32) + d_coarse).astype(BF16)
        for first in range(2):
            flights.start(f"d_coarse_{first}", gather_half(d_packed, first, (7, 15)[first]))
        normed_got[where.lat] = d_packed[...]
        flights.wait("core_a")
        add_pairs(core_a)
        flights.start("z_a", z_copies(core_a, z_a, z_sems.at[0]))
        sums = [jnp.zeros((LATS * CELL, 512), F32)] * 2
        for first in range(2):
            flights.wait(f"d_coarse_{first}")
            for lanes in rows_half(first):
                for n in range(2):
                    sums[n] = sums[n] + mm_nt(rows[:, lanes], w_merge[n * 512 : n * 512 + 512, lanes])
        merged[...] = pack(*sums)
        flights.start(
            "d_slices",
            spread(where, lambda peer: merged.at[peer], lambda lat: slices.at[lat], lat_sems.at[8]),
        )
        slices[where.lat] = merged[where.lat]

        def merge_shares(m, carry):
            grad = mm(slices_t[...], rows[:, pl.ds(pl.multiple_of(m * 256, 256), 256)]).astype(BF16)
            for c in range(2):
                share[c, m // 2, m % 2] = grad[:, c * 128 : c * 128 + 128]
            return carry

        lax.fori_loop(0, 8, merge_shares, 0)
        flights.start(
            "core_b",
            [remote(share.at[1 - core], core_b, share_sems.at[0, 1], share_sems.at[1, 1], sibling)],
        )
        flights.wait("d_slices")

        d_gathered = group_pullback(
            blended[...].reshape(16, CELL, E),
            slices[...].astype(F32).reshape(16, CELL, E),
            0,
            16 * E,
        )
        flights.wait("cot_fine")
        blended[...] = mm(to_cells[...], grid_in[...]) + d_gathered.reshape(16 * CELL, E)
        d_bf = blended[...].astype(BF16)
        send_in[...] = mm(in_send[...], d_bf).astype(BF16)
        flights.start("halo3", halo_copies(where, -1, send_in, got_in2, halo_sems.at[2]))
        own = mm(in_own[...], d_bf)
        flights.wait("core_b")
        add_pairs(core_b)
        flights.start("z_b", z_copies(core_b, z_b, z_sems.at[1]))
        flights.wait("halo3")
        d_out = (own + mm(in_halo[...], got_in2[...])).astype(BF16)
        grad = mm_tn(mixed_f[...], d_out).astype(BF16)
        for c in range(2):
            fine_p[:, :, c] = grad[:, c * 256 : c * 256 + 256].reshape(2, 8, 32, 256)
        mixed_f[...] = mm_nt(d_out, w_proj_f[...]).astype(BF16)

        def window_b(g):
            lanes = slice(g * 256, g * 256 + 256)

            def step(batch, carry):
                done = []
                for n in range(4):
                    w = batch * 4 + n
                    own_rows = pl.ds(pl.multiple_of(w * WIN, WIN), WIN)
                    weights = probs[w * 2 + g]
                    heads = stack_heads(q[own_rows, lanes], masks)
                    d_heads = stack_heads(mixed_f[own_rows, lanes], masks)
                    d_scores = scores_back(weights, mm_nt(d_heads, v[own_rows, lanes]))
                    new_q = pick_heads(mm(d_scores, k[own_rows, lanes]), masks).astype(BF16)
                    new_k = mm_tn(d_scores, heads).astype(BF16)
                    new_v = mm_tn(weights.astype(BF16), d_heads).astype(BF16)
                    done.append((own_rows, new_q, new_k, new_v))
                for own_rows, new_q, new_k, new_v in done:
                    q[own_rows, lanes] = new_q
                    k[own_rows, lanes] = new_k
                    v[own_rows, lanes] = new_v
                return carry

            return step

        def to_core(name, fine, pair, sems):
            flights.start(
                name, [remote(fine.at[1 - core], pair, sems.at[0], sems.at[1], sibling)]
            )

        def add_core(fine, pair):
            pair[...] = (fine[core].astype(F32) + pair[...].astype(F32)).astype(BF16)

        def to_lat(name, pair, got, sems):
            flights.start(name, spread(where, lambda peer: pair.at[peer], lambda lat: got.at[lat], sems))
            got[where.lat] = pair[where.lat]

        def to_y(name, piece, half, sems):
            flights.start(name, [remote(piece, half, sems.at[0], sems.at[1], other_y)])

        def to_z(name, piece, half, got, sems):
            half[...] = (piece[...].astype(F32) + half[...].astype(F32)).astype(BF16)
            copies = []
            for n in range(1, 4):
                there = where.lon_at(lax.rem(z + n, 4), y, core)
                copies.append(remote(half, got.at[z], sems.at[0, n], sems.at[1, n], there))
            flights.start(name, copies)
            got[z] = half[...]

        def to_all(name, src, dst_of, sems, pass_sems):
            copies = spread(where, lambda peer: src, dst_of, sems)
            for copy in copies:
                copy.start()

            def to_sibling(n):
                rows_of = dst_of(lax.rem(where.lat - n + LATS, LATS))
                return remote(rows_of, rows_of, pass_sems.at[0, n], pass_sems.at[1, n], sibling)

            passed = [to_sibling(n) for n in range(LATS)]
            passed[0].start()

            def forward():
                for n in range(1, LATS):
                    copies[n - 1].wait()
                    passed[n].start()

            def drain():
                for copy in passed:
                    copy.wait()

            return forward, drain

        def shard(lat):
            return pl.ds(pl.multiple_of(core * 256 + lat * 32, 32), 32)

        def qkv_half(g):
            return lambda lat: grad_qkv_f.at[:, shard(lat), pl.ds(g * 256, 256)]

        to_core("core_p", fine_p, pair_p, core_sems.at[4])
        flights.wait("z_a")
        z_a[0] = core_a[z]
        line_a[...] = sum_slots(z_a).astype(BF16)
        flights.start(
            "y_a", [remote(line_a.at[1 - y], y_a, share_sems.at[0, 2], share_sems.at[1, 2], other_y)]
        )
        lax.fori_loop(0, 2, window_b(0), 0)
        flights.wait("core_p")
        add_core(fine_p, pair_p)
        to_lat("lat_p", pair_p, lat_p, lat_sems.at[16])
        x_t = x[...].astype(F32).T.astype(BF16)
        for m, ref in enumerate((q, k, v)):
            fine_0[:, :, m] = mm(x_t, ref[:, :256]).astype(BF16).reshape(2, 8, 32, 256)
        to_core("core_0", fine_0, pair_0, core_sems.at[0])
        window_b(1)(0, 0)
        flights.wait("core_0")
        add_core(fine_0, pair_0)
        to_lat("lat_0", pair_0, lat_0, lat_sems.at[9])
        window_b(1)(1, 0)
        for m, ref in enumerate((q, k, v)):
            fine_1[:, :, m] = mm(x_t, ref[:, 256:]).astype(BF16).reshape(2, 8, 32, 256)
        to_core("core_1", fine_1, pair_1, core_sems.at[1])
        flights.wait("lat_p")
        piece_p[...] = sum_slots(lat_p).astype(BF16)
        to_y("y_p", piece_p, half_p, core_sems.at[5])
        d_shifted = mm_nt(q[...], w_qkv_f[0]) + mm_nt(k[...], w_qkv_f[1])
        d_shifted = (d_shifted + mm_nt(v[...], w_qkv_f[2])).astype(BF16)
        send_out[...] = mm(out_send[...], d_shifted).astype(BF16)
        flights.start("halo4", halo_copies(where, 1, send_out, got_out2, halo_sems.at[3]))
        flights.wait("core_1")
        add_core(fine_1, pair_1)
        to_lat("lat_1", pair_1, lat_1, lat_sems.at[10])
        flights.wait("y_p")
        to_z("lon_p", piece_p, half_p, lon_p, lon_sems.at[2])
        own = mm(out_own[...], d_shifted)
        flights.wait("lat_0")
        piece_0[...] = sum_slots(lat_0).astype(BF16)
        to_y("y_0", piece_0, half_0, core_sems.at[2])
        flights.wait("y_0")
        to_z("lon_0", piece_0, half_0, lon_0, lon_sems.at[0])
        flights.wait("lon_p")
        piece_p[...] = sum_slots(lon_p).astype(BF16)
        grad_proj_f[:, shard(where.lat)] = piece_p[...]
        ends = [
            to_all(
                "proj", piece_p, lambda lat: grad_proj_f.at[:, shard(lat)],
                lat_sems.at[12], pass_sems.at[1],
            )
        ]
        flights.wait("halo4")
        d_normed = (own + mm(out_halo[...], got_out2[...])).astype(BF16).astype(F32)
        grad = blended[...] + pullback(tg[...].astype(F32), d_normed)
        flights.wait("to_grid")
        grad_tokens[...] = mm(to_grid[...], grad.astype(BF16)).astype(BF16)
        flights.wait("lat_1")
        piece_1[...] = sum_slots(lat_1).astype(BF16)
        to_y("y_1", piece_1, half_1, core_sems.at[3])
        flights.wait("lon_0")
        piece_0[...] = sum_slots(lon_0).astype(BF16)
        grad_qkv_f[:, shard(where.lat), :256] = piece_0[...]
        ends.append(to_all("qkv_0", piece_0, qkv_half(0), lat_sems.at[11], pass_sems.at[0]))
        flights.wait("y_1")
        to_z("lon_1", piece_1, half_1, lon_1, lon_sems.at[1])
        flights.wait("z_b")
        z_b[0] = core_b[z]
        line_b[...] = sum_slots(z_b).astype(BF16)
        flights.start(
            "y_b", [remote(line_b.at[1 - y], y_b, share_sems.at[0, 3], share_sems.at[1, 3], other_y)]
        )
        ends[0][0]()
        flights.wait("lon_1")
        piece_1[...] = sum_slots(lon_1).astype(BF16)
        grad_qkv_f[:, shard(where.lat), 256:] = piece_1[...]
        ends.append(to_all("qkv_1", piece_1, qkv_half(1), lat_sems.at[13], pass_sems.at[2]))
        flights.wait("y_a")
        grad_proj_c[...] = line_a[y, :256].astype(F32) + y_a[:256].astype(F32)
        for n in range(6):
            own_rows = slice(256 + 128 * n, 384 + 128 * n)
            grad_qkv_c[n // 2, :, (n % 2) * 128 : (n % 2) * 128 + 128] = line_a[y, own_rows].astype(
                F32
            ) + y_a[own_rows].astype(F32)
        flights.wait("y_b")
        grad_merge[...] = line_b[y].astype(F32) + y_b[...].astype(F32)
        for forward, _ in ends[1:]:
            forward()
        for _, drain in ends:
            drain()

    body()


def dma(*shape):
    return pltpu.SemaphoreType.DMA(shape)


def bf(*shape):
    return pltpu.VMEM(shape, BF16)


def f32(*shape):
    return pltpu.VMEM(shape, F32)


def per_device(tokens, w_qkv_f, w_proj_f, w_merge, w_qkv_c, w_proj_c, cot_fine, cot_coarse):
    to_cells, in_send, in_own, in_halo, out_send, out_own, out_halo, to_grid = tables()
    flat = tokens.reshape(ROWS * COLS, E)
    cot_flat = cot_fine.reshape(ROWS * COLS, E)
    size = 16 * CELL
    wide = (LATS, 144, E)
    slim = (LATS, WIN, E)
    near = pl.BlockSpec(memory_space=pltpu.VMEM)
    far = pl.BlockSpec(memory_space=pl.ANY)
    shares = [bf(4, 2, 1024, 128)] * 2 + [bf(2, 1024, 128), bf(1024, 128)]
    grad_tokens, grad_qkv_f, grad_proj_f, grad_merge, grad_qkv_c, grad_proj_c = pl.pallas_call(
        whole,
        out_shape=[
            jax.ShapeDtypeStruct((ROWS * COLS, E), BF16),
            jax.ShapeDtypeStruct((3, E, E), BF16),
            jax.ShapeDtypeStruct((2, E, 256), BF16),
            jax.ShapeDtypeStruct((1024, 128), F32),
            jax.ShapeDtypeStruct((3, 128, 256), F32),
            jax.ShapeDtypeStruct((256, 128), F32),
        ],
        in_specs=[near] + [far] * 15,
        out_specs=[near] * 6,
        scratch_shapes=[
            *[bf(*t.shape) for t in (to_cells, in_send, in_own, in_halo)],
            *[bf(*t.shape) for t in (out_send, out_own, out_halo, to_grid, cot_flat)],
            *[bf(*t.shape) for t in (w_qkv_f, w_proj_f, w_merge, w_qkv_c, w_proj_c)],
            *[bf(size, E)] * 4, f32(16, 4 * WIN, WIN), bf(size, E), bf(size, E), f32(size, E),
            bf(*slim), bf(*slim),
            *[bf(224, E)] * 6,
            bf(144, E), bf(*wide), bf(*wide), f32(4, CELL, E), bf(144, E), bf(*wide), bf(320, 2048), bf(2048, 320),
            bf(320, 2048), bf(3, 320, 256), bf(320, 256), bf(320, 256), bf(320, 768),
            bf(144, E), bf(1024, 320),
            bf(2, 4, 2, 1024, 128), *shares, *shares,
            bf(2, 8, 2, 32, 256), *[bf(8, 2, 32, 256)] * 2, bf(4, 2, 32, 256), *[bf(2, 32, 256)] * 2,
            bf(2, 8, 3, 32, 256), *[bf(8, 3, 32, 256)] * 2, bf(4, 3, 32, 256), *[bf(3, 32, 256)] * 2,
            bf(2, 8, 3, 32, 256), *[bf(8, 3, 32, 256)] * 2, bf(4, 3, 32, 256), *[bf(3, 32, 256)] * 2,
            dma(14), dma(4, 2, 3), dma(17, 2, LATS), dma(2, 4), dma(2, 2, 4), dma(6, 2), dma(3, 2, 4),
            dma(3, 2, LATS),
        ],
        compiler_params=pltpu.CompilerParams(
            collective_id=1, has_side_effects=True, vmem_limit_bytes=VMEM_BYTES
        ),
    )(
        cot_coarse[0], flat, to_cells, in_send, in_own, in_halo, out_send, out_own, out_halo, to_grid, cot_flat,
        w_qkv_f, w_proj_f, w_merge, w_qkv_c, w_proj_c,
    )
    arrays = (grad_tokens, grad_qkv_f, grad_proj_f, grad_merge, grad_qkv_c, grad_proj_c)
    outs = [(ROWS * COLS, E), (3, E, E), (E, E), (1024, 128), (3, 128, 256), (256, 128)]
    steps = 4

    def cut(shape, dim):
        size = tuple(s // steps if d == dim else s for d, s in enumerate(shape))
        return pl.BlockSpec(size, lambda i: tuple(i if d == dim else 0 for d in range(len(shape))))

    dims = (0, 1, 0, 0, 1, 0)
    results = pl.pallas_call(
        finish,
        grid=(steps,),
        out_shape=[jax.ShapeDtypeStruct(s, F32 if n else BF16) for n, s in enumerate(outs)],
        in_specs=[cut(t.shape, 1 if n == 2 else d) for n, (t, d) in enumerate(zip(arrays, dims))],
        out_specs=[cut(s, d) for s, d in zip(outs, dims)],
    )(*arrays)
    return (results[0].reshape(tokens.shape), *results[1:])


def finish(tokens, qkv_f, proj_f, merge, qkv_c, proj_c, *outs):
    fine_scale, coarse_scale = 73728**-0.5, 4608**-0.5
    outs[0][...] = tokens[...]
    outs[1][...] = qkv_f[...].astype(F32) * fine_scale
    outs[2][:, :256] = proj_f[0].astype(F32) * fine_scale
    outs[2][:, 256:] = proj_f[1].astype(F32) * fine_scale
    for source, out in zip((merge, qkv_c, proj_c), outs[3:]):
        out[...] = source[...] * coarse_scale


def solution(mesh):
    return jax.shard_map(
        per_device,
        mesh=mesh,
        in_specs=(
            P(None, "lat", "lon", None),
            P(),
            P(),
            P("lat", None),
            P(None, None, "lat"),
            P("lat", None),
            P(None, "lat", "lon", None),
            P(None, "lat", "lon", None),
        ),
        out_specs=(
            P(None, "lat", "lon", None),
            P(),
            P(),
            P("lat", "lon"),
            P(None, "lon", "lat"),
            P("lat", "lon"),
        ),
        check_vma=False,
    )
```
